32 devices in a mesh: head: 4 (over y, core), doc: 8 (over z, x).
Axes of the slice: x: 2, y: 2, z: 4, core: 2. Of those that a mesh axis runs over, the one named last changes fastest.
Arguments:
- tokens: bfloat16 [3072, 1024], P('doc'), may hold values from -6 to 6
- w_qkv: bfloat16 [1024, 3, 1024], P(None, None, 'head'), may hold values from -0.1875 to 0.1875
- w_out: bfloat16 [1024, 1024], P('head'), may hold values from -0.1875 to 0.1875
- w_up: bfloat16 [1024, 4096], P(None, 'head'), may hold values from -0.1875 to 0.1875
- w_down: bfloat16 [4096, 1024], P('head'), may hold values from -0.09375 to 0.09375
- gain_one: float32 [1024], replicated, may hold values from 0.5 to 1.5
- gain_two: float32 [1024], replicated, may hold values from 0.5 to 1.5
- rel_table: bfloat16 [512, 1024], replicated, may hold values from -6 to 6
- prompt_cache: bfloat16 [2, 1024, 1024], P(None, 'doc', 'head'), may hold values from -480 to 480
- w_proj: bfloat16 [1024, 128], replicated, may hold values from -0.1875 to 0.1875
- doc_vectors: bfloat16 [512, 256, 128], P('doc'), may hold values from -0.5 to 0.5
- doc_lengths: int32 [512], P('doc'), may hold values from 8 to 256, as said below
- group_ids: int32 [96], P('doc'), may hold values from 0 to 15
- candidates: int32 [96, 32], P('doc', 'head'), may hold values from 0 to 511, as said below
Outputs:
- query_vectors: bfloat16 [3072, 128], P('doc')
- scores: float32 [96, 32], P('doc', 'head')
The draws below stay inside these ranges and needn't reach their ends.
Inputs may be any that keep to these rules, and one draw needn't show every extreme that they name: Split candidates into aligned blocks of 12 requests by 8 columns (one index of doc with one of head). Index o of doc holds documents o * 64 to o * 64 + 63. In each block at most 24 entries name documents held by one index of doc, and one index of doc, the same for all blocks, is named by exactly 24 entries of every block. The documents named within one block are distinct. Some document has exactly 256 tokens; token slots from doc_lengths on are padding.
All inputs are finite; a program needn't handle non-finite values.
Results may differ from the reference program's by a relative error of at most 0.02.
Values may be sent and summed in bfloat16 or wider, within the bound.
No kernel may reach another device: no remote copies, remote signals or barrier semaphores. Data moves between devices by JAX's collectives and lax.ppermute only.
A program may use at most 128 MiB of HBM per device.

```python
import math
import jax
import jax.numpy as jnp
from jax import lax

D = 1024
HEADS = 16
HD = 64
FF = 4096
RELS = 512
EMB = 128
QLEN = 32
PLEN = 64
DLEN = 256
DOC_DEV = 64
CAND_DEV = 8
REQ_DEV = 12
REQ = 96
TOKENS = 3072
CAND = 32
GROUPS = 16
DOCS = 512
CAP = 24
N_HEAD = 4
N_DOC = 8


def draw_prompt_cache(key, part):
    base_key = jax.random.fold_in(key, 0)
    values = jnp.clip(jax.random.normal(base_key, (2, GROUPS * PLEN, D), jnp.float32), -6.0, 6.0)
    return values.astype(jnp.bfloat16)


def draw_doc_lengths(key, part):
    first_key, second_key = jax.random.split(key, 2)
    lengths = jax.random.randint(first_key, (DOCS,), 8, DLEN + 1, dtype=jnp.int32)
    longest = jax.random.randint(second_key, (), 0, DOCS, dtype=jnp.int32)
    return jnp.where(jnp.arange(DOCS, dtype=jnp.int32) == longest, DLEN, lengths).astype(jnp.int32)


def draw_candidates(key, part):
    shards = REQ // REQ_DEV
    columns = CAND // CAND_DEV
    pairs = REQ_DEV * CAND_DEV
    slot_count = shards * CAP
    forced_key, block_key = jax.random.split(key, 2)
    forced = jax.random.randint(forced_key, (), 0, shards, dtype=jnp.int32)

    def one_block(block_seed):
        first_key, second_key, third_key = jax.random.split(block_seed, 3)
        shuffled = jax.random.permutation(first_key, slot_count).astype(jnp.int32)
        holder = shuffled // CAP
        priority = jnp.where(holder == forced, 0, 1) * slot_count + jnp.arange(slot_count, dtype=jnp.int32)
        order = jnp.argsort(priority, stable=True)
        picked = shuffled[order][:pairs]
        mixing = jax.random.permutation(second_key, pairs)
        picked = picked[mixing]
        owners = picked // CAP
        within = picked % CAP
        offsets = jax.random.randint(third_key, (shards,), 0, DOC_DEV, dtype=jnp.int32)
        local_doc = (within + offsets[owners]) % DOC_DEV
        return (owners * DOC_DEV + local_doc).reshape(REQ_DEV, CAND_DEV).astype(jnp.int32)
    seeds = jax.random.split(block_key, shards * columns)
    blocks = jax.vmap(one_block)(seeds).reshape(shards, columns, REQ_DEV, CAND_DEV)
    return jnp.transpose(blocks, (0, 2, 1, 3)).reshape(REQ, CAND).astype(jnp.int32)


def plant(array, stream_key, least, high):
    index_at = [jax.random.randint(jax.random.fold_in(stream_key, axis), (), 0, length) for axis, length in enumerate(array.shape)]
    widest = array.shape.index(max(array.shape))
    next_to = index_at[:widest] + [(index_at[widest] + 1) % array.shape[widest]] + index_at[widest + 1:]
    return array.at[tuple(index_at)].set(least).at[tuple(next_to)].set(high)


def levels(own_key, dims, cuts, smallest, high):
    def one(dim, blocks):
        heights = jax.random.uniform(jax.random.fold_in(jax.random.fold_in(own_key, 6), dim), (blocks,), jnp.float32, smallest / len(cuts), high / len(cuts))
        return jnp.repeat(jnp.exp(heights), dims[dim] // blocks).reshape((-1,) + (1,) * (len(dims) - dim - 1))

    factor_of = one(*cuts[0])
    for cut in cuts[1:]:
        factor_of = factor_of * one(*cut)
    return factor_of


def noise(key, dims, scale, reach, cuts=(), kind=jnp.bfloat16):
    array = scale * jax.random.normal(key, dims, jnp.float32)
    if cuts:
        array = array * levels(key, dims, cuts, -0.22, 0.18)
    return jnp.clip(array, -reach, reach).astype(kind)


def setup_inputs(seed: int = 0) -> dict:
    key_of = jax.random.split(jax.random.key(seed), 15)
    tokens = noise(key_of[0], (TOKENS, D), 1.0, 6.0, ((0, 8),))
    w_qkv = noise(key_of[1], (D, 3, D), D ** -0.5, 0.1875, ((2, 4),))
    w_out = noise(key_of[2], (D, D), D ** -0.5, 0.1875, ((0, 4),))
    w_up = noise(key_of[3], (D, FF), D ** -0.5, 0.1875, ((1, 4),))
    w_down = noise(key_of[4], (FF, D), FF ** -0.5, 0.09375, ((0, 4),))
    gain_one = jnp.clip(1.0 + 0.1 * jax.random.normal(key_of[5], (D,), jnp.float32), 0.5, 1.5)
    gain_two = jnp.clip(1.0 + 0.1 * jax.random.normal(key_of[6], (D,), jnp.float32), 0.5, 1.5)
    rel_table = noise(key_of[7], (RELS, D), 1.0, 6.0)
    prompt_cache = draw_prompt_cache(jax.random.fold_in(key_of[14], 71), 0)
    w_proj = noise(key_of[9], (D, EMB), D ** -0.5, 0.1875)
    doc_vectors = noise(key_of[10], (DOCS, DLEN, EMB), 0.0884, 0.5, ((0, 8),))
    doc_lengths = draw_doc_lengths(jax.random.fold_in(key_of[14], 71), 0)
    group_ids = plant(jax.random.randint(key_of[12], (REQ,), 0, GROUPS), jax.random.fold_in(key_of[12], 1), 0, GROUPS - 1).astype(jnp.int32)
    candidates = draw_candidates(jax.random.fold_in(key_of[14], 71), 0)
    return {"tokens": tokens, "w_qkv": w_qkv, "w_out": w_out, "w_up": w_up, "w_down": w_down, "gain_one": gain_one, "gain_two": gain_two, "rel_table": rel_table, "prompt_cache": prompt_cache, "w_proj": w_proj, "doc_vectors": doc_vectors, "doc_lengths": doc_lengths, "group_ids": group_ids, "candidates": candidates}


def layer_norm(values, gain):
    centre = values - lax.optimization_barrier(jnp.mean(values, axis=-1, keepdims=True))
    spread = lax.optimization_barrier(jnp.mean(centre * centre, axis=-1, keepdims=True))
    return centre * lax.rsqrt(spread + 1e-07) * gain.astype(jnp.float32)

def attend_request(query, keys_own, values_own, group, prompt_cache, rel_q, rel_k):
    start = (group * PLEN).astype(jnp.int32)
    cache_keys = lax.dynamic_slice_in_dim(prompt_cache[0], start, PLEN, 0).reshape(PLEN, HEADS, HD)
    cache_values = lax.dynamic_slice_in_dim(prompt_cache[1], start, PLEN, 0).reshape(PLEN, HEADS, HD)
    keys = jnp.concatenate([keys_own, cache_keys], axis=0).astype(jnp.float32)
    values = jnp.concatenate([values_own, cache_values], axis=0).astype(jnp.float32)
    query_f = query.astype(jnp.float32)
    pos_query = PLEN + jnp.arange(QLEN, dtype=jnp.int32)
    pos_key = jnp.concatenate([pos_query, jnp.arange(PLEN, dtype=jnp.int32)])
    total_keys = QLEN + PLEN
    query_rel = jnp.einsum('qhd,rhd->qhr', query_f, rel_k.astype(jnp.float32))
    index_one = pos_query[:, None] - pos_key[None, :] + RELS // 2
    c2p = jnp.take_along_axis(query_rel, jnp.broadcast_to(index_one[:, None, :], (QLEN, HEADS, total_keys)), axis=2)
    key_rel = jnp.einsum('khd,rhd->khr', keys, rel_q.astype(jnp.float32))
    index_two = pos_key[:, None] - pos_query[None, :] + RELS // 2
    p2c = jnp.take_along_axis(key_rel, jnp.broadcast_to(index_two[:, None, :], (total_keys, HEADS, QLEN)), axis=2)
    p2c = jnp.transpose(p2c, (2, 1, 0))
    logits = (jnp.einsum('qhd,khd->qhk', query_f, keys) + c2p + p2c) / math.sqrt(3 * HD)
    largest = lax.optimization_barrier(jnp.max(logits, axis=-1, keepdims=True))
    weights = jnp.exp(logits - largest)
    denominator = lax.optimization_barrier(jnp.sum(weights, axis=-1))
    rounded = lax.optimization_barrier(weights.astype(jnp.bfloat16)).astype(jnp.float32)
    output = jnp.einsum('qhk,khd->qhd', rounded, values) / denominator[..., None]
    return output.reshape(QLEN, D).astype(jnp.bfloat16)

def score_pair(request_vectors, cand, doc_vectors, doc_lengths):
    document = doc_vectors[cand]
    sims = jnp.dot(request_vectors, document.T, preferred_element_type=jnp.float32)
    live = jnp.arange(DLEN, dtype=jnp.int32) < doc_lengths[cand]
    best = lax.optimization_barrier(jnp.max(jnp.where(live[None, :], sims, -jnp.inf), axis=1))
    return jnp.sum(best)

def reference(tokens, w_qkv, w_out, w_up, w_down, gain_one, gain_two, rel_table, prompt_cache, w_proj, doc_vectors, doc_lengths, group_ids, candidates):
    projected_all = jnp.einsum('td,dcf->ctf', tokens.astype(jnp.float32), w_qkv.astype(jnp.float32)).astype(jnp.bfloat16)
    rel_both = jnp.einsum('rd,dcf->crf', rel_table.astype(jnp.float32), w_qkv[:, :2].astype(jnp.float32)).astype(jnp.bfloat16)
    rel_q = rel_both[0].reshape(RELS, HEADS, HD)
    rel_k = rel_both[1].reshape(RELS, HEADS, HD)
    shape = (N_DOC, REQ_DEV, QLEN, HEADS, HD)
    queries = projected_all[0].reshape(shape)
    keys_all = projected_all[1].reshape(shape)
    values_all = projected_all[2].reshape(shape)
    groups = group_ids.reshape(N_DOC, REQ_DEV)

    def per_shard(inputs):
        inner_fn = jax.vmap(attend_request, in_axes=(0, 0, 0, 0, None, None, None))
        return inner_fn(inputs[0], inputs[1], inputs[2], inputs[3], prompt_cache, rel_q, rel_k)
    attended = lax.map(per_shard, (queries, keys_all, values_all, groups)).reshape(TOKENS, D)
    width = D // N_HEAD
    total = jnp.zeros((TOKENS, D), jnp.float32)
    for block in range(N_HEAD):
        partial_sum = jnp.dot(attended[:, block * width:(block + 1) * width], w_out[block * width:(block + 1) * width], preferred_element_type=jnp.float32)
        total = total + lax.optimization_barrier(partial_sum.astype(jnp.bfloat16)).astype(jnp.float32)
    hidden_one = layer_norm(tokens.astype(jnp.float32) + total, gain_one).astype(jnp.bfloat16)
    inner = jax.nn.gelu(jnp.dot(hidden_one, w_up, preferred_element_type=jnp.float32), approximate=False).astype(jnp.bfloat16)
    hidden_width = FF // N_HEAD
    total_two = jnp.zeros((TOKENS, D), jnp.float32)
    for block in range(N_HEAD):
        partial_sum = jnp.dot(inner[:, block * hidden_width:(block + 1) * hidden_width], w_down[block * hidden_width:(block + 1) * hidden_width], preferred_element_type=jnp.float32)
        total_two = total_two + lax.optimization_barrier(partial_sum.astype(jnp.bfloat16)).astype(jnp.float32)
    hidden_two = layer_norm(hidden_one.astype(jnp.float32) + total_two, gain_two).astype(jnp.bfloat16)
    projected = jnp.dot(hidden_two, w_proj, preferred_element_type=jnp.float32)
    query_vectors = (projected * lax.rsqrt(lax.optimization_barrier(jnp.sum(projected * projected, axis=-1, keepdims=True)) + 1e-06)).astype(jnp.bfloat16)

    def score_shard(inputs):
        by_cand = jax.vmap(score_pair, in_axes=(None, 0, None, None))
        by_request = jax.vmap(by_cand, in_axes=(0, 0, None, None))
        return by_request(inputs[0], inputs[1], doc_vectors, doc_lengths)
    scores = lax.map(score_shard, (query_vectors.reshape(N_DOC, REQ_DEV, QLEN, EMB), candidates.reshape(N_DOC, REQ_DEV, CAND)))
    return (query_vectors, scores.reshape(REQ, CAND))
```

```python
import functools
import math

import jax
import jax.numpy as jnp
from jax import lax
from jax.experimental import pallas as pl
from jax.experimental.pallas import tpu as pltpu
from jax.sharding import PartitionSpec as P

HD = 64
RELS = 512
QLEN = 32
PLEN = 64
DOC_DEV = 64


def layer_norm(values, gain):
    centre = values - jnp.mean(values, axis=-1, keepdims=True)
    spread = jnp.mean(centre * centre, axis=-1, keepdims=True)
    return centre * lax.rsqrt(spread + 1e-07) * gain


def slot_order(holders):
    count = holders.shape[0]
    same = holders[:, None] == holders[None, :]
    earlier = jnp.arange(count)[:, None] > jnp.arange(count)[None, :]
    return jnp.sum(same & earlier, axis=1)


def rate_slots(slot_query, slot_doc, doc_vectors, doc_lengths):
    shape = slot_doc.shape
    flat_doc = slot_doc.reshape(-1)
    flat_query = slot_query.reshape((flat_doc.shape[0],) + slot_query.shape[-2:])
    safe_doc = jnp.maximum(flat_doc, 0)
    documents = doc_vectors[safe_doc]
    lengths = doc_lengths[safe_doc]
    sims = jnp.einsum("sqe,sje->sqj", flat_query, documents, preferred_element_type=jnp.float32)
    live = jnp.arange(documents.shape[1], dtype=jnp.int32)[None, None, :] < lengths[:, None, None]
    best = jnp.max(jnp.where(live, sims, -jnp.inf), axis=2)
    totals = jnp.where(flat_doc >= 0, jnp.sum(best, axis=1), 0.0)
    return totals.reshape(shape)


def body_any(
    tokens,
    w_qkv,
    w_out,
    w_up,
    w_down,
    gain_one,
    gain_two,
    rel_table,
    prompt_cache,
    w_proj,
    doc_vectors,
    doc_lengths,
    group_ids,
    candidates,
):
    rows_dev = tokens.shape[0]
    req_dev = rows_dev // QLEN
    width = w_qkv.shape[2]
    heads_loc = width // HD
    half = RELS // 2
    scale_root = math.sqrt(3 * HD)
    gathered = lax.all_gather(prompt_cache, "doc", axis=1, tiled=True)
    weights_split = w_qkv.reshape(w_qkv.shape[0], 3, heads_loc, HD)
    projected_all = jnp.einsum(
        "td,dchf->chtf", tokens, weights_split, preferred_element_type=jnp.float32
    ).astype(jnp.bfloat16)
    rel_both = jnp.einsum(
        "rd,dchf->chrf", rel_table, weights_split[:, :2], preferred_element_type=jnp.float32
    ).astype(jnp.bfloat16)
    head_shape = (heads_loc, req_dev, QLEN, HD)
    query_four = projected_all[0].reshape(head_shape)
    keys_four = projected_all[1].reshape(head_shape)
    values_four = projected_all[2].reshape(head_shape)
    groups_all = gathered.shape[1] // PLEN
    cache_all = gathered.reshape(2, groups_all, PLEN, heads_loc, HD)
    picked = jnp.transpose(cache_all[:, group_ids], (0, 3, 1, 2, 4))
    keys = jnp.concatenate([keys_four, picked[0]], axis=2)
    values = jnp.concatenate([values_four, picked[1]], axis=2)
    pos_query = PLEN + jnp.arange(QLEN, dtype=jnp.int32)
    pos_key = jnp.concatenate([pos_query, jnp.arange(PLEN, dtype=jnp.int32)])
    index_one = pos_query[:, None] - pos_key[None, :] + half
    index_two = pos_key[:, None] - pos_query[None, :] + half
    rel_k_rows = rel_both[1][:, index_one]
    rel_q_rows = rel_both[0][:, index_two]
    c2p = jnp.einsum("hrqd,hqkd->hrqk", query_four, rel_k_rows, preferred_element_type=jnp.float32)
    p2c = jnp.einsum("hrkd,hkqd->hrqk", keys, rel_q_rows, preferred_element_type=jnp.float32)
    content = jnp.einsum("hrqd,hrkd->hrqk", query_four, keys, preferred_element_type=jnp.float32)
    logits = (content + c2p + p2c) / scale_root
    largest = jnp.max(logits, axis=-1, keepdims=True)
    weights = jnp.exp(logits - largest)
    denominator = jnp.sum(weights, axis=-1)
    summed = jnp.einsum(
        "hrqk,hrkd->hrqd", weights.astype(jnp.bfloat16), values, preferred_element_type=jnp.float32
    )
    attended = (summed / denominator[..., None]).astype(jnp.bfloat16)
    out_split = w_out.reshape(heads_loc, HD, w_out.shape[1])
    attn_part = jnp.einsum(
        "hrqd,hde->rqe", attended, out_split, preferred_element_type=jnp.float32
    ).reshape(rows_dev, w_out.shape[1])
    attn_total = lax.psum(attn_part.astype(jnp.bfloat16), "head").astype(jnp.float32)
    hidden_one = layer_norm(tokens.astype(jnp.float32) + attn_total, gain_one).astype(jnp.bfloat16)
    inner = jax.nn.gelu(
        jnp.dot(hidden_one, w_up, preferred_element_type=jnp.float32), approximate=False
    ).astype(jnp.bfloat16)
    ffn_total = lax.psum(
        jnp.dot(inner, w_down, preferred_element_type=jnp.float32).astype(jnp.bfloat16), "head"
    ).astype(jnp.float32)
    hidden_two = layer_norm(hidden_one.astype(jnp.float32) + ffn_total, gain_two).astype(
        jnp.bfloat16
    )
    projected = jnp.dot(hidden_two, w_proj, preferred_element_type=jnp.float32)
    query_vectors = (
        projected * lax.rsqrt(jnp.sum(projected * projected, axis=-1, keepdims=True) + 1e-06)
    ).astype(jnp.bfloat16)
    shards = lax.axis_size("doc")
    cand_dev = candidates.shape[1]
    pairs = req_dev * cand_dev
    capacity = max(2, 2 * pairs // shards)
    flat_cand = candidates.reshape(-1)
    holders = flat_cand // DOC_DEV
    request_of = jnp.arange(pairs, dtype=jnp.int32) // cand_dev
    slot_rank = slot_order(holders)
    copies, cand_copies = (
        lax.all_gather(query_vectors, "doc", axis=0, tiled=True),
        lax.all_gather(candidates, "doc", axis=0, tiled=True),
    )
    all_query = copies.reshape(shards, req_dev, QLEN, copies.shape[1])
    all_cand = cand_copies.reshape(shards, pairs)
    holder_all = all_cand // DOC_DEV
    local_all = all_cand % DOC_DEV
    rank_all = jax.vmap(slot_order)(holder_all)
    own_index = lax.axis_index("doc")
    chosen = (holder_all[:, None, :] == own_index) & (
        rank_all[:, None, :] == jnp.arange(capacity, dtype=jnp.int32)[None, :, None]
    )
    filled = jnp.any(chosen, axis=2)
    slot_request = jnp.sum(jnp.where(chosen, request_of[None, None, :], 0), axis=2)
    slot_doc = jnp.where(
        filled, jnp.sum(jnp.where(chosen, local_all[:, None, :], 0), axis=2), -1
    ).astype(jnp.int32)
    slot_query = all_query[jnp.arange(shards)[:, None], slot_request]
    slot_scores = rate_slots(slot_query, slot_doc, doc_vectors, doc_lengths)
    returned = lax.all_to_all(slot_scores, "doc", split_axis=0, concat_axis=0, tiled=True)
    scores = returned.reshape(-1)[holders * capacity + slot_rank].reshape(candidates.shape)
    return (query_vectors, scores)


LANES = 128
MIB = 1 << 20


def full_specs(count):
    return [pl.BlockSpec(memory_space=pltpu.VMEM)] * count


def params():
    return pltpu.CompilerParams(vmem_limit_bytes=48 * MIB)


def attend_kernel(
    krow, vrow, qkv, relq, relk, k_zero, k_one, k_two, k_three, v_zero, v_one, att, k_all, v_all
):
    width = att.shape[1]
    heads = width // HD
    for place, piece in enumerate((k_zero, k_one, k_two, k_three)):
        k_all[place * piece.shape[0] : (place + 1) * piece.shape[0], :] = piece[...]
    for place, piece in enumerate((v_zero, v_one)):
        v_all[place * piece.shape[0] : (place + 1) * piece.shape[0], :] = piece[...]
    zero = jnp.bfloat16(0)
    turn = (
        lax.broadcasted_iota(jnp.int32, (LANES, LANES), 0)
        + lax.broadcasted_iota(jnp.int32, (LANES, LANES), 1)
        == LANES - 1
    )
    flip = jnp.where(turn, 1.0, 0.0).astype(jnp.bfloat16)
    rel_k = jnp.dot(flip, relk[...], preferred_element_type=jnp.float32).astype(jnp.bfloat16)
    rel_q = jnp.dot(flip, relq[...], preferred_element_type=jnp.float32).astype(jnp.bfloat16)
    head_of = lax.broadcasted_iota(jnp.int32, (LANES, width), 1) // HD
    rel_q_heads = jnp.concatenate([jnp.where(head_of == h, rel_q, zero) for h in range(heads)], axis=0)
    small_head = lax.broadcasted_iota(jnp.int32, (QLEN, width), 1) // HD
    slot = lax.broadcasted_iota(jnp.int32, (LANES, LANES), 1) // QLEN
    live = lax.broadcasted_iota(jnp.int32, (heads * QLEN, LANES), 1) < PLEN + QLEN
    padding = jnp.zeros((LANES - PLEN - QLEN, width), jnp.bfloat16)
    scale = 1.0 / math.sqrt(3 * HD)

    def one_request(r, carry):
        rows = pl.ds(pl.multiple_of(r * QLEN, QLEN), QLEN)
        q = qkv[rows, 0:width]
        k_own = qkv[rows, width : 2 * width]
        v_own = qkv[rows, 2 * width : 3 * width]
        k_group = k_all[pl.ds(pl.multiple_of(krow[r], PLEN), PLEN), :]
        v_group = v_all[pl.ds(pl.multiple_of(vrow[r], PLEN), PLEN), :]
        keys = jnp.concatenate([k_group, k_own, padding], axis=0)
        values = jnp.concatenate([v_group, v_own, padding], axis=0)
        q_heads = jnp.concatenate([jnp.where(small_head == h, q, zero) for h in range(heads)], axis=0)
        both = lax.dot_general(
            q_heads,
            jnp.concatenate([keys, rel_k], axis=0),
            (((1,), (1,)), ((), ())),
            preferred_element_type=jnp.float32,
        )
        content = both[:, :LANES]
        query_rel = both[:, LANES:]
        c2p = jnp.concatenate(
            [
                pltpu.roll(
                    query_rel[h * QLEN : (h + 1) * QLEN], 97, 1, stride=1, stride_axis=0
                )
                for h in range(heads)
            ],
            axis=0,
        )
        key_rel = lax.dot_general(
            keys, rel_q_heads, (((1,), (1,)), ((), ())), preferred_element_type=jnp.float32
        )
        turned = jnp.zeros((LANES, LANES), jnp.float32)
        for h in range(heads):
            rolled = pltpu.roll(
                key_rel[:, h * LANES : (h + 1) * LANES],
                (32 + h * QLEN) % LANES,
                1,
                stride=1,
                stride_axis=0,
            )
            turned = jnp.where(slot == h, rolled, turned)
        p2c = turned.T[: heads * QLEN]
        logits = jnp.where(live, (content + c2p + p2c) * scale, -jnp.inf)
        largest = jnp.max(logits, axis=1, keepdims=True)
        weights = jnp.exp(logits - largest)
        denominator = jnp.sum(weights, axis=1, keepdims=True)
        summed = jnp.dot(weights.astype(jnp.bfloat16), values, preferred_element_type=jnp.float32)
        summed = summed / denominator
        out = summed[:QLEN]
        for h in range(1, heads):
            out = jnp.where(small_head == h, summed[h * QLEN : (h + 1) * QLEN], out)
        att[rows, :] = out.astype(jnp.bfloat16)
        return carry

    lax.fori_loop(0, att.shape[0] // QLEN, one_request, 0, unroll=2)


def attend(krow, vrow, qkv, relq, relk, k_pieces, v_pieces):
    rows = qkv.shape[0]
    width = qkv.shape[1] // 3
    cached = sum(piece.shape[0] for piece in v_pieces)
    return pl.pallas_call(
        attend_kernel,
        out_shape=jax.ShapeDtypeStruct((rows, width), jnp.bfloat16),
        in_specs=[pl.BlockSpec(memory_space=pltpu.SMEM)] * 2 + full_specs(9),
        out_specs=pl.BlockSpec(memory_space=pltpu.VMEM),
        scratch_shapes=[
            pltpu.VMEM((cached, width), jnp.bfloat16),
            pltpu.VMEM((cached, width), jnp.bfloat16),
        ],
        compiler_params=params(),
        cost_estimate=pl.CostEstimate(flops=400 * MIB, bytes_accessed=2 * MIB, transcendentals=0),
        name="attend",
    )(krow, vrow, qkv, relq, relk, *k_pieces, *v_pieces)


def norm_rows(values, gain):
    centre = values - jnp.mean(values, axis=-1, keepdims=True)
    spread = jnp.mean(centre * centre, axis=-1, keepdims=True)
    return centre * lax.rsqrt(spread + 1e-07) * gain


def feed_rows(start, count, a, w, tokens, gain, w_up, w_down):
    rows = pl.ds(pl.multiple_of(start, 32), count)
    mixed = tokens[rows, :].astype(jnp.float32)
    for piece, weight in zip(a, w):
        mixed = mixed + jnp.dot(piece[rows, :], weight[...], preferred_element_type=jnp.float32)
    hidden = norm_rows(mixed, gain[...]).astype(jnp.bfloat16)
    total = None
    step = 256
    for at in range(0, w_up.shape[1], step):
        up = jnp.dot(hidden, w_up[:, at : at + step], preferred_element_type=jnp.float32)
        inner = (0.5 * up * (1.0 + lax.erf(up * math.sqrt(0.5)))).astype(jnp.bfloat16)
        part = jnp.dot(inner, w_down[at : at + step, :], preferred_element_type=jnp.float32)
        total = part if total is None else total + part
    return hidden, total


def feed_other_kernel(start, a0, a1, a2, a3, w0, w1, w2, w3, tokens, gain, w_up, w_down, out):
    _, total = feed_rows(
        start[0], out.shape[0], (a0, a1, a2, a3), (w0, w1, w2, w3), tokens, gain, w_up, w_down
    )
    out[...] = total.astype(out.dtype)


def feed_own_kernel(start, a0, a1, a2, a3, w0, w1, w2, w3, tokens, gain, w_up, w_down, out, own):
    pieces, weights = (a0, a1, a2, a3), (w0, w1, w2, w3)
    _, total = feed_rows(start[0], out.shape[0], pieces, weights, tokens, gain, w_up, w_down)
    out[...] = total
    hidden, total = feed_rows(start[1], own.shape[0], pieces, weights, tokens, gain, w_up, w_down)
    own[...] = hidden.astype(jnp.float32) + total


def feed(kernel, start, pieces, weights, tokens, gain, w_up, w_down, outs, name):
    return pl.pallas_call(
        kernel,
        out_shape=outs,
        in_specs=[pl.BlockSpec(memory_space=pltpu.SMEM)] + full_specs(12),
        out_specs=full_specs(len(outs)),
        compiler_params=params(),
        cost_estimate=pl.CostEstimate(flops=1600 * MIB, bytes_accessed=6 * MIB, transcendentals=0),
        name=name,
    )(start, *pieces, *weights, tokens, gain, w_up, w_down)


def project_kernel(own, from_core, from_y, gain, w_proj, out):
    after = own[...] + from_core[...].astype(jnp.float32) + from_y[...].astype(jnp.float32)
    hidden = norm_rows(after, gain[...]).astype(jnp.bfloat16)
    projected = jnp.dot(hidden, w_proj[...], preferred_element_type=jnp.float32)
    length = jnp.sum(projected * projected, axis=-1, keepdims=True)
    vectors = (projected * lax.rsqrt(length + 1e-06)).astype(jnp.bfloat16)
    for place in range(out.shape[0]):
        out[place] = vectors


def score_kernel(slots, count, lengths, queries, docs, out):
    lanes = out.shape[1]
    flat = (
        lax.broadcasted_iota(jnp.int32, out.shape, 0) * lanes
        + lax.broadcasted_iota(jnp.int32, out.shape, 1)
    )
    slots_doc = docs.shape[1]
    position = lax.broadcasted_iota(jnp.int32, (QLEN, slots_doc), 1)
    unroll = 4

    def some(i, totals):
        for u in range(unroll):
            packed = slots[i * unroll + u]
            entry = packed & 4095
            group = (packed >> 12) & 255
            doc = packed >> 20
            query = queries[pl.ds(pl.multiple_of(group * QLEN, QLEN), QLEN), :]
            sims = lax.dot_general(
                query, docs[doc], (((1,), (1,)), ((), ())), preferred_element_type=jnp.float32
            )
            sims = jnp.where(position < lengths[doc], sims, -jnp.inf)
            best = jnp.max(sims, axis=1, keepdims=True)
            total = jnp.sum(best, axis=0, keepdims=True)
            totals = jnp.where(flat == entry, total, totals)
        return totals

    out[...] = lax.fori_loop(
        0, (count[0] + unroll - 1) // unroll, some, jnp.zeros(out.shape, jnp.float32)
    )


def body(
    tokens,
    w_qkv,
    w_out,
    w_up,
    w_down,
    gain_one,
    gain_two,
    rel_table,
    prompt_cache,
    w_proj,
    doc_vectors,
    doc_lengths,
    group_ids,
    candidates,
):
    rows = tokens.shape[0]
    width = w_qkv.shape[2]
    n_doc = lax.axis_size("doc")
    n_head = lax.axis_size("head")
    me = lax.axis_index("doc")
    place = lax.axis_index("head")
    own_y, own_c = place // 2, place % 2
    half, quarter = rows // 2, rows // 4

    def over_doc(x, k):
        return lax.ppermute(x, "doc", [(i, i ^ k) for i in range(n_doc)])

    def over_head(x, k):
        return lax.ppermute(x, "head", [(i, i ^ k) for i in range(n_head)])

    keys, values = prompt_cache[0], prompt_cache[1]
    keys_two = jnp.concatenate([keys, over_doc(keys, 1)], axis=0)
    values_four = jnp.concatenate([values] + [over_doc(values, k) for k in (2, 4, 6)], axis=0)
    key_pieces = [keys_two] + [over_doc(keys_two, k) for k in (2, 4, 6)]
    value_pieces = [values_four, over_doc(values_four, 1)]
    groups_dev = keys.shape[0] // PLEN
    relative = (group_ids // groups_dev) ^ me
    within = group_ids % groups_dev * PLEN
    krow = relative * keys.shape[0] + within
    vrow = (relative // 2 + relative % 2 * (n_doc // 2)) * keys.shape[0] + within

    weight = w_qkv.reshape(w_qkv.shape[0], 3 * width)
    qkv = jnp.dot(tokens, weight, preferred_element_type=jnp.float32).astype(jnp.bfloat16)
    low_q = RELS // 2 - PLEN - QLEN + 1
    low_k = RELS // 2 - QLEN
    relq = jnp.dot(
        rel_table[low_q : low_q + LANES], weight[:, :width], preferred_element_type=jnp.float32
    ).astype(jnp.bfloat16)
    relk = jnp.dot(
        rel_table[low_k : low_k + LANES],
        weight[:, width : 2 * width],
        preferred_element_type=jnp.float32,
    ).astype(jnp.bfloat16)

    reqs = candidates.shape[0] // n_head
    cols = candidates.shape[1]
    sent = candidates.reshape(2, 2, reqs * cols).transpose(1, 0, 2).reshape(1, n_head, reqs * cols)
    sent = jnp.broadcast_to(sent, (n_doc, n_head, reqs * cols)).reshape(n_doc * n_head, reqs * cols)
    entries = lax.all_to_all(sent, ("doc", "head"), 0, 0, tiled=True).reshape(n_doc, n_head * reqs * cols)
    block = n_head * reqs * cols
    doc_at = jnp.arange(n_doc, dtype=jnp.int32)[:, None]
    entry_at = jnp.arange(block, dtype=jnp.int32)[None, :]
    group_at = doc_at * reqs + entry_at // cols % reqs
    packed = (doc_at * LANES + entry_at) | (group_at << 12) | ((entries % DOC_DEV) << 20)
    packed = packed.reshape(-1)
    mine = (entries // DOC_DEV == me).reshape(-1)
    rank = jnp.cumsum(mine.astype(jnp.int32)) - 1
    total_slots = n_doc * block
    chosen = mine[None, :] & (rank[None, :] == jnp.arange(total_slots, dtype=jnp.int32)[:, None])
    slots = jnp.sum(jnp.where(chosen, packed[None, :], 0), axis=1)
    count = jnp.sum(mine.astype(jnp.int32))
    slots = jnp.where(jnp.arange(total_slots) < count, slots, LANES - 1)

    out_one = over_head(w_out, 2)
    out_pieces = [w_out, over_head(w_out, 1), out_one, over_head(out_one, 1)]

    att = attend(krow, vrow, qkv, relq, relk, key_pieces, value_pieces)
    att_y = over_head(att, 2)
    att_pieces = [att, over_head(att, 1), att_y, over_head(att_y, 1)]

    gain_rows = gain_one.reshape(1, -1)
    common = (att_pieces, out_pieces, tokens, gain_rows, w_up, w_down)
    start_other = ((1 - own_c) * half).astype(jnp.int32).reshape(1)
    other = feed(
        feed_other_kernel,
        start_other,
        *common,
        [jax.ShapeDtypeStruct((half, tokens.shape[1]), jnp.bfloat16)],
        "feed_other",
    )[0]
    from_core = over_head(other, 1)
    start_own = jnp.stack(
        [own_c * half + (1 - own_y) * quarter, own_c * half + own_y * quarter]
    ).astype(jnp.int32)
    for_y, own = feed(
        feed_own_kernel,
        start_own,
        *common,
        [jax.ShapeDtypeStruct((quarter, tokens.shape[1]), jnp.float32)] * 2,
        "feed_own",
    )
    core_y = lax.dynamic_slice_in_dim(from_core, (1 - own_y) * quarter, quarter, 0)
    core_own = lax.dynamic_slice_in_dim(from_core, own_y * quarter, quarter, 0)
    from_y = over_head((for_y + core_y.astype(jnp.float32)).astype(jnp.bfloat16), 2)

    emb = w_proj.shape[1]
    vectors = pl.pallas_call(
        project_kernel,
        out_shape=jax.ShapeDtypeStruct((n_doc, quarter, emb), jnp.bfloat16),
        in_specs=full_specs(5),
        out_specs=full_specs(1)[0],
        compiler_params=params(),
        name="project",
    )(own, core_own, from_y, gain_two.reshape(1, -1), w_proj)
    queries = lax.all_to_all(vectors, "doc", 0, 0, tiled=True).reshape(n_doc * quarter, emb)

    mine_rows = vectors[0]
    y_rows = over_head(mine_rows, 2)
    pair = jnp.where(
        own_y == 0, jnp.concatenate([mine_rows, y_rows]), jnp.concatenate([y_rows, mine_rows])
    )
    core_pair = over_head(pair, 1)
    query_vectors = jnp.where(
        own_c == 0, jnp.concatenate([pair, core_pair]), jnp.concatenate([core_pair, pair])
    )

    smem = pl.BlockSpec(memory_space=pltpu.SMEM)
    rated = pl.pallas_call(
        score_kernel,
        out_shape=jax.ShapeDtypeStruct((n_doc, LANES), jnp.float32),
        in_specs=[smem, smem, smem] + full_specs(2),
        out_specs=full_specs(1)[0],
        compiler_params=params(),
        name="rate",
    )(slots, count.reshape(1), doc_lengths, queries, doc_vectors)
    tiles = rated[:, :block].reshape(n_doc * n_head, reqs * cols)
    back = lax.all_to_all(tiles, ("doc", "head"), 0, 0, tiled=True)
    scores = jnp.sum(back.reshape(n_doc, n_head, reqs, cols), axis=0)
    scores = scores.reshape(2, 2, reqs, cols).transpose(1, 0, 2, 3).reshape(n_head * reqs, cols)
    return (query_vectors, scores)


def solution(mesh):
    placed = (
        P("doc", None),
        P(None, None, "head"),
        P("head", None),
        P(None, "head"),
        P("head", None),
        P(),
        P(),
        P(),
        P(None, "doc", "head"),
        P(),
        P("doc", None, None),
        P("doc"),
        P("doc"),
        P("doc", "head"),
    )
    fits = mesh.shape["head"] == 4 and mesh.shape["doc"] == 8
    return jax.shard_map(
        body if fits else body_any,
        mesh=mesh,
        in_specs=placed,
        out_specs=(P("doc", None), P("doc", "head")),
        check_vma=False,
    )
```

```python
import functools
import math

import jax
import jax.numpy as jnp
from jax import lax
from jax.experimental import pallas as pl
from jax.experimental.pallas import tpu as pltpu
from jax.sharding import PartitionSpec as P

HD = 64
RELS = 512
QLEN = 32
PLEN = 64
DOC_DEV = 64


def layer_norm(values, gain):
    centre = values - jnp.mean(values, axis=-1, keepdims=True)
    spread = jnp.mean(centre * centre, axis=-1, keepdims=True)
    return centre * lax.rsqrt(spread + 1e-07) * gain


def slot_order(holders):
    count = holders.shape[0]
    same = holders[:, None] == holders[None, :]
    earlier = jnp.arange(count)[:, None] > jnp.arange(count)[None, :]
    return jnp.sum(same & earlier, axis=1)


def rate_slots(slot_query, slot_doc, doc_vectors, doc_lengths):
    shape = slot_doc.shape
    flat_doc = slot_doc.reshape(-1)
    flat_query = slot_query.reshape((flat_doc.shape[0],) + slot_query.shape[-2:])
    safe_doc = jnp.maximum(flat_doc, 0)
    documents = doc_vectors[safe_doc]
    lengths = doc_lengths[safe_doc]
    sims = jnp.einsum("sqe,sje->sqj", flat_query, documents, preferred_element_type=jnp.float32)
    live = jnp.arange(documents.shape[1], dtype=jnp.int32)[None, None, :] < lengths[:, None, None]
    best = jnp.max(jnp.where(live, sims, -jnp.inf), axis=2)
    totals = jnp.where(flat_doc >= 0, jnp.sum(best, axis=1), 0.0)
    return totals.reshape(shape)


def body_any(
    tokens,
    w_qkv,
    w_out,
    w_up,
    w_down,
    gain_one,
    gain_two,
    rel_table,
    prompt_cache,
    w_proj,
    doc_vectors,
    doc_lengths,
    group_ids,
    candidates,
):
    rows_dev = tokens.shape[0]
    req_dev = rows_dev // QLEN
    width = w_qkv.shape[2]
    heads_loc = width // HD
    half = RELS // 2
    scale_root = math.sqrt(3 * HD)
    gathered = lax.all_gather(prompt_cache, "doc", axis=1, tiled=True)
    weights_split = w_qkv.reshape(w_qkv.shape[0], 3, heads_loc, HD)
    projected_all = jnp.einsum(
        "td,dchf->chtf", tokens, weights_split, preferred_element_type=jnp.float32
    ).astype(jnp.bfloat16)
    rel_both = jnp.einsum(
        "rd,dchf->chrf", rel_table, weights_split[:, :2], preferred_element_type=jnp.float32
    ).astype(jnp.bfloat16)
    head_shape = (heads_loc, req_dev, QLEN, HD)
    query_four = projected_all[0].reshape(head_shape)
    keys_four = projected_all[1].reshape(head_shape)
    values_four = projected_all[2].reshape(head_shape)
    groups_all = gathered.shape[1] // PLEN
    cache_all = gathered.reshape(2, groups_all, PLEN, heads_loc, HD)
    picked = jnp.transpose(cache_all[:, group_ids], (0, 3, 1, 2, 4))
    keys = jnp.concatenate([keys_four, picked[0]], axis=2)
    values = jnp.concatenate([values_four, picked[1]], axis=2)
    pos_query = PLEN + jnp.arange(QLEN, dtype=jnp.int32)
    pos_key = jnp.concatenate([pos_query, jnp.arange(PLEN, dtype=jnp.int32)])
    index_one = pos_query[:, None] - pos_key[None, :] + half
    index_two = pos_key[:, None] - pos_query[None, :] + half
    rel_k_rows = rel_both[1][:, index_one]
    rel_q_rows = rel_both[0][:, index_two]
    c2p = jnp.einsum("hrqd,hqkd->hrqk", query_four, rel_k_rows, preferred_element_type=jnp.float32)
    p2c = jnp.einsum("hrkd,hkqd->hrqk", keys, rel_q_rows, preferred_element_type=jnp.float32)
    content = jnp.einsum("hrqd,hrkd->hrqk", query_four, keys, preferred_element_type=jnp.float32)
    logits = (content + c2p + p2c) / scale_root
    largest = jnp.max(logits, axis=-1, keepdims=True)
    weights = jnp.exp(logits - largest)
    denominator = jnp.sum(weights, axis=-1)
    summed = jnp.einsum(
        "hrqk,hrkd->hrqd", weights.astype(jnp.bfloat16), values, preferred_element_type=jnp.float32
    )
    attended = (summed / denominator[..., None]).astype(jnp.bfloat16)
    out_split = w_out.reshape(heads_loc, HD, w_out.shape[1])
    attn_part = jnp.einsum(
        "hrqd,hde->rqe", attended, out_split, preferred_element_type=jnp.float32
    ).reshape(rows_dev, w_out.shape[1])
    attn_total = lax.psum(attn_part.astype(jnp.bfloat16), "head").astype(jnp.float32)
    hidden_one = layer_norm(tokens.astype(jnp.float32) + attn_total, gain_one).astype(jnp.bfloat16)
    inner = jax.nn.gelu(
        jnp.dot(hidden_one, w_up, preferred_element_type=jnp.float32), approximate=False
    ).astype(jnp.bfloat16)
    ffn_total = lax.psum(
        jnp.dot(inner, w_down, preferred_element_type=jnp.float32).astype(jnp.bfloat16), "head"
    ).astype(jnp.float32)
    hidden_two = layer_norm(hidden_one.astype(jnp.float32) + ffn_total, gain_two).astype(
        jnp.bfloat16
    )
    projected = jnp.dot(hidden_two, w_proj, preferred_element_type=jnp.float32)
    query_vectors = (
        projected * lax.rsqrt(jnp.sum(projected * projected, axis=-1, keepdims=True) + 1e-06)
    ).astype(jnp.bfloat16)
    shards = lax.axis_size("doc")
    cand_dev = candidates.shape[1]
    pairs = req_dev * cand_dev
    capacity = max(2, 2 * pairs // shards)
    flat_cand = candidates.reshape(-1)
    holders = flat_cand // DOC_DEV
    request_of = jnp.arange(pairs, dtype=jnp.int32) // cand_dev
    slot_rank = slot_order(holders)
    copies, cand_copies = (
        lax.all_gather(query_vectors, "doc", axis=0, tiled=True),
        lax.all_gather(candidates, "doc", axis=0, tiled=True),
    )
    all_query = copies.reshape(shards, req_dev, QLEN, copies.shape[1])
    all_cand = cand_copies.reshape(shards, pairs)
    holder_all = all_cand // DOC_DEV
    local_all = all_cand % DOC_DEV
    rank_all = jax.vmap(slot_order)(holder_all)
    own_index = lax.axis_index("doc")
    chosen = (holder_all[:, None, :] == own_index) & (
        rank_all[:, None, :] == jnp.arange(capacity, dtype=jnp.int32)[None, :, None]
    )
    filled = jnp.any(chosen, axis=2)
    slot_request = jnp.sum(jnp.where(chosen, request_of[None, None, :], 0), axis=2)
    slot_doc = jnp.where(
        filled, jnp.sum(jnp.where(chosen, local_all[:, None, :], 0), axis=2), -1
    ).astype(jnp.int32)
    slot_query = all_query[jnp.arange(shards)[:, None], slot_request]
    slot_scores = rate_slots(slot_query, slot_doc, doc_vectors, doc_lengths)
    returned = lax.all_to_all(slot_scores, "doc", split_axis=0, concat_axis=0, tiled=True)
    scores = returned.reshape(-1)[holders * capacity + slot_rank].reshape(candidates.shape)
    return (query_vectors, scores)


LANES = 128
MIB = 1 << 20
PREP_UNROLL = 4
ATT_UNROLL = 4


def full_specs(count):
    return [pl.BlockSpec(memory_space=pltpu.VMEM)] * count


def params(mib):
    return pltpu.CompilerParams(vmem_limit_bytes=mib * MIB)


def by_head(values):
    head_of = lax.broadcasted_iota(jnp.int32, values.shape, 1) // HD
    heads = values.shape[1] // HD
    zero = jnp.zeros_like(values)
    return jnp.concatenate([jnp.where(head_of == h, values, zero) for h in range(heads)], axis=0)


def times_rows(left, right):
    return lax.dot_general(left, right, (((1,), (1,)), ((), ())), preferred_element_type=jnp.float32)


def key_terms(keys, rel_q_heads, first):
    key_rel = times_rows(keys, rel_q_heads)
    slot = lax.broadcasted_iota(jnp.int32, (keys.shape[0], LANES), 1) // QLEN
    turned = None
    for h in range(rel_q_heads.shape[0] // LANES):
        shift = (LANES - PLEN - QLEN + first + h * QLEN) % LANES
        rolled = pltpu.roll(
            key_rel[:, h * LANES : (h + 1) * LANES], shift, 1, stride=1, stride_axis=0
        )
        turned = rolled if turned is None else jnp.where(slot == h, rolled, turned)
    return turned


def prepare_kernel(tokens, weight, rel_rows, qkv, base, rel_q_heads):
    width = weight.shape[1] // 3
    heads = width // HD
    qkv[...] = jnp.dot(tokens[...], weight[...], preferred_element_type=jnp.float32).astype(
        jnp.bfloat16
    )
    rel = jnp.dot(
        rel_rows[...], weight[:, : 2 * width], preferred_element_type=jnp.float32
    ).astype(jnp.bfloat16)
    count = rel_rows.shape[0]
    both = lax.broadcasted_iota(jnp.int32, (LANES, count), 0) + lax.broadcasted_iota(
        jnp.int32, (LANES, count), 1
    )
    flip_q = jnp.where(both == LANES, 1.0, 0.0).astype(jnp.bfloat16)
    flip_k = jnp.where(both == LANES + PLEN - 1, 1.0, 0.0).astype(jnp.bfloat16)
    rel_q = jnp.dot(flip_q, rel[:, :width], preferred_element_type=jnp.float32)
    rel_k = jnp.dot(flip_k, rel[:, width:], preferred_element_type=jnp.float32)
    rel_k = rel_k.astype(jnp.bfloat16)
    rel_q_heads[...] = by_head(rel_q.astype(jnp.bfloat16))
    live = lax.broadcasted_iota(jnp.int32, (heads * QLEN, LANES), 1) < PLEN + QLEN
    above = jnp.zeros((PLEN, width), jnp.bfloat16)
    below = jnp.zeros((LANES - PLEN - QLEN, width), jnp.bfloat16)
    above_terms = jnp.zeros((PLEN, LANES), jnp.float32)
    below_terms = jnp.zeros((LANES - PLEN - QLEN, LANES), jnp.float32)
    scale = 1.0 / math.sqrt(3 * HD)

    def one_request(r, carry):
        rows = pl.ds(pl.multiple_of(r * QLEN, QLEN), QLEN)
        keys = qkv[rows, width : 2 * width]
        right = jnp.concatenate([above, keys, below, rel_k], axis=0)
        product = times_rows(by_head(qkv[rows, 0:width]), right)
        query_rel = product[:, LANES:]
        c2p = jnp.concatenate(
            [
                pltpu.roll(
                    query_rel[h * QLEN : (h + 1) * QLEN],
                    LANES - QLEN + 1,
                    1,
                    stride=1,
                    stride_axis=0,
                )
                for h in range(heads)
            ],
            axis=0,
        )
        terms = key_terms(keys, rel_q_heads[...], PLEN)
        p2c = jnp.concatenate([above_terms, terms, below_terms], axis=0).T[: heads * QLEN]
        logits = (product[:, :LANES] + c2p + p2c) * scale
        base[r] = jnp.where(live, logits, -jnp.inf)
        return carry

    lax.fori_loop(0, base.shape[0], one_request, 0, unroll=PREP_UNROLL)


def prepare(tokens, weight, rel_rows):
    rows = tokens.shape[0]
    width = weight.shape[1] // 3
    heads = width // HD
    return pl.pallas_call(
        prepare_kernel,
        out_shape=[
            jax.ShapeDtypeStruct((rows, 3 * width), jnp.bfloat16),
            jax.ShapeDtypeStruct((rows // QLEN, heads * QLEN, LANES), jnp.float32),
            jax.ShapeDtypeStruct((heads * LANES, width), jnp.bfloat16),
        ],
        in_specs=full_specs(3),
        out_specs=full_specs(3),
        compiler_params=params(12),
        cost_estimate=pl.CostEstimate(flops=4000 * MIB, bytes_accessed=4 * MIB, transcendentals=0),
        name="prepare",
    )(tokens, weight, rel_rows)


def attend_kernel(krow, qkv, base, rel_q_heads, *rest):
    pieces, (att, cache, arrived) = rest[:-3], rest[-3:]
    copies = [
        pltpu.make_async_copy(piece, cache.at[at], arrived.at[at]) for at, piece in enumerate(pieces)
    ]
    for copy in copies:
        copy.start()
    for copy in copies:
        copy.wait()
    width = att.shape[1]
    heads = width // HD
    held = cache.shape[2]
    padding = jnp.zeros((LANES - PLEN - QLEN, width), jnp.bfloat16)
    below = jnp.zeros((LANES - PLEN, width), jnp.bfloat16)
    below_terms = jnp.zeros((LANES - PLEN, LANES), jnp.float32)
    small_head = lax.broadcasted_iota(jnp.int32, (QLEN, width), 1) // HD
    scale = 1.0 / math.sqrt(3 * HD)

    def one_request(r, carry):
        rows = pl.ds(pl.multiple_of(r * QLEN, QLEN), QLEN)
        piece = krow[r] // held
        within = pl.ds(pl.multiple_of(krow[r] % held, PLEN), PLEN)
        keys = cache[piece, 0, within, :]
        content = times_rows(by_head(qkv[rows, 0:width]), jnp.concatenate([keys, below], axis=0))
        terms = key_terms(keys, rel_q_heads[...], 0)
        p2c = jnp.concatenate([terms, below_terms], axis=0).T[: heads * QLEN]
        logits = base[r] + (content + p2c) * scale
        largest = jnp.max(logits, axis=1, keepdims=True)
        weights = jnp.exp(logits - largest)
        denominator = jnp.sum(weights, axis=1, keepdims=True)
        values = jnp.concatenate(
            [cache[piece, 1, within, :], qkv[rows, 2 * width : 3 * width], padding], axis=0
        )
        summed = jnp.dot(weights.astype(jnp.bfloat16), values, preferred_element_type=jnp.float32)
        summed = summed * (1.0 / denominator)
        out = summed[:QLEN]
        for h in range(1, heads):
            out = jnp.where(small_head == h, summed[h * QLEN : (h + 1) * QLEN], out)
        att[rows, :] = out.astype(jnp.bfloat16)
        return carry

    lax.fori_loop(0, base.shape[0], one_request, 0, unroll=ATT_UNROLL)


def attend(krow, qkv, base, rel_q_heads, pieces):
    rows = qkv.shape[0]
    width = qkv.shape[1] // 3
    return pl.pallas_call(
        attend_kernel,
        out_shape=jax.ShapeDtypeStruct((rows, width), jnp.bfloat16),
        in_specs=[pl.BlockSpec(memory_space=pltpu.SMEM)]
        + full_specs(3)
        + [pl.BlockSpec(memory_space=pl.ANY)] * len(pieces),
        out_specs=pl.BlockSpec(memory_space=pltpu.VMEM),
        scratch_shapes=[
            pltpu.VMEM((len(pieces),) + pieces[0].shape, jnp.bfloat16),
            pltpu.SemaphoreType.DMA((len(pieces),)),
        ],
        compiler_params=params(12),
        cost_estimate=pl.CostEstimate(flops=2000 * MIB, bytes_accessed=2 * MIB, transcendentals=0),
        name="attend",
    )(krow, qkv, base, rel_q_heads, *pieces)


def norm_rows(values, gain):
    centre = values - jnp.mean(values, axis=-1, keepdims=True)
    spread = jnp.mean(centre * centre, axis=-1, keepdims=True)
    return centre * lax.rsqrt(spread + 1e-07) * gain


def feed_rows(start, count, a, w, tokens, gain, w_up, w_down):
    rows = pl.ds(pl.multiple_of(start, 32), count)
    mixed = tokens[rows, :].astype(jnp.float32)
    for piece, weight in zip(a, w):
        mixed = mixed + jnp.dot(piece[rows, :], weight[...], preferred_element_type=jnp.float32)
    hidden = norm_rows(mixed, gain[...]).astype(jnp.bfloat16)
    total = None
    step = 256
    for at in range(0, w_up.shape[1], step):
        up = jnp.dot(hidden, w_up[:, at : at + step], preferred_element_type=jnp.float32)
        inner = (0.5 * up * (1.0 + lax.erf(up * math.sqrt(0.5)))).astype(jnp.bfloat16)
        part = jnp.dot(inner, w_down[at : at + step, :], preferred_element_type=jnp.float32)
        total = part if total is None else total + part
    return hidden, total


def feed_other_kernel(start, a0, a1, a2, a3, w0, w1, w2, w3, tokens, gain, w_up, w_down, out):
    _, total = feed_rows(
        start[0], out.shape[0], (a0, a1, a2, a3), (w0, w1, w2, w3), tokens, gain, w_up, w_down
    )
    out[...] = total.astype(out.dtype)


def feed_own_kernel(start, a0, a1, a2, a3, w0, w1, w2, w3, tokens, gain, w_up, w_down, out, own):
    pieces, weights = (a0, a1, a2, a3), (w0, w1, w2, w3)
    count = out.shape[0]
    hidden, total = feed_rows(start[0], 2 * count, pieces, weights, tokens, gain, w_up, w_down)

    @pl.when(start[1] == 0)
    def first():
        out[...] = total[count:]
        own[...] = hidden[:count].astype(jnp.float32) + total[:count]

    @pl.when(start[1] != 0)
    def second():
        out[...] = total[:count]
        own[...] = hidden[count:].astype(jnp.float32) + total[count:]


def feed(kernel, start, pieces, weights, tokens, gain, w_up, w_down, outs, name):
    return pl.pallas_call(
        kernel,
        out_shape=outs,
        in_specs=[pl.BlockSpec(memory_space=pltpu.SMEM)] + full_specs(12),
        out_specs=full_specs(len(outs)),
        compiler_params=params(20),
        cost_estimate=pl.CostEstimate(flops=1600 * MIB, bytes_accessed=6 * MIB, transcendentals=0),
        name=name,
    )(start, *pieces, *weights, tokens, gain, w_up, w_down)


def project_kernel(own, from_core, from_y, gain, w_proj, out):
    after = own[...] + from_core[...].astype(jnp.float32) + from_y[...].astype(jnp.float32)
    hidden = norm_rows(after, gain[...]).astype(jnp.bfloat16)
    projected = jnp.dot(hidden, w_proj[...], preferred_element_type=jnp.float32)
    length = jnp.sum(projected * projected, axis=-1, keepdims=True)
    vectors = (projected * lax.rsqrt(length + 1e-06)).astype(jnp.bfloat16)
    for place in range(out.shape[0]):
        out[place] = vectors


def score_kernel(slots, count, lengths, queries, docs, out):
    shape = (8, LANES)
    flat = lax.broadcasted_iota(jnp.int32, shape, 0) * LANES + lax.broadcasted_iota(jnp.int32, shape, 1)
    position = lax.broadcasted_iota(jnp.int32, (QLEN, docs.shape[1]), 1)
    unroll = 16

    def some(i, totals):
        for u in range(unroll):
            packed = slots[i * unroll + u]
            entry = packed & 4095
            group = (packed >> 12) & 255
            doc = packed >> 20
            query = queries[pl.ds(pl.multiple_of(group * QLEN, QLEN), QLEN), :]
            sims = lax.dot_general(
                query, docs[doc], (((1,), (1,)), ((), ())), preferred_element_type=jnp.float32
            )
            sims = jnp.where(position < lengths[doc], sims, -jnp.inf)
            best = jnp.max(sims, axis=1, keepdims=True)
            total = jnp.sum(best, axis=0, keepdims=True)
            totals = jnp.where(flat == entry, total, totals)
        return totals

    totals = lax.fori_loop(
        0, (count[0] + unroll - 1) // unroll, some, jnp.zeros(shape, jnp.float32)
    )
    for o in range(out.shape[0]):
        row = jnp.broadcast_to(totals[o : o + 1], shape)
        for h in range(out.shape[1]):
            out[o, h] = row


def collect_kernel(place, tiles, out):
    n_head = tiles.shape[1]
    cols = out.shape[1]
    reqs = out.shape[0] // n_head
    for h in range(n_head):
        total = tiles[0, h]
        for o in range(1, tiles.shape[0]):
            total = total + tiles[o, h]
        total = pltpu.roll(total, LANES - place[0] * (reqs * cols), 1)
        at = (h % 2 * 2 + h // 2) * reqs
        for r in range(reqs):
            row = total if r == 0 else pltpu.roll(total, LANES - r * cols, 1)
            out[at + r : at + r + 1, :] = row[:1, :cols]


def body(
    tokens,
    w_qkv,
    w_out,
    w_up,
    w_down,
    gain_one,
    gain_two,
    rel_table,
    prompt_cache,
    w_proj,
    doc_vectors,
    doc_lengths,
    group_ids,
    candidates,
):
    rows = tokens.shape[0]
    width = w_qkv.shape[2]
    n_doc = lax.axis_size("doc")
    n_head = lax.axis_size("head")
    me = lax.axis_index("doc")
    place = lax.axis_index("head")
    own_y, own_c = place // 2, place % 2
    half, quarter = rows // 2, rows // 4

    def over_doc(x, k):
        return lax.ppermute(x, "doc", [(i, i ^ k) for i in range(n_doc)])

    def over_head(x, k):
        return lax.ppermute(x, "head", [(i, i ^ k) for i in range(n_head)])

    along_z = [prompt_cache] + [over_doc(prompt_cache, k) for k in (2, 4, 6)]
    pieces = along_z + [over_doc(piece, 1) for piece in along_z]
    held = prompt_cache.shape[1]
    groups_dev = held // PLEN
    relative = (group_ids // groups_dev) ^ me
    krow = (relative // 2 + relative % 2 * (n_doc // 2)) * held + group_ids % groups_dev * PLEN

    weight = w_qkv.reshape(w_qkv.shape[0], 3 * width)
    low = RELS // 2 - PLEN - QLEN
    qkv, base, rel_q_heads = prepare(tokens, weight, rel_table[low : low + 2 * (PLEN + QLEN)])

    reqs = candidates.shape[0] // n_head
    cols = candidates.shape[1]
    sent = candidates.reshape(2, 2, reqs * cols).transpose(1, 0, 2).reshape(1, n_head, reqs * cols)
    sent = jnp.broadcast_to(sent, (n_doc, n_head, reqs * cols)).reshape(n_doc * n_head, reqs * cols)
    entries = lax.all_to_all(sent, ("doc", "head"), 0, 0, tiled=True).reshape(n_doc, n_head * reqs * cols)
    block = n_head * reqs * cols
    doc_at = jnp.arange(n_doc, dtype=jnp.int32)[:, None]
    entry_at = jnp.arange(block, dtype=jnp.int32)[None, :]
    group_at = doc_at * reqs + entry_at // cols % reqs
    packed = (doc_at * LANES + entry_at) | (group_at << 12) | ((entries % DOC_DEV) << 20)
    packed = packed.reshape(-1)
    mine = (entries // DOC_DEV == me).reshape(-1)
    rank = jnp.cumsum(mine.astype(jnp.int32)) - 1
    total_slots = n_doc * block
    chosen = mine[None, :] & (rank[None, :] == jnp.arange(total_slots, dtype=jnp.int32)[:, None])
    slots = jnp.sum(jnp.where(chosen, packed[None, :], 0), axis=1)
    count = jnp.sum(mine.astype(jnp.int32))
    slots = jnp.where(jnp.arange(total_slots) < count, slots, LANES - 1)

    out_one = over_head(w_out, 2)
    out_pieces = [w_out, over_head(w_out, 1), out_one, over_head(out_one, 1)]

    att = attend(krow, qkv, base, rel_q_heads, pieces)
    att_y = over_head(att, 2)
    att_pieces = [att, over_head(att, 1), att_y, over_head(att_y, 1)]

    gain_rows = gain_one.reshape(1, -1)
    common = (att_pieces, out_pieces, tokens, gain_rows, w_up, w_down)
    start_other = ((1 - own_c) * half).astype(jnp.int32).reshape(1)
    other = feed(
        feed_other_kernel,
        start_other,
        *common,
        [jax.ShapeDtypeStruct((half, tokens.shape[1]), jnp.bfloat16)],
        "feed_other",
    )[0]
    from_core = over_head(other, 1)
    start_own = jnp.stack([own_c * half, own_y]).astype(jnp.int32)
    for_y, own = feed(
        feed_own_kernel,
        start_own,
        *common,
        [jax.ShapeDtypeStruct((quarter, tokens.shape[1]), jnp.float32)] * 2,
        "feed_own",
    )
    core_y = lax.dynamic_slice_in_dim(from_core, (1 - own_y) * quarter, quarter, 0)
    core_own = lax.dynamic_slice_in_dim(from_core, own_y * quarter, quarter, 0)
    from_y = over_head((for_y + core_y.astype(jnp.float32)).astype(jnp.bfloat16), 2)

    emb = w_proj.shape[1]
    vectors = pl.pallas_call(
        project_kernel,
        out_shape=jax.ShapeDtypeStruct((n_doc, quarter, emb), jnp.bfloat16),
        in_specs=full_specs(5),
        out_specs=full_specs(1)[0],
        compiler_params=params(8),
        name="project",
    )(own, core_own, from_y, gain_two.reshape(1, -1), w_proj)
    queries = lax.all_to_all(vectors, "doc", 0, 0, tiled=True).reshape(n_doc * quarter, emb)

    mine_rows = vectors[0]
    y_rows = over_head(mine_rows, 2)
    pair = jnp.where(
        own_y == 0, jnp.concatenate([mine_rows, y_rows]), jnp.concatenate([y_rows, mine_rows])
    )
    core_pair = over_head(pair, 1)
    query_vectors = jnp.where(
        own_c == 0, jnp.concatenate([pair, core_pair]), jnp.concatenate([core_pair, pair])
    )

    smem = pl.BlockSpec(memory_space=pltpu.SMEM)
    rated = pl.pallas_call(
        score_kernel,
        out_shape=jax.ShapeDtypeStruct((n_doc, n_head, 8, LANES), jnp.float32),
        in_specs=[smem, smem, smem] + full_specs(2),
        out_specs=full_specs(1)[0],
        compiler_params=params(8),
        name="rate",
    )(slots, count.reshape(1), doc_lengths, queries, doc_vectors)
    tiles = rated.reshape(n_doc * n_head * 8, LANES)
    back = lax.all_to_all(tiles, ("doc", "head"), 0, 0, tiled=True)
    scores = pl.pallas_call(
        collect_kernel,
        out_shape=jax.ShapeDtypeStruct(candidates.shape, jnp.float32),
        in_specs=[smem] + full_specs(1),
        out_specs=full_specs(1)[0],
        compiler_params=params(4),
        name="collect",
    )(place.reshape(1), back.reshape(n_doc, n_head, 8, LANES))
    return (query_vectors, scores)


def solution(mesh):
    placed = (
        P("doc", None),
        P(None, None, "head"),
        P("head", None),
        P(None, "head"),
        P("head", None),
        P(),
        P(),
        P(),
        P(None, "doc", "head"),
        P(),
        P("doc", None, None),
        P("doc"),
        P("doc"),
        P("doc", "head"),
    )
    fits = mesh.shape["head"] == 4 and mesh.shape["doc"] == 8
    return jax.shard_map(
        body if fits else body_any,
        mesh=mesh,
        in_specs=placed,
        out_specs=(P("doc", None), P("doc", "head")),
        check_vma=False,
    )
```

```python
import functools
import math

import jax
import jax.numpy as jnp
from jax import lax
from jax.experimental import pallas as pl
from jax.experimental.pallas import tpu as pltpu
from jax.sharding import PartitionSpec as P

HD = 64
RELS = 512
QLEN = 32
PLEN = 64
DOC_DEV = 64


def layer_norm(values, gain):
    centre = values - jnp.mean(values, axis=-1, keepdims=True)
    spread = jnp.mean(centre * centre, axis=-1, keepdims=True)
    return centre * lax.rsqrt(spread + 1e-07) * gain


def slot_order(holders):
    count = holders.shape[0]
    same = holders[:, None] == holders[None, :]
    earlier = jnp.arange(count)[:, None] > jnp.arange(count)[None, :]
    return jnp.sum(same & earlier, axis=1)


def rate_slots(slot_query, slot_doc, doc_vectors, doc_lengths):
    shape = slot_doc.shape
    flat_doc = slot_doc.reshape(-1)
    flat_query = slot_query.reshape((flat_doc.shape[0],) + slot_query.shape[-2:])
    safe_doc = jnp.maximum(flat_doc, 0)
    documents = doc_vectors[safe_doc]
    lengths = doc_lengths[safe_doc]
    sims = jnp.einsum("sqe,sje->sqj", flat_query, documents, preferred_element_type=jnp.float32)
    live = jnp.arange(documents.shape[1], dtype=jnp.int32)[None, None, :] < lengths[:, None, None]
    best = jnp.max(jnp.where(live, sims, -jnp.inf), axis=2)
    totals = jnp.where(flat_doc >= 0, jnp.sum(best, axis=1), 0.0)
    return totals.reshape(shape)


def body_any(
    tokens,
    w_qkv,
    w_out,
    w_up,
    w_down,
    gain_one,
    gain_two,
    rel_table,
    prompt_cache,
    w_proj,
    doc_vectors,
    doc_lengths,
    group_ids,
    candidates,
):
    rows_dev = tokens.shape[0]
    req_dev = rows_dev // QLEN
    width = w_qkv.shape[2]
    heads_loc = width // HD
    half = RELS // 2
    scale_root = math.sqrt(3 * HD)
    gathered = lax.all_gather(prompt_cache, "doc", axis=1, tiled=True)
    weights_split = w_qkv.reshape(w_qkv.shape[0], 3, heads_loc, HD)
    projected_all = jnp.einsum(
        "td,dchf->chtf", tokens, weights_split, preferred_element_type=jnp.float32
    ).astype(jnp.bfloat16)
    rel_both = jnp.einsum(
        "rd,dchf->chrf", rel_table, weights_split[:, :2], preferred_element_type=jnp.float32
    ).astype(jnp.bfloat16)
    head_shape = (heads_loc, req_dev, QLEN, HD)
    query_four = projected_all[0].reshape(head_shape)
    keys_four = projected_all[1].reshape(head_shape)
    values_four = projected_all[2].reshape(head_shape)
    groups_all = gathered.shape[1] // PLEN
    cache_all = gathered.reshape(2, groups_all, PLEN, heads_loc, HD)
    picked = jnp.transpose(cache_all[:, group_ids], (0, 3, 1, 2, 4))
    keys = jnp.concatenate([keys_four, picked[0]], axis=2)
    values = jnp.concatenate([values_four, picked[1]], axis=2)
    pos_query = PLEN + jnp.arange(QLEN, dtype=jnp.int32)
    pos_key = jnp.concatenate([pos_query, jnp.arange(PLEN, dtype=jnp.int32)])
    index_one = pos_query[:, None] - pos_key[None, :] + half
    index_two = pos_key[:, None] - pos_query[None, :] + half
    rel_k_rows = rel_both[1][:, index_one]
    rel_q_rows = rel_both[0][:, index_two]
    c2p = jnp.einsum("hrqd,hqkd->hrqk", query_four, rel_k_rows, preferred_element_type=jnp.float32)
    p2c = jnp.einsum("hrkd,hkqd->hrqk", keys, rel_q_rows, preferred_element_type=jnp.float32)
    content = jnp.einsum("hrqd,hrkd->hrqk", query_four, keys, preferred_element_type=jnp.float32)
    logits = (content + c2p + p2c) / scale_root
    largest = jnp.max(logits, axis=-1, keepdims=True)
    weights = jnp.exp(logits - largest)
    denominator = jnp.sum(weights, axis=-1)
    summed = jnp.einsum(
        "hrqk,hrkd->hrqd", weights.astype(jnp.bfloat16), values, preferred_element_type=jnp.float32
    )
    attended = (summed / denominator[..., None]).astype(jnp.bfloat16)
    out_split = w_out.reshape(heads_loc, HD, w_out.shape[1])
    attn_part = jnp.einsum(
        "hrqd,hde->rqe", attended, out_split, preferred_element_type=jnp.float32
    ).reshape(rows_dev, w_out.shape[1])
    attn_total = lax.psum(attn_part.astype(jnp.bfloat16), "head").astype(jnp.float32)
    hidden_one = layer_norm(tokens.astype(jnp.float32) + attn_total, gain_one).astype(jnp.bfloat16)
    inner = jax.nn.gelu(
        jnp.dot(hidden_one, w_up, preferred_element_type=jnp.float32), approximate=False
    ).astype(jnp.bfloat16)
    ffn_total = lax.psum(
        jnp.dot(inner, w_down, preferred_element_type=jnp.float32).astype(jnp.bfloat16), "head"
    ).astype(jnp.float32)
    hidden_two = layer_norm(hidden_one.astype(jnp.float32) + ffn_total, gain_two).astype(
        jnp.bfloat16
    )
    projected = jnp.dot(hidden_two, w_proj, preferred_element_type=jnp.float32)
    query_vectors = (
        projected * lax.rsqrt(jnp.sum(projected * projected, axis=-1, keepdims=True) + 1e-06)
    ).astype(jnp.bfloat16)
    shards = lax.axis_size("doc")
    cand_dev = candidates.shape[1]
    pairs = req_dev * cand_dev
    capacity = max(2, 2 * pairs // shards)
    flat_cand = candidates.reshape(-1)
    holders = flat_cand // DOC_DEV
    request_of = jnp.arange(pairs, dtype=jnp.int32) // cand_dev
    slot_rank = slot_order(holders)
    copies, cand_copies = (
        lax.all_gather(query_vectors, "doc", axis=0, tiled=True),
        lax.all_gather(candidates, "doc", axis=0, tiled=True),
    )
    all_query = copies.reshape(shards, req_dev, QLEN, copies.shape[1])
    all_cand = cand_copies.reshape(shards, pairs)
    holder_all = all_cand // DOC_DEV
    local_all = all_cand % DOC_DEV
    rank_all = jax.vmap(slot_order)(holder_all)
    own_index = lax.axis_index("doc")
    chosen = (holder_all[:, None, :] == own_index) & (
        rank_all[:, None, :] == jnp.arange(capacity, dtype=jnp.int32)[None, :, None]
    )
    filled = jnp.any(chosen, axis=2)
    slot_request = jnp.sum(jnp.where(chosen, request_of[None, None, :], 0), axis=2)
    slot_doc = jnp.where(
        filled, jnp.sum(jnp.where(chosen, local_all[:, None, :], 0), axis=2), -1
    ).astype(jnp.int32)
    slot_query = all_query[jnp.arange(shards)[:, None], slot_request]
    slot_scores = rate_slots(slot_query, slot_doc, doc_vectors, doc_lengths)
    returned = lax.all_to_all(slot_scores, "doc", split_axis=0, concat_axis=0, tiled=True)
    scores = returned.reshape(-1)[holders * capacity + slot_rank].reshape(candidates.shape)
    return (query_vectors, scores)


LANES = 128
MIB = 1 << 20
EXTRA = 16
PREP_UNROLL = 6
ATT_UNROLL = 6
SCORE_UNROLL = 16


def full_specs(count):
    return [pl.BlockSpec(memory_space=pltpu.VMEM)] * count


def params(mib):
    return pltpu.CompilerParams(vmem_limit_bytes=mib * MIB)


def by_head(values):
    head_of = lax.broadcasted_iota(jnp.int32, values.shape, 1) // HD
    heads = values.shape[1] // HD
    zero = jnp.zeros_like(values)
    return jnp.concatenate([jnp.where(head_of == h, values, zero) for h in range(heads)], axis=0)


def times_rows(left, right):
    return lax.dot_general(left, right, (((1,), (1,)), ((), ())), preferred_element_type=jnp.float32)


def key_terms(key_rel, first):
    slot = lax.broadcasted_iota(jnp.int32, (key_rel.shape[0], LANES), 1) // QLEN
    turned = None
    for h in range(key_rel.shape[1] // LANES):
        shift = (LANES - PLEN - QLEN + first + h * QLEN) % LANES
        rolled = pltpu.roll(
            key_rel[:, h * LANES : (h + 1) * LANES], shift, 1, stride=1, stride_axis=0
        )
        turned = rolled if turned is None else jnp.where(slot == h, rolled, turned)
    return turned


def prepare_kernel(tokens, weight, rel_table, qkv, base, rel_q_heads, q_heads, query_rel, key_rel):
    width = weight.shape[2]
    heads = width // HD
    for i in range(3):
        qkv[:, i * width : (i + 1) * width] = jnp.dot(
            tokens[...], weight[i], preferred_element_type=jnp.float32
        ).astype(jnp.bfloat16)
    count = 2 * (PLEN + QLEN)
    low = RELS // 2 - PLEN - QLEN
    rel = [
        jnp.dot(
            rel_table[low : low + count, :], weight[i], preferred_element_type=jnp.float32
        ).astype(jnp.bfloat16)
        for i in range(2)
    ]
    both = lax.broadcasted_iota(jnp.int32, (LANES, count), 0) + lax.broadcasted_iota(
        jnp.int32, (LANES, count), 1
    )
    flip_q = jnp.where(both == LANES, 1.0, 0.0).astype(jnp.bfloat16)
    flip_k = jnp.where(both == LANES + PLEN - 1, 1.0, 0.0).astype(jnp.bfloat16)
    rel_q = jnp.dot(flip_q, rel[0], preferred_element_type=jnp.float32)
    rel_k = jnp.dot(flip_k, rel[1], preferred_element_type=jnp.float32)
    rel_q_heads[...] = by_head(rel_q.astype(jnp.bfloat16))
    requests, many, _ = base.shape
    for r in range(requests):
        q_heads[r * many : (r + 1) * many, :] = by_head(qkv[r * QLEN : (r + 1) * QLEN, :width])
    query_rel[...] = times_rows(q_heads[...], rel_k.astype(jnp.bfloat16))
    key_rel[...] = times_rows(qkv[:, width : 2 * width], rel_q_heads[...])
    live = lax.broadcasted_iota(jnp.int32, (many, LANES), 1) < PLEN + QLEN
    above = jnp.zeros((PLEN, LANES), jnp.float32)
    below = jnp.zeros((LANES - PLEN - QLEN, LANES), jnp.float32)
    scale = 1.0 / math.sqrt(3 * HD)

    def one_request(r, carry):
        rows = pl.ds(pl.multiple_of(r * QLEN, QLEN), QLEN)
        spread = pl.ds(pl.multiple_of(r * many, many), many)
        turned = times_rows(qkv[rows, width : 2 * width], q_heads[spread, :])
        turned = turned + key_terms(key_rel[rows, :], PLEN)
        own = jnp.concatenate([above, turned, below], axis=0).T[:many]
        spread_rel = query_rel[spread, :]
        c2p = jnp.concatenate(
            [
                pltpu.roll(
                    spread_rel[h * QLEN : (h + 1) * QLEN],
                    LANES - QLEN + 1,
                    1,
                    stride=1,
                    stride_axis=0,
                )
                for h in range(heads)
            ],
            axis=0,
        )
        base[r] = jnp.where(live, (own + c2p) * scale, -jnp.inf)
        return carry

    lax.fori_loop(0, requests, one_request, 0, unroll=PREP_UNROLL)


def prepare(tokens, weight, rel_table):
    rows = tokens.shape[0]
    width = weight.shape[2]
    heads = width // HD
    return pl.pallas_call(
        prepare_kernel,
        out_shape=[
            jax.ShapeDtypeStruct((rows, 3 * width), jnp.bfloat16),
            jax.ShapeDtypeStruct((rows // QLEN, heads * QLEN, LANES), jnp.float32),
            jax.ShapeDtypeStruct((heads * LANES, width), jnp.bfloat16),
        ],
        in_specs=full_specs(3),
        out_specs=full_specs(3),
        scratch_shapes=[
            pltpu.VMEM((rows * heads, width), jnp.bfloat16),
            pltpu.VMEM((rows * heads, LANES), jnp.float32),
            pltpu.VMEM((rows, heads * LANES), jnp.float32),
        ],
        compiler_params=params(12),
        cost_estimate=pl.CostEstimate(flops=4000 * MIB, bytes_accessed=4 * MIB, transcendentals=0),
        name="prepare",
    )(tokens, weight, rel_table)


def attend_kernel(group_ids, qkv, base, rel_q_heads, columns, *rest):
    pieces, (att, cache, picked, key_rel, arrived) = rest[:-5], rest[-5:]
    copies = [
        [
            pltpu.make_async_copy(piece.at[kind], cache.at[kind, at], arrived.at[kind, at])
            for at, piece in enumerate(pieces)
        ]
        for kind in range(2)
    ]
    for copy in copies[0] + copies[1]:
        copy.start()
    requests, _, _ = base.shape
    tokens = requests * QLEN
    ids = columns[...].T
    spare = jnp.zeros((1, LANES - columns.shape[0] * columns.shape[1]), jnp.int32)
    line = jnp.concatenate([ids[r : r + 1, :] for r in range(ids.shape[0])] + [spare], axis=1)
    line = jnp.concatenate([line // DOC_DEV, line % DOC_DEV], axis=1)
    extra = jnp.broadcast_to(line.astype(jnp.float32), (EXTRA, line.shape[1]))
    att[tokens:, :] = extra.astype(att.dtype)
    width = att.shape[1]
    heads = width // HD
    groups_dev = cache.shape[2] // PLEN
    me = lax.axis_index("doc")
    padding = jnp.zeros((LANES - PLEN - QLEN, width), jnp.bfloat16)
    below_terms = jnp.zeros((LANES - PLEN, LANES), jnp.float32)
    small_head = lax.broadcasted_iota(jnp.int32, (QLEN, width), 1) // HD
    scale = 1.0 / math.sqrt(3 * HD)

    def place_of(r):
        owner = group_ids[r] // groups_dev
        within = pl.multiple_of((group_ids[r] - owner * groups_dev) * PLEN, PLEN)
        return owner ^ me, pl.ds(within, PLEN)

    for copy in copies[0]:
        copy.wait()
    for r in range(requests):
        piece, within = place_of(r)
        picked[r * PLEN : (r + 1) * PLEN, :] = cache[0, piece, within, :]
    key_rel[...] = times_rows(picked[...], rel_q_heads[...])
    for copy in copies[1]:
        copy.wait()

    def one_request(r, carry):
        rows = pl.ds(pl.multiple_of(r * QLEN, QLEN), QLEN)
        cached = pl.ds(pl.multiple_of(r * PLEN, PLEN), PLEN)
        turned = times_rows(picked[cached, :], by_head(qkv[rows, 0:width]))
        turned = (turned + key_terms(key_rel[cached, :], 0)) * scale
        logits = base[r] + jnp.concatenate([turned, below_terms], axis=0).T[: heads * QLEN]
        largest = jnp.max(logits, axis=1, keepdims=True)
        weights = jnp.exp(logits - largest)
        weights = weights * (1.0 / jnp.sum(weights, axis=1, keepdims=True))
        piece, within = place_of(r)
        values = jnp.concatenate(
            [cache[1, piece, within, :], qkv[rows, 2 * width : 3 * width], padding], axis=0
        )
        summed = jnp.dot(weights.astype(jnp.bfloat16), values, preferred_element_type=jnp.float32)
        out = summed[:QLEN]
        for h in range(1, heads):
            out = jnp.where(small_head == h, summed[h * QLEN : (h + 1) * QLEN], out)
        att[rows, :] = out.astype(jnp.bfloat16)
        return carry

    lax.fori_loop(0, requests, one_request, 0, unroll=ATT_UNROLL)


def attend(group_ids, qkv, base, rel_q_heads, columns, pieces):
    rows = qkv.shape[0]
    width = qkv.shape[1] // 3
    cached = rows // QLEN * PLEN
    return pl.pallas_call(
        attend_kernel,
        out_shape=jax.ShapeDtypeStruct((rows + EXTRA, width), jnp.bfloat16),
        in_specs=[pl.BlockSpec(memory_space=pltpu.SMEM)]
        + full_specs(4)
        + [pl.BlockSpec(memory_space=pl.ANY)] * len(pieces),
        out_specs=pl.BlockSpec(memory_space=pltpu.VMEM),
        scratch_shapes=[
            pltpu.VMEM((2, len(pieces)) + pieces[0].shape[1:], jnp.bfloat16),
            pltpu.VMEM((cached, width), jnp.bfloat16),
            pltpu.VMEM((cached, rel_q_heads.shape[0]), jnp.float32),
            pltpu.SemaphoreType.DMA((2, len(pieces))),
        ],
        compiler_params=params(12),
        cost_estimate=pl.CostEstimate(flops=2000 * MIB, bytes_accessed=2 * MIB, transcendentals=0),
        name="attend",
    )(group_ids, qkv, base, rel_q_heads, columns, *pieces)


def norm_rows(values, gain):
    centre = values - jnp.mean(values, axis=-1, keepdims=True)
    spread = jnp.mean(centre * centre, axis=-1, keepdims=True)
    return centre * lax.rsqrt(spread + 1e-07) * gain


def feed_rows(start, count, a, w, tokens, gain, w_up, w_down):
    rows = pl.ds(pl.multiple_of(start, 32), count)
    mixed = tokens[rows, :].astype(jnp.float32)
    for piece, weight in zip(a, w):
        mixed = mixed + jnp.dot(piece[rows, :], weight[...], preferred_element_type=jnp.float32)
    hidden = norm_rows(mixed, gain[...]).astype(jnp.bfloat16)
    total = None
    step = 256
    for at in range(0, w_up.shape[1], step):
        up = jnp.dot(hidden, w_up[:, at : at + step], preferred_element_type=jnp.float32)
        inner = (0.5 * up * (1.0 + lax.erf(up * math.sqrt(0.5)))).astype(jnp.bfloat16)
        part = jnp.dot(inner, w_down[at : at + step, :], preferred_element_type=jnp.float32)
        total = part if total is None else total + part
    return hidden, total


def feed_other_kernel(a0, a1, a2, a3, w0, w1, w2, w3, tokens, gain, w_up, w_down, out):
    core = lax.axis_index("head") % 2
    _, total = feed_rows(
        (1 - core) * out.shape[0], out.shape[0], (a0, a1, a2, a3), (w0, w1, w2, w3), tokens, gain, w_up, w_down
    )
    out[...] = total.astype(out.dtype)


def feed_own_kernel(a0, a1, a2, a3, w0, w1, w2, w3, tokens, gain, w_up, w_down, out, own):
    pieces, weights = (a0, a1, a2, a3), (w0, w1, w2, w3)
    count = out.shape[0]
    place = lax.axis_index("head")
    start = place % 2 * (2 * count)
    hidden, total = feed_rows(start, 2 * count, pieces, weights, tokens, gain, w_up, w_down)

    @pl.when(place // 2 == 0)
    def first():
        out[...] = total[count:]
        own[...] = hidden[:count].astype(jnp.float32) + total[:count]

    @pl.when(place // 2 != 0)
    def second():
        out[...] = total[:count]
        own[...] = hidden[count:].astype(jnp.float32) + total[count:]


def feed(kernel, pieces, weights, tokens, gain, w_up, w_down, outs, name):
    return pl.pallas_call(
        kernel,
        out_shape=outs,
        in_specs=full_specs(12),
        out_specs=full_specs(len(outs)),
        compiler_params=params(20),
        cost_estimate=pl.CostEstimate(flops=1600 * MIB, bytes_accessed=6 * MIB, transcendentals=0),
        name=name,
    )(*pieces, *weights, tokens, gain, w_up, w_down)


def fold_kernel(for_y, from_core, out):
    count = out.shape[0]
    other = 1 - lax.axis_index("head") // 2
    rows = pl.ds(pl.multiple_of(other * count, 32), count)
    out[...] = (for_y[...] + from_core[rows, :].astype(jnp.float32)).astype(out.dtype)


def block_of(head):
    return head % 2 * 2 + head // 2


def project_kernel(own, from_core, from_y, gain, w_proj, a0, a1, a2, a3, out, single):
    count = own.shape[0]
    place = lax.axis_index("head")
    rows = pl.ds(pl.multiple_of(place // 2 * count, 32), count)
    after = own[...] + from_core[rows, :].astype(jnp.float32) + from_y[...].astype(jnp.float32)
    hidden = norm_rows(after, gain[...]).astype(jnp.bfloat16)
    projected = jnp.dot(hidden, w_proj[...], preferred_element_type=jnp.float32)
    length = jnp.sum(projected * projected, axis=-1, keepdims=True)
    vectors = (projected * lax.rsqrt(length + 1e-06)).astype(jnp.bfloat16)
    single[...] = vectors
    pieces = (a0, a1, a2, a3)
    part = LANES // len(pieces) * 3 // 4
    lane = lax.broadcasted_iota(jnp.int32, (EXTRA, LANES), 1)
    lines = []
    for kind in range(2):
        line = jnp.zeros((EXTRA, LANES), jnp.float32)
        for x, piece in enumerate(pieces):
            from_head = place ^ x
            values = piece[piece.shape[0] - EXTRA :, kind * LANES : (kind + 1) * LANES]
            shift = lax.rem((from_head - block_of(place)) * part + LANES, LANES)
            rolled = pltpu.roll(values.astype(jnp.float32), shift, 1)
            line = jnp.where(lane // part == from_head, rolled, line)
        lines.append(line)
    which = lax.broadcasted_iota(jnp.int32, (EXTRA, LANES), 0)
    tail = jnp.where(which == 0, lines[0], lines[1]).astype(out.dtype)
    for o in range(out.shape[0]):
        out[o, :count] = vectors
        out[o, count:] = tail


def make_slots(queries, n_doc):
    rows = queries.shape[0] // n_doc
    part = (rows - EXTRA) // QLEN * 8
    me = lax.axis_index("doc")
    shape = (n_doc, LANES)
    lane = lax.broadcasted_iota(jnp.int32, shape, 1)
    row = lax.broadcasted_iota(jnp.int32, shape, 0)
    tails = [
        queries[o * rows + rows - EXTRA : (o + 1) * rows, :].astype(jnp.float32) for o in range(n_doc)
    ]
    holder = jnp.concatenate([tail[:1] for tail in tails], axis=0).astype(jnp.int32)
    doc = jnp.concatenate([tail[1:2] for tail in tails], axis=0).astype(jnp.int32)
    mine = (lane < 4 * part) & (holder == me)
    entry = row * LANES + lane
    group = (row * rows + lane % part // 8 * QLEN) // 16
    packed = entry | (group << 12) | (doc << 20)
    ones = jnp.where(mine, 1.0, 0.0)
    earlier = lax.broadcasted_iota(jnp.int32, (LANES, LANES), 0) < lax.broadcasted_iota(
        jnp.int32, (LANES, LANES), 1
    )
    before = jnp.where(earlier, 1.0, 0.0).astype(jnp.bfloat16)
    rank = jnp.dot(ones.astype(jnp.bfloat16), before, preferred_element_type=jnp.float32)
    in_row = jnp.sum(ones, axis=1, keepdims=True)
    above = jnp.zeros((1, 1), jnp.float32)
    starts = []
    for o in range(n_doc):
        starts.append(above)
        above = above + in_row[o : o + 1]
    rank = (rank + jnp.concatenate(starts, axis=0)).astype(jnp.int32)
    rank = jnp.where(mine, rank, -1)
    pad = jnp.zeros((LANES - n_doc, LANES), jnp.int32)
    rank_columns = jnp.concatenate([rank, pad], axis=0).T
    packed_columns = jnp.concatenate([packed, pad], axis=0).T
    square_lane = lax.broadcasted_iota(jnp.int32, (LANES, LANES), 1)
    lines = []
    for block in range(n_doc * 4 * part // LANES):
        total = jnp.zeros((LANES, LANES), jnp.int32)
        for o in range(n_doc):
            hit = rank_columns[:, o : o + 1] == square_lane + block * LANES
            total = total + jnp.where(hit, packed_columns[:, o : o + 1], 0)
        lines.append(jnp.sum(total, axis=0, keepdims=True))
    count = jnp.broadcast_to(above.astype(jnp.int32), (8 - len(lines), LANES))
    return jnp.concatenate(lines + [count], axis=0)


def score_kernel(lengths, queries, docs, out, held, listed, slots, arrived, ready):
    chunks = arrived.shape[0]
    per = docs.shape[0] // chunks
    copies = [
        pltpu.make_async_copy(
            docs.at[pl.ds(c * per, per)], held.at[pl.ds(c * per, per)], arrived.at[c]
        )
        for c in range(chunks)
    ]
    for copy in copies:
        copy.start()
    listed[...] = make_slots(queries, out.shape[0])
    to_scalars = pltpu.make_async_copy(listed, slots, ready)
    to_scalars.start()
    to_scalars.wait()
    for copy in copies:
        copy.wait()

    shape = (8, LANES)
    flat = lax.broadcasted_iota(jnp.int32, shape, 0) * LANES + lax.broadcasted_iota(jnp.int32, shape, 1)
    position = lax.broadcasted_iota(jnp.int32, (QLEN, docs.shape[1]), 1)
    unroll = SCORE_UNROLL
    count = slots[slots.shape[0] - 1, 0]

    def packed_of(s):
        return slots[s // LANES, s % LANES]

    def some(i, totals):
        for u in range(unroll):
            packed = packed_of(i * unroll + u)
            entry = jnp.where(i * unroll + u < count, packed & 4095, shape[0] * LANES)
            group = (packed >> 12) & 255
            doc = packed >> 20
            query = queries[pl.ds(pl.multiple_of(group * 16, 16), QLEN), :]
            sims = times_rows(query, held[doc])
            sims = jnp.where(position < lengths[doc], sims, -jnp.inf)
            best = jnp.max(sims, axis=1, keepdims=True)
            total = jnp.sum(best, axis=0, keepdims=True)
            totals = jnp.where(flat == entry, total, totals)
        return totals

    totals = lax.fori_loop(
        0, (count + unroll - 1) // unroll, some, jnp.zeros(shape, jnp.float32)
    )
    for o in range(out.shape[0]):
        row = jnp.broadcast_to(totals[o : o + 1], shape)
        for h in range(out.shape[1]):
            out[o, h] = row


def collect_kernel(tiles, out):
    n_head = tiles.shape[1]
    cols, reqs_all = out.shape
    reqs = reqs_all // n_head
    place = lax.axis_index("head")
    lines = []
    for h in range(n_head):
        total = tiles[0, h]
        for o in range(1, tiles.shape[0]):
            total = total + tiles[o, h]
        total = pltpu.roll(total, LANES - place * (reqs * cols), 1)
        lines.append(total[:1, : reqs * cols])
    order = sorted(range(n_head), key=block_of)
    rows = [lines[h][:, r * cols : (r + 1) * cols] for h in order for r in range(reqs)]
    out[...] = jnp.concatenate(rows, axis=0).T


def body(
    tokens,
    w_qkv,
    w_out,
    w_up,
    w_down,
    gain_one,
    gain_two,
    rel_table,
    prompt_cache,
    w_proj,
    doc_vectors,
    doc_lengths,
    group_ids,
    candidates,
):
    rows, depth = tokens.shape
    n_doc = lax.axis_size("doc")
    n_head = lax.axis_size("head")
    half, quarter = rows // 2, rows // n_head
    cand_rows, cols = candidates.shape
    reqs = cand_rows // n_head
    smem = pl.BlockSpec(memory_space=pltpu.SMEM)

    def over_doc(x, k):
        return lax.ppermute(x, "doc", [(i, i ^ k) for i in range(n_doc)])

    def over_head(x, k):
        return lax.ppermute(x, "head", [(i, i ^ k) for i in range(n_head)])

    tile = (8, LANES)
    pieces = {k: over_doc(prompt_cache, k) for k in (4, 6, 2, 1, 3)}
    pieces[0] = prompt_cache
    pieces[4], pieces[6], rel_table = lax.optimization_barrier((pieces[4], pieces[6], rel_table))
    pieces[5], pieces[7] = over_doc(pieces[4], 1), over_doc(pieces[6], 1)
    pieces = [pieces[k] for k in range(n_doc)]
    weight = jnp.transpose(w_qkv, (1, 0, 2))
    qkv, base, rel_q_heads = prepare(tokens, weight, rel_table)

    out_one = over_head(w_out, 2)
    out_pieces = [w_out, over_head(w_out, 1), out_one, over_head(out_one, 1)]

    att = attend(group_ids, qkv, base, rel_q_heads, candidates.T, pieces)
    att_y = over_head(att, 2)
    att_pieces = [att, over_head(att, 1), att_y, over_head(att_y, 1)]

    common = (att_pieces, out_pieces, tokens, gain_one.reshape(1, -1), w_up, w_down)
    other = feed(
        feed_other_kernel,
        *common,
        [jax.ShapeDtypeStruct((half, depth), jnp.bfloat16)],
        "feed_other",
    )[0]
    from_core = over_head(other, 1)
    for_y, own = feed(
        feed_own_kernel,
        *common,
        [jax.ShapeDtypeStruct((quarter, depth), jnp.float32)] * 2,
        "feed_own",
    )
    folded = pl.pallas_call(
        fold_kernel,
        out_shape=jax.ShapeDtypeStruct((quarter, depth), jnp.bfloat16),
        in_specs=full_specs(2),
        out_specs=full_specs(1)[0],
        compiler_params=params(4),
        name="fold",
    )(for_y, from_core)
    from_y = over_head(folded, 2)

    emb = w_proj.shape[1]
    vectors, single = pl.pallas_call(
        project_kernel,
        out_shape=[
            jax.ShapeDtypeStruct((n_doc, quarter + EXTRA, emb), jnp.bfloat16),
            jax.ShapeDtypeStruct((quarter, emb), jnp.bfloat16),
        ],
        in_specs=full_specs(9),
        out_specs=full_specs(2),
        compiler_params=params(8),
        name="project",
    )(own, from_core, from_y, gain_two.reshape(1, -1), w_proj, *att_pieces)
    queries = lax.all_to_all(vectors, "doc", 0, 0, tiled=True).reshape(-1, emb)

    rated = pl.pallas_call(
        score_kernel,
        out_shape=jax.ShapeDtypeStruct((n_doc, n_head) + tile, jnp.float32),
        in_specs=[smem] + full_specs(1) + [pl.BlockSpec(memory_space=pltpu.HBM)],
        out_specs=full_specs(1)[0],
        scratch_shapes=[
            pltpu.VMEM(doc_vectors.shape, jnp.bfloat16),
            pltpu.VMEM(tile, jnp.int32),
            pltpu.SMEM(tile, jnp.int32),
            pltpu.SemaphoreType.DMA((8,)),
            pltpu.SemaphoreType.DMA,
        ],
        compiler_params=params(56),
        name="rate",
    )(doc_lengths, queries, doc_vectors)
    back = lax.all_to_all(rated.reshape(-1, LANES), ("doc", "head"), 0, 0, tiled=True)

    place = lax.axis_index("head")
    own_y, own_c = place // 2, place % 2
    y_rows = over_head(single, 2)
    pair = jnp.where(
        own_y == 0, jnp.concatenate([single, y_rows]), jnp.concatenate([y_rows, single])
    )
    core_pair = over_head(pair, 1)
    query_vectors = jnp.where(
        own_c == 0, jnp.concatenate([pair, core_pair]), jnp.concatenate([core_pair, pair])
    )

    scores = pl.pallas_call(
        collect_kernel,
        out_shape=jax.ShapeDtypeStruct((cols, cand_rows), jnp.float32),
        in_specs=full_specs(1),
        out_specs=full_specs(1)[0],
        compiler_params=params(4),
        name="collect",
    )(back.reshape((n_doc, n_head) + tile))
    return (query_vectors, scores.T)


def solution(mesh):
    placed = (
        P("doc", None),
        P(None, None, "head"),
        P("head", None),
        P(None, "head"),
        P("head", None),
        P(),
        P(),
        P(),
        P(None, "doc", "head"),
        P(),
        P("doc", None, None),
        P("doc"),
        P("doc"),
        P("doc", "head"),
    )
    fits = mesh.shape["head"] == 4 and mesh.shape["doc"] == 8
    return jax.shard_map(
        body if fits else body_any,
        mesh=mesh,
        in_specs=placed,
        out_specs=(P("doc", None), P("doc", "head")),
        check_vma=False,
    )
```

```python
import functools
import math

import jax
import jax.numpy as jnp
from jax import lax
from jax.experimental import pallas as pl
from jax.experimental.pallas import tpu as pltpu
from jax.sharding import PartitionSpec as P

HD = 64
RELS = 512
QLEN = 32
PLEN = 64
DOC_DEV = 64


def layer_norm(values, gain):
    centre = values - jnp.mean(values, axis=-1, keepdims=True)
    spread = jnp.mean(centre * centre, axis=-1, keepdims=True)
    return centre * lax.rsqrt(spread + 1e-07) * gain


def slot_order(holders):
    count = holders.shape[0]
    same = holders[:, None] == holders[None, :]
    earlier = jnp.arange(count)[:, None] > jnp.arange(count)[None, :]
    return jnp.sum(same & earlier, axis=1)


def rate_slots(slot_query, slot_doc, doc_vectors, doc_lengths):
    shape = slot_doc.shape
    flat_doc = slot_doc.reshape(-1)
    flat_query = slot_query.reshape((flat_doc.shape[0],) + slot_query.shape[-2:])
    safe_doc = jnp.maximum(flat_doc, 0)
    documents = doc_vectors[safe_doc]
    lengths = doc_lengths[safe_doc]
    sims = jnp.einsum("sqe,sje->sqj", flat_query, documents, preferred_element_type=jnp.float32)
    live = jnp.arange(documents.shape[1], dtype=jnp.int32)[None, None, :] < lengths[:, None, None]
    best = jnp.max(jnp.where(live, sims, -jnp.inf), axis=2)
    totals = jnp.where(flat_doc >= 0, jnp.sum(best, axis=1), 0.0)
    return totals.reshape(shape)


def body_any(
    tokens,
    w_qkv,
    w_out,
    w_up,
    w_down,
    gain_one,
    gain_two,
    rel_table,
    prompt_cache,
    w_proj,
    doc_vectors,
    doc_lengths,
    group_ids,
    candidates,
):
    rows_dev = tokens.shape[0]
    req_dev = rows_dev // QLEN
    width = w_qkv.shape[2]
    heads_loc = width // HD
    half = RELS // 2
    scale_root = math.sqrt(3 * HD)
    gathered = lax.all_gather(prompt_cache, "doc", axis=1, tiled=True)
    weights_split = w_qkv.reshape(w_qkv.shape[0], 3, heads_loc, HD)
    projected_all = jnp.einsum(
        "td,dchf->chtf", tokens, weights_split, preferred_element_type=jnp.float32
    ).astype(jnp.bfloat16)
    rel_both = jnp.einsum(
        "rd,dchf->chrf", rel_table, weights_split[:, :2], preferred_element_type=jnp.float32
    ).astype(jnp.bfloat16)
    head_shape = (heads_loc, req_dev, QLEN, HD)
    query_four = projected_all[0].reshape(head_shape)
    keys_four = projected_all[1].reshape(head_shape)
    values_four = projected_all[2].reshape(head_shape)
    groups_all = gathered.shape[1] // PLEN
    cache_all = gathered.reshape(2, groups_all, PLEN, heads_loc, HD)
    picked = jnp.transpose(cache_all[:, group_ids], (0, 3, 1, 2, 4))
    keys = jnp.concatenate([keys_four, picked[0]], axis=2)
    values = jnp.concatenate([values_four, picked[1]], axis=2)
    pos_query = PLEN + jnp.arange(QLEN, dtype=jnp.int32)
    pos_key = jnp.concatenate([pos_query, jnp.arange(PLEN, dtype=jnp.int32)])
    index_one = pos_query[:, None] - pos_key[None, :] + half
    index_two = pos_key[:, None] - pos_query[None, :] + half
    rel_k_rows = rel_both[1][:, index_one]
    rel_q_rows = rel_both[0][:, index_two]
    c2p = jnp.einsum("hrqd,hqkd->hrqk", query_four, rel_k_rows, preferred_element_type=jnp.float32)
    p2c = jnp.einsum("hrkd,hkqd->hrqk", keys, rel_q_rows, preferred_element_type=jnp.float32)
    content = jnp.einsum("hrqd,hrkd->hrqk", query_four, keys, preferred_element_type=jnp.float32)
    logits = (content + c2p + p2c) / scale_root
    largest = jnp.max(logits, axis=-1, keepdims=True)
    weights = jnp.exp(logits - largest)
    denominator = jnp.sum(weights, axis=-1)
    summed = jnp.einsum(
        "hrqk,hrkd->hrqd", weights.astype(jnp.bfloat16), values, preferred_element_type=jnp.float32
    )
    attended = (summed / denominator[..., None]).astype(jnp.bfloat16)
    out_split = w_out.reshape(heads_loc, HD, w_out.shape[1])
    attn_part = jnp.einsum(
        "hrqd,hde->rqe", attended, out_split, preferred_element_type=jnp.float32
    ).reshape(rows_dev, w_out.shape[1])
    attn_total = lax.psum(attn_part.astype(jnp.bfloat16), "head").astype(jnp.float32)
    hidden_one = layer_norm(tokens.astype(jnp.float32) + attn_total, gain_one).astype(jnp.bfloat16)
    inner = jax.nn.gelu(
        jnp.dot(hidden_one, w_up, preferred_element_type=jnp.float32), approximate=False
    ).astype(jnp.bfloat16)
    ffn_total = lax.psum(
        jnp.dot(inner, w_down, preferred_element_type=jnp.float32).astype(jnp.bfloat16), "head"
    ).astype(jnp.float32)
    hidden_two = layer_norm(hidden_one.astype(jnp.float32) + ffn_total, gain_two).astype(
        jnp.bfloat16
    )
    projected = jnp.dot(hidden_two, w_proj, preferred_element_type=jnp.float32)
    query_vectors = (
        projected * lax.rsqrt(jnp.sum(projected * projected, axis=-1, keepdims=True) + 1e-06)
    ).astype(jnp.bfloat16)
    shards = lax.axis_size("doc")
    cand_dev = candidates.shape[1]
    pairs = req_dev * cand_dev
    capacity = max(2, 2 * pairs // shards)
    flat_cand = candidates.reshape(-1)
    holders = flat_cand // DOC_DEV
    request_of = jnp.arange(pairs, dtype=jnp.int32) // cand_dev
    slot_rank = slot_order(holders)
    copies, cand_copies = (
        lax.all_gather(query_vectors, "doc", axis=0, tiled=True),
        lax.all_gather(candidates, "doc", axis=0, tiled=True),
    )
    all_query = copies.reshape(shards, req_dev, QLEN, copies.shape[1])
    all_cand = cand_copies.reshape(shards, pairs)
    holder_all = all_cand // DOC_DEV
    local_all = all_cand % DOC_DEV
    rank_all = jax.vmap(slot_order)(holder_all)
    own_index = lax.axis_index("doc")
    chosen = (holder_all[:, None, :] == own_index) & (
        rank_all[:, None, :] == jnp.arange(capacity, dtype=jnp.int32)[None, :, None]
    )
    filled = jnp.any(chosen, axis=2)
    slot_request = jnp.sum(jnp.where(chosen, request_of[None, None, :], 0), axis=2)
    slot_doc = jnp.where(
        filled, jnp.sum(jnp.where(chosen, local_all[:, None, :], 0), axis=2), -1
    ).astype(jnp.int32)
    slot_query = all_query[jnp.arange(shards)[:, None], slot_request]
    slot_scores = rate_slots(slot_query, slot_doc, doc_vectors, doc_lengths)
    returned = lax.all_to_all(slot_scores, "doc", split_axis=0, concat_axis=0, tiled=True)
    scores = returned.reshape(-1)[holders * capacity + slot_rank].reshape(candidates.shape)
    return (query_vectors, scores)


LANES = 128
MIB = 1 << 20
EXTRA = 16
PREP_UNROLL = 6
ATT_UNROLL = 6
SCORE_UNROLL = 32


def full_specs(count):
    return [pl.BlockSpec(memory_space=pltpu.VMEM)] * count


def params(mib):
    return pltpu.CompilerParams(vmem_limit_bytes=mib * MIB)


def by_head(values):
    head_of = lax.broadcasted_iota(jnp.int32, values.shape, 1) // HD
    heads = values.shape[1] // HD
    zero = jnp.zeros_like(values)
    return jnp.concatenate([jnp.where(head_of == h, values, zero) for h in range(heads)], axis=0)


def times_rows(left, right):
    return lax.dot_general(left, right, (((1,), (1,)), ((), ())), preferred_element_type=jnp.float32)


def key_terms(key_rel, first):
    slot = lax.broadcasted_iota(jnp.int32, (key_rel.shape[0], LANES), 1) // QLEN
    turned = None
    for h in range(key_rel.shape[1] // LANES):
        shift = (LANES - PLEN - QLEN + first + h * QLEN) % LANES
        rolled = pltpu.roll(
            key_rel[:, h * LANES : (h + 1) * LANES], shift, 1, stride=1, stride_axis=0
        )
        turned = rolled if turned is None else jnp.where(slot == h, rolled, turned)
    return turned


def prepare_kernel(tokens, weight, rel_table, qkv, base, rel_q_heads, q_heads, query_rel, key_rel):
    width = weight.shape[2]
    heads = width // HD
    for i in range(3):
        qkv[:, i * width : (i + 1) * width] = jnp.dot(
            tokens[...], weight[i], preferred_element_type=jnp.float32
        ).astype(jnp.bfloat16)
    count = 2 * (PLEN + QLEN)
    low = RELS // 2 - PLEN - QLEN
    rel = [
        jnp.dot(
            rel_table[low : low + count, :], weight[i], preferred_element_type=jnp.float32
        ).astype(jnp.bfloat16)
        for i in range(2)
    ]
    both = lax.broadcasted_iota(jnp.int32, (LANES, count), 0) + lax.broadcasted_iota(
        jnp.int32, (LANES, count), 1
    )
    flip_q = jnp.where(both == LANES, 1.0, 0.0).astype(jnp.bfloat16)
    flip_k = jnp.where(both == LANES + PLEN - 1, 1.0, 0.0).astype(jnp.bfloat16)
    rel_q = jnp.dot(flip_q, rel[0], preferred_element_type=jnp.float32)
    rel_k = jnp.dot(flip_k, rel[1], preferred_element_type=jnp.float32)
    rel_q_heads[...] = by_head(rel_q.astype(jnp.bfloat16))
    requests, many, _ = base.shape
    for r in range(requests):
        q_heads[r * many : (r + 1) * many, :] = by_head(qkv[r * QLEN : (r + 1) * QLEN, :width])
    query_rel[...] = times_rows(q_heads[...], rel_k.astype(jnp.bfloat16))
    key_rel[...] = times_rows(qkv[:, width : 2 * width], rel_q_heads[...])
    live = lax.broadcasted_iota(jnp.int32, (many, LANES), 1) < PLEN + QLEN
    above = jnp.zeros((PLEN, LANES), jnp.float32)
    below = jnp.zeros((LANES - PLEN - QLEN, LANES), jnp.float32)
    scale = 1.0 / math.sqrt(3 * HD)

    def one_request(r, carry):
        rows = pl.ds(pl.multiple_of(r * QLEN, QLEN), QLEN)
        spread = pl.ds(pl.multiple_of(r * many, many), many)
        turned = times_rows(qkv[rows, width : 2 * width], q_heads[spread, :])
        turned = turned + key_terms(key_rel[rows, :], PLEN)
        own = jnp.concatenate([above, turned, below], axis=0).T[:many]
        spread_rel = query_rel[spread, :]
        c2p = jnp.concatenate(
            [
                pltpu.roll(
                    spread_rel[h * QLEN : (h + 1) * QLEN],
                    LANES - QLEN + 1,
                    1,
                    stride=1,
                    stride_axis=0,
                )
                for h in range(heads)
            ],
            axis=0,
        )
        base[r] = jnp.where(live, (own + c2p) * scale, -jnp.inf)
        return carry

    lax.fori_loop(0, requests, one_request, 0, unroll=PREP_UNROLL)


def prepare(tokens, weight, rel_table):
    rows = tokens.shape[0]
    width = weight.shape[2]
    heads = width // HD
    return pl.pallas_call(
        prepare_kernel,
        out_shape=[
            jax.ShapeDtypeStruct((rows, 3 * width), jnp.bfloat16),
            jax.ShapeDtypeStruct((rows // QLEN, heads * QLEN, LANES), jnp.float32),
            jax.ShapeDtypeStruct((heads * LANES, width), jnp.bfloat16),
        ],
        in_specs=full_specs(3),
        out_specs=full_specs(3),
        scratch_shapes=[
            pltpu.VMEM((rows * heads, width), jnp.bfloat16),
            pltpu.VMEM((rows * heads, LANES), jnp.float32),
            pltpu.VMEM((rows, heads * LANES), jnp.float32),
        ],
        compiler_params=params(12),
        cost_estimate=pl.CostEstimate(flops=4000 * MIB, bytes_accessed=4 * MIB, transcendentals=0),
        name="prepare",
    )(tokens, weight, rel_table)


def attend_kernel(group_ids, qkv, base, rel_q_heads, columns, *rest):
    pieces, (att, cache, picked, key_rel, arrived) = rest[:-5], rest[-5:]
    copies = [
        [
            pltpu.make_async_copy(piece.at[kind], cache.at[kind, at], arrived.at[kind, at])
            for at, piece in enumerate(pieces)
        ]
        for kind in range(2)
    ]
    for copy in copies[0] + copies[1]:
        copy.start()
    requests, _, _ = base.shape
    tokens = requests * QLEN
    ids = columns[...].T
    spare = jnp.zeros((1, LANES - columns.shape[0] * columns.shape[1]), jnp.int32)
    line = jnp.concatenate([ids[r : r + 1, :] for r in range(ids.shape[0])] + [spare], axis=1)
    line = jnp.concatenate([line // DOC_DEV, line % DOC_DEV], axis=1)
    extra = jnp.broadcast_to(line.astype(jnp.float32), (EXTRA, line.shape[1]))
    att[tokens:, :] = extra.astype(att.dtype)
    width = att.shape[1]
    heads = width // HD
    groups_dev = cache.shape[2] // PLEN
    me = lax.axis_index("doc")
    padding = jnp.zeros((LANES - PLEN - QLEN, width), jnp.bfloat16)
    below_terms = jnp.zeros((LANES - PLEN, LANES), jnp.float32)
    small_head = lax.broadcasted_iota(jnp.int32, (QLEN, width), 1) // HD
    scale = 1.0 / math.sqrt(3 * HD)

    def place_of(r):
        owner = group_ids[r] // groups_dev
        within = pl.multiple_of((group_ids[r] - owner * groups_dev) * PLEN, PLEN)
        return owner ^ me, pl.ds(within, PLEN)

    for copy in copies[0]:
        copy.wait()
    for r in range(requests):
        piece, within = place_of(r)
        picked[r * PLEN : (r + 1) * PLEN, :] = cache[0, piece, within, :]
    key_rel[...] = times_rows(picked[...], rel_q_heads[...])
    for copy in copies[1]:
        copy.wait()

    def one_request(r, carry):
        rows = pl.ds(pl.multiple_of(r * QLEN, QLEN), QLEN)
        cached = pl.ds(pl.multiple_of(r * PLEN, PLEN), PLEN)
        turned = times_rows(picked[cached, :], by_head(qkv[rows, 0:width]))
        turned = (turned + key_terms(key_rel[cached, :], 0)) * scale
        logits = base[r] + jnp.concatenate([turned, below_terms], axis=0).T[: heads * QLEN]
        largest = jnp.max(logits, axis=1, keepdims=True)
        weights = jnp.exp(logits - largest)
        weights = weights * (1.0 / jnp.sum(weights, axis=1, keepdims=True))
        piece, within = place_of(r)
        values = jnp.concatenate(
            [cache[1, piece, within, :], qkv[rows, 2 * width : 3 * width], padding], axis=0
        )
        summed = jnp.dot(weights.astype(jnp.bfloat16), values, preferred_element_type=jnp.float32)
        out = summed[:QLEN]
        for h in range(1, heads):
            out = jnp.where(small_head == h, summed[h * QLEN : (h + 1) * QLEN], out)
        att[rows, :] = out.astype(jnp.bfloat16)
        return carry

    lax.fori_loop(0, requests, one_request, 0, unroll=ATT_UNROLL)


def attend(group_ids, qkv, base, rel_q_heads, columns, pieces):
    rows = qkv.shape[0]
    width = qkv.shape[1] // 3
    cached = rows // QLEN * PLEN
    return pl.pallas_call(
        attend_kernel,
        out_shape=jax.ShapeDtypeStruct((rows + EXTRA, width), jnp.bfloat16),
        in_specs=[pl.BlockSpec(memory_space=pltpu.SMEM)]
        + full_specs(4)
        + [pl.BlockSpec(memory_space=pl.ANY)] * len(pieces),
        out_specs=pl.BlockSpec(memory_space=pltpu.VMEM),
        scratch_shapes=[
            pltpu.VMEM((2, len(pieces)) + pieces[0].shape[1:], jnp.bfloat16),
            pltpu.VMEM((cached, width), jnp.bfloat16),
            pltpu.VMEM((cached, rel_q_heads.shape[0]), jnp.float32),
            pltpu.SemaphoreType.DMA((2, len(pieces))),
        ],
        compiler_params=params(12),
        cost_estimate=pl.CostEstimate(flops=2000 * MIB, bytes_accessed=2 * MIB, transcendentals=0),
        name="attend",
    )(group_ids, qkv, base, rel_q_heads, columns, *pieces)


def norm_rows(values, gain):
    centre = values - jnp.mean(values, axis=-1, keepdims=True)
    spread = jnp.mean(centre * centre, axis=-1, keepdims=True)
    return centre * lax.rsqrt(spread + 1e-07) * gain


def feed_rows(start, count, a, w, tokens, gain, w_up, w_down):
    rows = pl.ds(pl.multiple_of(start, 32), count)
    mixed = tokens[rows, :].astype(jnp.float32)
    for piece, weight in zip(a, w):
        mixed = mixed + jnp.dot(piece[rows, :], weight[...], preferred_element_type=jnp.float32)
    hidden = norm_rows(mixed, gain[...]).astype(jnp.bfloat16)
    total = None
    step = 256
    for at in range(0, w_up.shape[1], step):
        up = jnp.dot(hidden, w_up[:, at : at + step], preferred_element_type=jnp.float32)
        inner = (0.5 * up * (1.0 + lax.erf(up * math.sqrt(0.5)))).astype(jnp.bfloat16)
        part = jnp.dot(inner, w_down[at : at + step, :], preferred_element_type=jnp.float32)
        total = part if total is None else total + part
    return hidden, total


def feed_other_kernel(a0, a1, a2, a3, w0, w1, w2, w3, tokens, gain, w_up, w_down, out):
    core = lax.axis_index("head") % 2
    _, total = feed_rows(
        (1 - core) * out.shape[0], out.shape[0], (a0, a1, a2, a3), (w0, w1, w2, w3), tokens, gain, w_up, w_down
    )
    out[...] = total.astype(out.dtype)


def feed_own_kernel(a0, a1, a2, a3, w0, w1, w2, w3, tokens, gain, w_up, w_down, out, own):
    pieces, weights = (a0, a1, a2, a3), (w0, w1, w2, w3)
    count = out.shape[0]
    place = lax.axis_index("head")
    start = place % 2 * (2 * count)
    hidden, total = feed_rows(start, 2 * count, pieces, weights, tokens, gain, w_up, w_down)

    @pl.when(place // 2 == 0)
    def first():
        out[...] = total[count:]
        own[...] = hidden[:count].astype(jnp.float32) + total[:count]

    @pl.when(place // 2 != 0)
    def second():
        out[...] = total[:count]
        own[...] = hidden[count:].astype(jnp.float32) + total[count:]


def feed(kernel, pieces, weights, tokens, gain, w_up, w_down, outs, name):
    return pl.pallas_call(
        kernel,
        out_shape=outs,
        in_specs=full_specs(12),
        out_specs=full_specs(len(outs)),
        compiler_params=params(20),
        cost_estimate=pl.CostEstimate(flops=1600 * MIB, bytes_accessed=6 * MIB, transcendentals=0),
        name=name,
    )(*pieces, *weights, tokens, gain, w_up, w_down)


def fold_kernel(for_y, from_core, out):
    count = out.shape[0]
    other = 1 - lax.axis_index("head") // 2
    rows = pl.ds(pl.multiple_of(other * count, 32), count)
    out[...] = (for_y[...] + from_core[rows, :].astype(jnp.float32)).astype(out.dtype)


def block_of(head):
    return head % 2 * 2 + head // 2


def project_kernel(own, from_core, from_y, gain, w_proj, a0, a1, a2, a3, out, single):
    count = own.shape[0]
    place = lax.axis_index("head")
    rows = pl.ds(pl.multiple_of(place // 2 * count, 32), count)
    after = own[...] + from_core[rows, :].astype(jnp.float32) + from_y[...].astype(jnp.float32)
    hidden = norm_rows(after, gain[...]).astype(jnp.bfloat16)
    projected = jnp.dot(hidden, w_proj[...], preferred_element_type=jnp.float32)
    length = jnp.sum(projected * projected, axis=-1, keepdims=True)
    vectors = (projected * lax.rsqrt(length + 1e-06)).astype(jnp.bfloat16)
    single[...] = vectors
    pieces = (a0, a1, a2, a3)
    part = LANES // len(pieces) * 3 // 4
    lane = lax.broadcasted_iota(jnp.int32, (EXTRA, LANES), 1)
    lines = []
    for kind in range(2):
        line = jnp.zeros((EXTRA, LANES), jnp.float32)
        for x, piece in enumerate(pieces):
            from_head = place ^ x
            values = piece[piece.shape[0] - EXTRA :, kind * LANES : (kind + 1) * LANES]
            shift = lax.rem((from_head - block_of(place)) * part + LANES, LANES)
            rolled = pltpu.roll(values.astype(jnp.float32), shift, 1)
            line = jnp.where(lane // part == from_head, rolled, line)
        lines.append(line)
    which = lax.broadcasted_iota(jnp.int32, (EXTRA, LANES), 0)
    tail = jnp.where(which == 0, lines[0], lines[1]).astype(out.dtype)
    for o in range(out.shape[0]):
        out[o, :count] = vectors
        out[o, count:] = tail


def list_slots(queries, n_doc, listed):
    rows = queries.shape[0] // n_doc
    part = (rows - EXTRA) // QLEN * 8
    me = lax.axis_index("doc")
    shape = (n_doc, LANES)
    lane = lax.broadcasted_iota(jnp.int32, shape, 1)
    row = lax.broadcasted_iota(jnp.int32, shape, 0)
    tails = [
        queries[o * rows + rows - EXTRA : (o + 1) * rows, :].astype(jnp.float32) for o in range(n_doc)
    ]
    holder = jnp.concatenate([tail[:1] for tail in tails], axis=0).astype(jnp.int32)
    doc = jnp.concatenate([tail[1:2] for tail in tails], axis=0).astype(jnp.int32)
    mine = (lane < 4 * part) & (holder == me)
    group = (row * rows + lane % part // 8 * QLEN) // 16
    listed[n_doc : 2 * n_doc, :] = group | (doc << 8)
    ones = jnp.where(mine, 1.0, 0.0)
    until = lax.broadcasted_iota(jnp.int32, (LANES, LANES), 0) <= lax.broadcasted_iota(
        jnp.int32, (LANES, LANES), 1
    )
    until = jnp.where(until, 1.0, 0.0).astype(jnp.bfloat16)
    reached = jnp.dot(ones.astype(jnp.bfloat16), until, preferred_element_type=jnp.float32)
    in_row = jnp.sum(ones, axis=1, keepdims=True)
    above = jnp.zeros((1, 1), jnp.float32)
    starts = []
    for o in range(n_doc):
        starts.append(above)
        above = above + in_row[o : o + 1]
    reached = (reached + jnp.concatenate(starts, axis=0)).astype(jnp.int32)
    pad = jnp.zeros((LANES - n_doc, LANES), jnp.int32)
    columns = jnp.concatenate([reached, pad], axis=0).T
    square_lane = lax.broadcasted_iota(jnp.int32, (LANES, LANES), 1)
    blocks = (jnp.sum(ones).astype(jnp.int32) + LANES - 1) // LANES

    def one_block(block, carry):
        total = jnp.zeros((LANES, LANES), jnp.int32)
        for o in range(n_doc):
            passed = columns[:, o : o + 1] <= square_lane + block * LANES
            total = total + jnp.where(passed, 1, 0)
        listed[pl.ds(block, 1), :] = jnp.sum(total, axis=0, keepdims=True)
        return carry

    lax.fori_loop(0, blocks, one_block, 0)
    listed[n_doc - 1 : n_doc, :] = jnp.broadcast_to(above.astype(jnp.int32), (1, LANES))


def score_kernel(lengths, queries, docs, out, held, listed, slots, arrived, ready):
    chunks = arrived.shape[0]
    per = docs.shape[0] // chunks
    copies = [
        pltpu.make_async_copy(
            docs.at[pl.ds(c * per, per)], held.at[pl.ds(c * per, per)], arrived.at[c]
        )
        for c in range(chunks)
    ]
    for copy in copies:
        copy.start()
    list_slots(queries, out.shape[0], listed)
    to_scalars = pltpu.make_async_copy(listed, slots, ready)
    to_scalars.start()
    to_scalars.wait()
    for copy in copies:
        copy.wait()

    shape = (8, LANES)
    flat = lax.broadcasted_iota(jnp.int32, shape, 0) * LANES + lax.broadcasted_iota(jnp.int32, shape, 1)
    unroll = SCORE_UNROLL
    zero = jnp.zeros((QLEN, docs.shape[2]), jnp.bfloat16)
    position = lax.broadcasted_iota(jnp.int32, (docs.shape[1], 2 * QLEN), 0)
    side = lax.broadcasted_iota(jnp.int32, (1, 2 * QLEN), 1) < QLEN
    tables = out.shape[0]
    count = slots[tables - 1, 0]

    def some(i, totals):
        for u in range(0, unroll, 2):
            left, right, marks, limits = [], [], [], []
            for v in range(2):
                s = i * unroll + u + v
                used = s < count
                entry = jnp.where(used, slots[s >> 7, s & 127], 0)
                found = slots[tables + (entry >> 7), entry & 127]
                query = queries[pl.ds(pl.multiple_of((found & 255) * 16, 16), QLEN), :]
                doc = found >> 8
                left.append(jnp.concatenate([query, zero] if v == 0 else [zero, query], axis=1))
                right.append(held[doc])
                marks.append(jnp.where(used, entry, -1))
                limits.append(lengths[doc])
            sims = times_rows(jnp.concatenate(right, axis=1), jnp.concatenate(left, axis=0))
            limit = jnp.where(side, limits[0], limits[1])
            best = jnp.max(jnp.where(position < limit, sims, -jnp.inf), axis=0, keepdims=True)
            for v in range(2):
                total = jnp.sum(jnp.where(side if v == 0 else ~side, best, 0.0), axis=1, keepdims=True)
                totals = jnp.where(flat == marks[v], total, totals)
        return totals

    totals = lax.fori_loop(
        0, (count + unroll - 1) // unroll, some, jnp.zeros(shape, jnp.float32)
    )
    for o in range(out.shape[0]):
        row = jnp.broadcast_to(totals[o : o + 1], shape)
        for h in range(out.shape[1]):
            out[o, h] = row


def arrange_kernel(*refs):
    shares, out = refs[:-1], refs[-1]
    place = lax.axis_index("head")
    for k, share in enumerate(shares):
        count = share.shape[0]
        out[pl.ds(pl.multiple_of(block_of(place ^ k) * count, 32), count), :] = share[...]


def collect_kernel(tiles, out):
    n_head = tiles.shape[1]
    cols, reqs_all = out.shape
    reqs = reqs_all // n_head
    place = lax.axis_index("head")
    lines = []
    for h in range(n_head):
        total = tiles[0, h]
        for o in range(1, tiles.shape[0]):
            total = total + tiles[o, h]
        total = pltpu.roll(total, LANES - place * (reqs * cols), 1)
        lines.append(total[:1, : reqs * cols])
    order = sorted(range(n_head), key=block_of)
    rows = [lines[h][:, r * cols : (r + 1) * cols] for h in order for r in range(reqs)]
    out[...] = jnp.concatenate(rows, axis=0).T


def body(
    tokens,
    w_qkv,
    w_out,
    w_up,
    w_down,
    gain_one,
    gain_two,
    rel_table,
    prompt_cache,
    w_proj,
    doc_vectors,
    doc_lengths,
    group_ids,
    candidates,
):
    rows, depth = tokens.shape
    n_doc = lax.axis_size("doc")
    n_head = lax.axis_size("head")
    half, quarter = rows // 2, rows // n_head
    cand_rows, cols = candidates.shape
    reqs = cand_rows // n_head
    smem = pl.BlockSpec(memory_space=pltpu.SMEM)

    def over_doc(x, k):
        return lax.ppermute(x, "doc", [(i, i ^ k) for i in range(n_doc)])

    def over_head(x, k):
        return lax.ppermute(x, "head", [(i, i ^ k) for i in range(n_head)])

    tile = (8, LANES)
    pieces = {k: over_doc(prompt_cache, k) for k in (4, 1, 2, 3)}
    pieces[1], again = lax.optimization_barrier((pieces[1], prompt_cache))
    pieces[6] = over_doc(again, 6)
    pieces[0] = prompt_cache
    pieces[4], pieces[6], rel_table = lax.optimization_barrier((pieces[4], pieces[6], rel_table))
    pieces[5], pieces[7] = over_doc(pieces[4], 1), over_doc(pieces[6], 1)
    pieces = [pieces[k] for k in range(n_doc)]
    weight = jnp.transpose(w_qkv, (1, 0, 2))
    qkv, base, rel_q_heads = prepare(tokens, weight, rel_table)

    out_one = over_head(w_out, 2)
    out_pieces = [w_out, over_head(w_out, 1), out_one, over_head(out_one, 1)]

    att = attend(group_ids, qkv, base, rel_q_heads, candidates.T, pieces)
    att_y = over_head(att, 2)
    att_pieces = [att, over_head(att, 1), att_y, over_head(att_y, 1)]

    common = (att_pieces, out_pieces, tokens, gain_one.reshape(1, -1), w_up, w_down)
    other = feed(
        feed_other_kernel,
        *common,
        [jax.ShapeDtypeStruct((half, depth), jnp.bfloat16)],
        "feed_other",
    )[0]
    from_core = over_head(other, 1)
    for_y, own = feed(
        feed_own_kernel,
        *common,
        [jax.ShapeDtypeStruct((quarter, depth), jnp.float32)] * 2,
        "feed_own",
    )
    folded = pl.pallas_call(
        fold_kernel,
        out_shape=jax.ShapeDtypeStruct((quarter, depth), jnp.bfloat16),
        in_specs=full_specs(2),
        out_specs=full_specs(1)[0],
        compiler_params=params(4),
        name="fold",
    )(for_y, from_core)
    from_y = over_head(folded, 2)

    emb = w_proj.shape[1]
    vectors, single = pl.pallas_call(
        project_kernel,
        out_shape=[
            jax.ShapeDtypeStruct((n_doc, quarter + EXTRA, emb), jnp.bfloat16),
            jax.ShapeDtypeStruct((quarter, emb), jnp.bfloat16),
        ],
        in_specs=full_specs(9),
        out_specs=full_specs(2),
        compiler_params=params(8),
        name="project",
    )(own, from_core, from_y, gain_two.reshape(1, -1), w_proj, *att_pieces)
    queries = lax.all_to_all(vectors, "doc", 0, 0, tiled=True).reshape(-1, emb)

    rated = pl.pallas_call(
        score_kernel,
        out_shape=jax.ShapeDtypeStruct((n_doc, n_head) + tile, jnp.float32),
        in_specs=[smem] + full_specs(1) + [pl.BlockSpec(memory_space=pltpu.HBM)],
        out_specs=full_specs(1)[0],
        scratch_shapes=[
            pltpu.VMEM(doc_vectors.shape, jnp.bfloat16),
            pltpu.VMEM((2 * n_doc, LANES), jnp.int32),
            pltpu.SMEM((2 * n_doc, LANES), jnp.int32),
            pltpu.SemaphoreType.DMA((8,)),
            pltpu.SemaphoreType.DMA,
        ],
        compiler_params=params(56),
        name="rate",
    )(doc_lengths, queries, doc_vectors)
    back = lax.all_to_all(rated.reshape(-1, LANES), ("doc", "head"), 0, 0, tiled=True)

    single, _ = lax.optimization_barrier((single, rated))
    shares = [single] + [over_head(single, k) for k in range(1, n_head)]
    query_vectors = pl.pallas_call(
        arrange_kernel,
        out_shape=jax.ShapeDtypeStruct((rows, emb), jnp.bfloat16),
        in_specs=full_specs(n_head),
        out_specs=full_specs(1)[0],
        compiler_params=params(4),
        name="arrange",
    )(*shares)

    scores = pl.pallas_call(
        collect_kernel,
        out_shape=jax.ShapeDtypeStruct((cols, cand_rows), jnp.float32),
        in_specs=full_specs(1),
        out_specs=full_specs(1)[0],
        compiler_params=params(4),
        name="collect",
    )(back.reshape((n_doc, n_head) + tile))
    return (query_vectors, scores.T)


def solution(mesh):
    placed = (
        P("doc", None),
        P(None, None, "head"),
        P("head", None),
        P(None, "head"),
        P("head", None),
        P(),
        P(),
        P(),
        P(None, "doc", "head"),
        P(),
        P("doc", None, None),
        P("doc"),
        P("doc"),
        P("doc", "head"),
    )
    fits = mesh.shape["head"] == 4 and mesh.shape["doc"] == 8
    return jax.shard_map(
        body if fits else body_any,
        mesh=mesh,
        in_specs=placed,
        out_specs=(P("doc", None), P("doc", "head")),
        check_vma=False,
    )
```

```python
import functools
import math

import jax
import jax.numpy as jnp
from jax import lax
from jax.experimental import pallas as pl
from jax.experimental.pallas import tpu as pltpu
from jax.sharding import PartitionSpec as P

HD = 64
RELS = 512
QLEN = 32
PLEN = 64
DOC_DEV = 64


def layer_norm(values, gain):
    centre = values - jnp.mean(values, axis=-1, keepdims=True)
    spread = jnp.mean(centre * centre, axis=-1, keepdims=True)
    return centre * lax.rsqrt(spread + 1e-07) * gain


def slot_order(holders):
    count = holders.shape[0]
    same = holders[:, None] == holders[None, :]
    earlier = jnp.arange(count)[:, None] > jnp.arange(count)[None, :]
    return jnp.sum(same & earlier, axis=1)


def rate_slots(slot_query, slot_doc, doc_vectors, doc_lengths):
    shape = slot_doc.shape
    flat_doc = slot_doc.reshape(-1)
    flat_query = slot_query.reshape((flat_doc.shape[0],) + slot_query.shape[-2:])
    safe_doc = jnp.maximum(flat_doc, 0)
    documents = doc_vectors[safe_doc]
    lengths = doc_lengths[safe_doc]
    sims = jnp.einsum("sqe,sje->sqj", flat_query, documents, preferred_element_type=jnp.float32)
    live = jnp.arange(documents.shape[1], dtype=jnp.int32)[None, None, :] < lengths[:, None, None]
    best = jnp.max(jnp.where(live, sims, -jnp.inf), axis=2)
    totals = jnp.where(flat_doc >= 0, jnp.sum(best, axis=1), 0.0)
    return totals.reshape(shape)


def body_any(
    tokens,
    w_qkv,
    w_out,
    w_up,
    w_down,
    gain_one,
    gain_two,
    rel_table,
    prompt_cache,
    w_proj,
    doc_vectors,
    doc_lengths,
    group_ids,
    candidates,
):
    rows_dev = tokens.shape[0]
    req_dev = rows_dev // QLEN
    width = w_qkv.shape[2]
    heads_loc = width // HD
    half = RELS // 2
    scale_root = math.sqrt(3 * HD)
    gathered = lax.all_gather(prompt_cache, "doc", axis=1, tiled=True)
    weights_split = w_qkv.reshape(w_qkv.shape[0], 3, heads_loc, HD)
    projected_all = jnp.einsum(
        "td,dchf->chtf", tokens, weights_split, preferred_element_type=jnp.float32
    ).astype(jnp.bfloat16)
    rel_both = jnp.einsum(
        "rd,dchf->chrf", rel_table, weights_split[:, :2], preferred_element_type=jnp.float32
    ).astype(jnp.bfloat16)
    head_shape = (heads_loc, req_dev, QLEN, HD)
    query_four = projected_all[0].reshape(head_shape)
    keys_four = projected_all[1].reshape(head_shape)
    values_four = projected_all[2].reshape(head_shape)
    groups_all = gathered.shape[1] // PLEN
    cache_all = gathered.reshape(2, groups_all, PLEN, heads_loc, HD)
    picked = jnp.transpose(cache_all[:, group_ids], (0, 3, 1, 2, 4))
    keys = jnp.concatenate([keys_four, picked[0]], axis=2)
    values = jnp.concatenate([values_four, picked[1]], axis=2)
    pos_query = PLEN + jnp.arange(QLEN, dtype=jnp.int32)
    pos_key = jnp.concatenate([pos_query, jnp.arange(PLEN, dtype=jnp.int32)])
    index_one = pos_query[:, None] - pos_key[None, :] + half
    index_two = pos_key[:, None] - pos_query[None, :] + half
    rel_k_rows = rel_both[1][:, index_one]
    rel_q_rows = rel_both[0][:, index_two]
    c2p = jnp.einsum("hrqd,hqkd->hrqk", query_four, rel_k_rows, preferred_element_type=jnp.float32)
    p2c = jnp.einsum("hrkd,hkqd->hrqk", keys, rel_q_rows, preferred_element_type=jnp.float32)
    content = jnp.einsum("hrqd,hrkd->hrqk", query_four, keys, preferred_element_type=jnp.float32)
    logits = (content + c2p + p2c) / scale_root
    largest = jnp.max(logits, axis=-1, keepdims=True)
    weights = jnp.exp(logits - largest)
    denominator = jnp.sum(weights, axis=-1)
    summed = jnp.einsum(
        "hrqk,hrkd->hrqd", weights.astype(jnp.bfloat16), values, preferred_element_type=jnp.float32
    )
    attended = (summed / denominator[..., None]).astype(jnp.bfloat16)
    out_split = w_out.reshape(heads_loc, HD, w_out.shape[1])
    attn_part = jnp.einsum(
        "hrqd,hde->rqe", attended, out_split, preferred_element_type=jnp.float32
    ).reshape(rows_dev, w_out.shape[1])
    attn_total = lax.psum(attn_part.astype(jnp.bfloat16), "head").astype(jnp.float32)
    hidden_one = layer_norm(tokens.astype(jnp.float32) + attn_total, gain_one).astype(jnp.bfloat16)
    inner = jax.nn.gelu(
        jnp.dot(hidden_one, w_up, preferred_element_type=jnp.float32), approximate=False
    ).astype(jnp.bfloat16)
    ffn_total = lax.psum(
        jnp.dot(inner, w_down, preferred_element_type=jnp.float32).astype(jnp.bfloat16), "head"
    ).astype(jnp.float32)
    hidden_two = layer_norm(hidden_one.astype(jnp.float32) + ffn_total, gain_two).astype(
        jnp.bfloat16
    )
    projected = jnp.dot(hidden_two, w_proj, preferred_element_type=jnp.float32)
    query_vectors = (
        projected * lax.rsqrt(jnp.sum(projected * projected, axis=-1, keepdims=True) + 1e-06)
    ).astype(jnp.bfloat16)
    shards = lax.axis_size("doc")
    cand_dev = candidates.shape[1]
    pairs = req_dev * cand_dev
    capacity = max(2, 2 * pairs // shards)
    flat_cand = candidates.reshape(-1)
    holders = flat_cand // DOC_DEV
    request_of = jnp.arange(pairs, dtype=jnp.int32) // cand_dev
    slot_rank = slot_order(holders)
    copies, cand_copies = (
        lax.all_gather(query_vectors, "doc", axis=0, tiled=True),
        lax.all_gather(candidates, "doc", axis=0, tiled=True),
    )
    all_query = copies.reshape(shards, req_dev, QLEN, copies.shape[1])
    all_cand = cand_copies.reshape(shards, pairs)
    holder_all = all_cand // DOC_DEV
    local_all = all_cand % DOC_DEV
    rank_all = jax.vmap(slot_order)(holder_all)
    own_index = lax.axis_index("doc")
    chosen = (holder_all[:, None, :] == own_index) & (
        rank_all[:, None, :] == jnp.arange(capacity, dtype=jnp.int32)[None, :, None]
    )
    filled = jnp.any(chosen, axis=2)
    slot_request = jnp.sum(jnp.where(chosen, request_of[None, None, :], 0), axis=2)
    slot_doc = jnp.where(
        filled, jnp.sum(jnp.where(chosen, local_all[:, None, :], 0), axis=2), -1
    ).astype(jnp.int32)
    slot_query = all_query[jnp.arange(shards)[:, None], slot_request]
    slot_scores = rate_slots(slot_query, slot_doc, doc_vectors, doc_lengths)
    returned = lax.all_to_all(slot_scores, "doc", split_axis=0, concat_axis=0, tiled=True)
    scores = returned.reshape(-1)[holders * capacity + slot_rank].reshape(candidates.shape)
    return (query_vectors, scores)


LANES = 128
MIB = 1 << 20
EXTRA = 16
PREP_UNROLL = 6
ATT_UNROLL = 6
SCORE_UNROLL = 32


def full_specs(count):
    return [pl.BlockSpec(memory_space=pltpu.VMEM)] * count


def far(x):
    return pltpu.with_memory_space_constraint(x, pltpu.HBM)


def params(mib):
    return pltpu.CompilerParams(vmem_limit_bytes=mib * MIB)


def by_head(values):
    head_of = lax.broadcasted_iota(jnp.int32, values.shape, 1) // HD
    heads = values.shape[1] // HD
    zero = jnp.zeros_like(values)
    return jnp.concatenate([jnp.where(head_of == h, values, zero) for h in range(heads)], axis=0)


def times_rows(left, right):
    return lax.dot_general(left, right, (((1,), (1,)), ((), ())), preferred_element_type=jnp.float32)


def key_terms(key_rel, first):
    slot = lax.broadcasted_iota(jnp.int32, (key_rel.shape[0], LANES), 1) // QLEN
    turned = None
    for h in range(key_rel.shape[1] // LANES):
        shift = (LANES - PLEN - QLEN + first + h * QLEN) % LANES
        rolled = pltpu.roll(
            key_rel[:, h * LANES : (h + 1) * LANES], shift, 1, stride=1, stride_axis=0
        )
        turned = rolled if turned is None else jnp.where(slot == h, rolled, turned)
    return turned


def prepare_kernel(
    tokens_far, weight_far, rel_table, qkv, base, rel_q_heads, q_heads, query_rel, key_rel, *scratch
):
    tokens, weight, rel_rows, arrived = scratch
    rel_far = rel_table.at[pl.ds(RELS // 2 - PLEN - QLEN, rel_rows.shape[0])]
    copies = [pltpu.make_async_copy(tokens_far, tokens, arrived.at[0])]
    copies += [pltpu.make_async_copy(weight_far.at[i], weight.at[i], arrived.at[1 + i]) for i in range(3)]
    copies += [pltpu.make_async_copy(rel_far, rel_rows, arrived.at[4])]
    for copy in copies:
        copy.start()
    copies[0].wait()
    width = weight.shape[2]
    heads = width // HD
    for i in range(3):
        copies[1 + i].wait()
        qkv[:, i * width : (i + 1) * width] = jnp.dot(
            tokens[...], weight[i], preferred_element_type=jnp.float32
        ).astype(jnp.bfloat16)
    count = rel_rows.shape[0]
    copies[4].wait()
    rel = [
        jnp.dot(rel_rows[...], weight[i], preferred_element_type=jnp.float32).astype(jnp.bfloat16)
        for i in range(2)
    ]
    both = lax.broadcasted_iota(jnp.int32, (LANES, count), 0) + lax.broadcasted_iota(
        jnp.int32, (LANES, count), 1
    )
    flip_q = jnp.where(both == LANES, 1.0, 0.0).astype(jnp.bfloat16)
    flip_k = jnp.where(both == LANES + PLEN - 1, 1.0, 0.0).astype(jnp.bfloat16)
    rel_q = jnp.dot(flip_q, rel[0], preferred_element_type=jnp.float32)
    rel_k = jnp.dot(flip_k, rel[1], preferred_element_type=jnp.float32)
    rel_q_heads[...] = by_head(rel_q.astype(jnp.bfloat16))
    requests, many, _ = base.shape
    for r in range(requests):
        q_heads[r * many : (r + 1) * many, :] = by_head(qkv[r * QLEN : (r + 1) * QLEN, :width])
    query_rel[...] = times_rows(q_heads[...], rel_k.astype(jnp.bfloat16))
    key_rel[...] = times_rows(qkv[:, width : 2 * width], rel_q_heads[...])
    live = lax.broadcasted_iota(jnp.int32, (many, LANES), 1) < PLEN + QLEN
    above = jnp.zeros((PLEN, LANES), jnp.float32)
    below = jnp.zeros((LANES - PLEN - QLEN, LANES), jnp.float32)
    scale = 1.0 / math.sqrt(3 * HD)

    def one_request(r, carry):
        rows = pl.ds(pl.multiple_of(r * QLEN, QLEN), QLEN)
        spread = pl.ds(pl.multiple_of(r * many, many), many)
        turned = times_rows(qkv[rows, width : 2 * width], q_heads[spread, :])
        turned = turned + key_terms(key_rel[rows, :], PLEN)
        own = jnp.concatenate([above, turned, below], axis=0).T[:many]
        spread_rel = query_rel[spread, :]
        c2p = jnp.concatenate(
            [
                pltpu.roll(
                    spread_rel[h * QLEN : (h + 1) * QLEN],
                    LANES - QLEN + 1,
                    1,
                    stride=1,
                    stride_axis=0,
                )
                for h in range(heads)
            ],
            axis=0,
        )
        base[r] = jnp.where(live, (own + c2p) * scale, -jnp.inf)
        return carry

    lax.fori_loop(0, requests, one_request, 0, unroll=PREP_UNROLL)


def prepare(tokens, weight, rel_table):
    rows = tokens.shape[0]
    width = weight.shape[2]
    heads = width // HD
    return pl.pallas_call(
        prepare_kernel,
        out_shape=[
            jax.ShapeDtypeStruct((rows, 3 * width), jnp.bfloat16),
            jax.ShapeDtypeStruct((rows // QLEN, heads * QLEN, LANES), jnp.float32),
            jax.ShapeDtypeStruct((heads * LANES, width), jnp.bfloat16),
        ],
        in_specs=[pl.BlockSpec(memory_space=pltpu.HBM)] * 3,
        out_specs=full_specs(3),
        scratch_shapes=[
            pltpu.VMEM((rows * heads, width), jnp.bfloat16),
            pltpu.VMEM((rows * heads, LANES), jnp.float32),
            pltpu.VMEM((rows, heads * LANES), jnp.float32),
            pltpu.VMEM(tokens.shape, jnp.bfloat16),
            pltpu.VMEM(weight.shape, jnp.bfloat16),
            pltpu.VMEM((2 * (PLEN + QLEN), rel_table.shape[1]), jnp.bfloat16),
            pltpu.SemaphoreType.DMA((5,)),
        ],
        compiler_params=params(16),
        cost_estimate=pl.CostEstimate(flops=4000 * MIB, bytes_accessed=4 * MIB, transcendentals=0),
        name="prepare",
    )(far(tokens), far(weight), far(rel_table))


def attend_kernel(group_ids, qkv, base, rel_q_heads, columns, *rest):
    pieces, (att, cache, picked, key_rel, arrived) = rest[:-5], rest[-5:]
    copies = [
        [
            pltpu.make_async_copy(piece.at[kind], cache.at[kind, at], arrived.at[kind, at])
            for at, piece in enumerate(pieces)
        ]
        for kind in range(2)
    ]
    for copy in copies[0] + copies[1]:
        copy.start()
    requests, _, _ = base.shape
    tokens = requests * QLEN
    ids = columns[...].T
    spare = jnp.zeros((1, LANES - columns.shape[0] * columns.shape[1]), jnp.int32)
    line = jnp.concatenate([ids[r : r + 1, :] for r in range(ids.shape[0])] + [spare], axis=1)
    line = jnp.concatenate([line // DOC_DEV, line % DOC_DEV], axis=1)
    extra = jnp.broadcast_to(line.astype(jnp.float32), (EXTRA, line.shape[1]))
    att[tokens:, :] = extra.astype(att.dtype)
    width = att.shape[1]
    heads = width // HD
    groups_dev = cache.shape[2] // PLEN
    me = lax.axis_index("doc")
    padding = jnp.zeros((LANES - PLEN - QLEN, width), jnp.bfloat16)
    below_terms = jnp.zeros((LANES - PLEN, LANES), jnp.float32)
    small_head = lax.broadcasted_iota(jnp.int32, (QLEN, width), 1) // HD
    scale = 1.0 / math.sqrt(3 * HD)

    def place_of(r):
        owner = group_ids[r] // groups_dev
        within = pl.multiple_of((group_ids[r] - owner * groups_dev) * PLEN, PLEN)
        return owner ^ me, pl.ds(within, PLEN)

    for copy in copies[0]:
        copy.wait()
    for r in range(requests):
        piece, within = place_of(r)
        picked[r * PLEN : (r + 1) * PLEN, :] = cache[0, piece, within, :]
    key_rel[...] = times_rows(picked[...], rel_q_heads[...])
    for copy in copies[1]:
        copy.wait()

    def one_request(r, carry):
        rows = pl.ds(pl.multiple_of(r * QLEN, QLEN), QLEN)
        cached = pl.ds(pl.multiple_of(r * PLEN, PLEN), PLEN)
        turned = times_rows(picked[cached, :], by_head(qkv[rows, 0:width]))
        turned = (turned + key_terms(key_rel[cached, :], 0)) * scale
        logits = base[r] + jnp.concatenate([turned, below_terms], axis=0).T[: heads * QLEN]
        largest = jnp.max(logits, axis=1, keepdims=True)
        weights = jnp.exp(logits - largest)
        weights = weights * (1.0 / jnp.sum(weights, axis=1, keepdims=True))
        piece, within = place_of(r)
        values = jnp.concatenate(
            [cache[1, piece, within, :], qkv[rows, 2 * width : 3 * width], padding], axis=0
        )
        summed = jnp.dot(weights.astype(jnp.bfloat16), values, preferred_element_type=jnp.float32)
        out = summed[:QLEN]
        for h in range(1, heads):
            out = jnp.where(small_head == h, summed[h * QLEN : (h + 1) * QLEN], out)
        att[rows, :] = out.astype(jnp.bfloat16)
        return carry

    lax.fori_loop(0, requests, one_request, 0, unroll=ATT_UNROLL)


def attend(group_ids, qkv, base, rel_q_heads, columns, pieces):
    rows = qkv.shape[0]
    width = qkv.shape[1] // 3
    cached = rows // QLEN * PLEN
    return pl.pallas_call(
        attend_kernel,
        out_shape=jax.ShapeDtypeStruct((rows + EXTRA, width), jnp.bfloat16),
        in_specs=[pl.BlockSpec(memory_space=pltpu.SMEM)]
        + full_specs(4)
        + [pl.BlockSpec(memory_space=pl.ANY)] * len(pieces),
        out_specs=pl.BlockSpec(memory_space=pltpu.VMEM),
        scratch_shapes=[
            pltpu.VMEM((2, len(pieces)) + pieces[0].shape[1:], jnp.bfloat16),
            pltpu.VMEM((cached, width), jnp.bfloat16),
            pltpu.VMEM((cached, rel_q_heads.shape[0]), jnp.float32),
            pltpu.SemaphoreType.DMA((2, len(pieces))),
        ],
        compiler_params=params(12),
        cost_estimate=pl.CostEstimate(flops=2000 * MIB, bytes_accessed=2 * MIB, transcendentals=0),
        name="attend",
    )(group_ids, qkv, base, rel_q_heads, columns, *pieces)


def norm_rows(values, gain):
    centre = values - jnp.mean(values, axis=-1, keepdims=True)
    spread = jnp.mean(centre * centre, axis=-1, keepdims=True)
    return centre * lax.rsqrt(spread + 1e-07) * gain


def feed_rows(start, count, a, w, tokens, gain, w_up, w_down):
    rows = pl.ds(pl.multiple_of(start, 32), count)
    mixed = tokens[rows, :].astype(jnp.float32)
    for piece, weight in zip(a, w):
        mixed = mixed + jnp.dot(piece[rows, :], weight[...], preferred_element_type=jnp.float32)
    hidden = norm_rows(mixed, gain[...]).astype(jnp.bfloat16)
    total = None
    step = 256
    for at in range(0, w_up.shape[1], step):
        up = jnp.dot(hidden, w_up[:, at : at + step], preferred_element_type=jnp.float32)
        inner = (0.5 * up * (1.0 + lax.erf(up * math.sqrt(0.5)))).astype(jnp.bfloat16)
        part = jnp.dot(inner, w_down[at : at + step, :], preferred_element_type=jnp.float32)
        total = part if total is None else total + part
    return hidden, total


def feed_other_kernel(a0, a1, a2, a3, w0, w1, w2, w3, tokens, gain, w_up, w_down, out):
    core = lax.axis_index("head") % 2
    _, total = feed_rows(
        (1 - core) * out.shape[0], out.shape[0], (a0, a1, a2, a3), (w0, w1, w2, w3), tokens, gain, w_up, w_down
    )
    out[...] = total.astype(out.dtype)


def feed_own_kernel(a0, a1, a2, a3, w0, w1, w2, w3, tokens, gain, w_up, w_down, out, own):
    pieces, weights = (a0, a1, a2, a3), (w0, w1, w2, w3)
    count = out.shape[0]
    place = lax.axis_index("head")
    start = place % 2 * (2 * count)
    hidden, total = feed_rows(start, 2 * count, pieces, weights, tokens, gain, w_up, w_down)

    @pl.when(place // 2 == 0)
    def first():
        out[...] = total[count:]
        own[...] = hidden[:count].astype(jnp.float32) + total[:count]

    @pl.when(place // 2 != 0)
    def second():
        out[...] = total[:count]
        own[...] = hidden[count:].astype(jnp.float32) + total[count:]


def feed(kernel, pieces, weights, tokens, gain, w_up, w_down, outs, name):
    return pl.pallas_call(
        kernel,
        out_shape=outs,
        in_specs=full_specs(12),
        out_specs=full_specs(len(outs)),
        compiler_params=params(20),
        cost_estimate=pl.CostEstimate(flops=1600 * MIB, bytes_accessed=6 * MIB, transcendentals=0),
        name=name,
    )(*pieces, *weights, tokens, gain, w_up, w_down)


def fold_kernel(for_y, from_core, out):
    count = out.shape[0]
    other = 1 - lax.axis_index("head") // 2
    rows = pl.ds(pl.multiple_of(other * count, 32), count)
    out[...] = (for_y[...] + from_core[rows, :].astype(jnp.float32)).astype(out.dtype)


def block_of(head):
    return head % 2 * 2 + head // 2


def project_kernel(own, from_core, from_y, gain, w_proj, a0, a1, a2, a3, out, single):
    count = own.shape[0]
    place = lax.axis_index("head")
    rows = pl.ds(pl.multiple_of(place // 2 * count, 32), count)
    after = own[...] + from_core[rows, :].astype(jnp.float32) + from_y[...].astype(jnp.float32)
    hidden = norm_rows(after, gain[...]).astype(jnp.bfloat16)
    projected = jnp.dot(hidden, w_proj[...], preferred_element_type=jnp.float32)
    length = jnp.sum(projected * projected, axis=-1, keepdims=True)
    vectors = (projected * lax.rsqrt(length + 1e-06)).astype(jnp.bfloat16)
    single[...] = vectors
    pieces = (a0, a1, a2, a3)
    part = LANES // len(pieces) * 3 // 4
    lane = lax.broadcasted_iota(jnp.int32, (EXTRA, LANES), 1)
    lines = []
    for kind in range(2):
        line = jnp.zeros((EXTRA, LANES), jnp.float32)
        for x, piece in enumerate(pieces):
            from_head = place ^ x
            values = piece[piece.shape[0] - EXTRA :, kind * LANES : (kind + 1) * LANES]
            shift = lax.rem((from_head - block_of(place)) * part + LANES, LANES)
            rolled = pltpu.roll(values.astype(jnp.float32), shift, 1)
            line = jnp.where(lane // part == from_head, rolled, line)
        lines.append(line)
    which = lax.broadcasted_iota(jnp.int32, (EXTRA, LANES), 0)
    tail = jnp.where(which == 0, lines[0], lines[1]).astype(out.dtype)
    for o in range(out.shape[0]):
        out[o, :count] = vectors
        out[o, count:] = tail


def list_slots(queries, n_doc, listed):
    rows = queries.shape[0] // n_doc
    part = (rows - EXTRA) // QLEN * 8
    me = lax.axis_index("doc")
    shape = (n_doc, LANES)
    lane = lax.broadcasted_iota(jnp.int32, shape, 1)
    row = lax.broadcasted_iota(jnp.int32, shape, 0)
    tails = [
        queries[o * rows + rows - EXTRA : (o + 1) * rows, :].astype(jnp.float32) for o in range(n_doc)
    ]
    holder = jnp.concatenate([tail[:1] for tail in tails], axis=0).astype(jnp.int32)
    doc = jnp.concatenate([tail[1:2] for tail in tails], axis=0).astype(jnp.int32)
    mine = (lane < 4 * part) & (holder == me)
    group = (row * rows + lane % part // 8 * QLEN) // 16
    listed[n_doc : 2 * n_doc, :] = group | (doc << 8)
    ones = jnp.where(mine, 1.0, 0.0)
    until = lax.broadcasted_iota(jnp.int32, (LANES, LANES), 0) <= lax.broadcasted_iota(
        jnp.int32, (LANES, LANES), 1
    )
    until = jnp.where(until, 1.0, 0.0).astype(jnp.bfloat16)
    reached = jnp.dot(ones.astype(jnp.bfloat16), until, preferred_element_type=jnp.float32)
    in_row = jnp.sum(ones, axis=1, keepdims=True)
    above = jnp.zeros((1, 1), jnp.float32)
    starts = []
    for o in range(n_doc):
        starts.append(above)
        above = above + in_row[o : o + 1]
    reached = (reached + jnp.concatenate(starts, axis=0)).astype(jnp.int32)
    pad = jnp.zeros((LANES - n_doc, LANES), jnp.int32)
    columns = jnp.concatenate([reached, pad], axis=0).T
    square_lane = lax.broadcasted_iota(jnp.int32, (LANES, LANES), 1)
    blocks = (jnp.sum(ones).astype(jnp.int32) + LANES - 1) // LANES

    def one_block(block, carry):
        total = jnp.zeros((LANES, LANES), jnp.int32)
        for o in range(n_doc):
            passed = columns[:, o : o + 1] <= square_lane + block * LANES
            total = total + jnp.where(passed, 1, 0)
        listed[pl.ds(block, 1), :] = jnp.sum(total, axis=0, keepdims=True)
        return carry

    lax.fori_loop(0, blocks, one_block, 0)
    listed[n_doc - 1 : n_doc, :] = jnp.broadcast_to(above.astype(jnp.int32), (1, LANES))


def score_kernel(lengths, queries, docs, out, held, listed, slots, arrived, ready):
    chunks = arrived.shape[0]
    per = docs.shape[0] // chunks
    copies = [
        pltpu.make_async_copy(
            docs.at[pl.ds(c * per, per)], held.at[pl.ds(c * per, per)], arrived.at[c]
        )
        for c in range(chunks)
    ]
    for copy in copies:
        copy.start()
    list_slots(queries, out.shape[0], listed)
    to_scalars = pltpu.make_async_copy(listed, slots, ready)
    to_scalars.start()
    to_scalars.wait()
    for copy in copies:
        copy.wait()

    shape = (8, LANES)
    flat = lax.broadcasted_iota(jnp.int32, shape, 0) * LANES + lax.broadcasted_iota(jnp.int32, shape, 1)
    unroll = SCORE_UNROLL
    zero = jnp.zeros((QLEN, docs.shape[2]), jnp.bfloat16)
    position = lax.broadcasted_iota(jnp.int32, (docs.shape[1], 2 * QLEN), 0)
    side = lax.broadcasted_iota(jnp.int32, (1, 2 * QLEN), 1) < QLEN
    tables = out.shape[0]
    count = slots[tables - 1, 0]

    def some(i, totals):
        for u in range(0, unroll, 2):
            left, right, marks, limits = [], [], [], []
            for v in range(2):
                s = i * unroll + u + v
                used = s < count
                entry = jnp.where(used, slots[s >> 7, s & 127], 0)
                found = slots[tables + (entry >> 7), entry & 127]
                query = queries[pl.ds(pl.multiple_of((found & 255) * 16, 16), QLEN), :]
                doc = found >> 8
                left.append(jnp.concatenate([query, zero] if v == 0 else [zero, query], axis=1))
                right.append(held[doc])
                marks.append(jnp.where(used, entry, -1))
                limits.append(lengths[doc])
            sims = times_rows(jnp.concatenate(right, axis=1), jnp.concatenate(left, axis=0))
            limit = jnp.where(side, limits[0], limits[1])
            best = jnp.max(jnp.where(position < limit, sims, -jnp.inf), axis=0, keepdims=True)
            for v in range(2):
                total = jnp.sum(jnp.where(side if v == 0 else ~side, best, 0.0), axis=1, keepdims=True)
                totals = jnp.where(flat == marks[v], total, totals)
        return totals

    totals = lax.fori_loop(
        0, (count + unroll - 1) // unroll, some, jnp.zeros(shape, jnp.float32)
    )
    for o in range(out.shape[0]):
        row = jnp.broadcast_to(totals[o : o + 1], shape)
        for h in range(out.shape[1]):
            out[o, h] = row


def arrange_kernel(*refs):
    shares, out = refs[:-1], refs[-1]
    place = lax.axis_index("head")
    for k, share in enumerate(shares):
        count = share.shape[0]
        out[pl.ds(pl.multiple_of(block_of(place ^ k) * count, 32), count), :] = share[...]


def collect_kernel(tiles, out):
    n_head = tiles.shape[1]
    cols, reqs_all = out.shape
    reqs = reqs_all // n_head
    place = lax.axis_index("head")
    lines = []
    for h in range(n_head):
        total = tiles[0, h]
        for o in range(1, tiles.shape[0]):
            total = total + tiles[o, h]
        total = pltpu.roll(total, LANES - place * (reqs * cols), 1)
        lines.append(total[:1, : reqs * cols])
    order = sorted(range(n_head), key=block_of)
    rows = [lines[h][:, r * cols : (r + 1) * cols] for h in order for r in range(reqs)]
    out[...] = jnp.concatenate(rows, axis=0).T


def body(
    tokens,
    w_qkv,
    w_out,
    w_up,
    w_down,
    gain_one,
    gain_two,
    rel_table,
    prompt_cache,
    w_proj,
    doc_vectors,
    doc_lengths,
    group_ids,
    candidates,
):
    rows, depth = tokens.shape
    n_doc = lax.axis_size("doc")
    n_head = lax.axis_size("head")
    half, quarter = rows // 2, rows // n_head
    cand_rows, cols = candidates.shape
    reqs = cand_rows // n_head
    smem = pl.BlockSpec(memory_space=pltpu.SMEM)

    def over_doc(x, k):
        return lax.ppermute(x, "doc", [(i, i ^ k) for i in range(n_doc)])

    def over_head(x, k):
        return lax.ppermute(x, "head", [(i, i ^ k) for i in range(n_head)])

    tile = (8, LANES)
    pieces = {k: over_doc(prompt_cache, k) for k in (6, 5, 4, 3, 1, 2)}
    pieces[0] = prompt_cache
    pieces[6], rel_table = lax.optimization_barrier((pieces[6], rel_table))
    pieces[7] = over_doc(pieces[6], 1)
    pieces = [pieces[k] for k in range(n_doc)]
    weight = jnp.transpose(w_qkv, (1, 0, 2))
    qkv, base, rel_q_heads = prepare(tokens, weight, rel_table)

    out_one = over_head(w_out, 2)
    out_pieces = [w_out, over_head(w_out, 1), out_one, over_head(out_one, 1)]

    att = attend(group_ids, qkv, base, rel_q_heads, candidates.T, pieces)
    att_y = over_head(att, 2)
    att_pieces = [att, over_head(att, 1), att_y, over_head(att_y, 1)]

    common = (att_pieces, out_pieces, tokens, gain_one.reshape(1, -1), w_up, w_down)
    other = feed(
        feed_other_kernel,
        *common,
        [jax.ShapeDtypeStruct((half, depth), jnp.bfloat16)],
        "feed_other",
    )[0]
    from_core = over_head(other, 1)
    for_y, own = feed(
        feed_own_kernel,
        *common,
        [jax.ShapeDtypeStruct((quarter, depth), jnp.float32)] * 2,
        "feed_own",
    )
    folded = pl.pallas_call(
        fold_kernel,
        out_shape=jax.ShapeDtypeStruct((quarter, depth), jnp.bfloat16),
        in_specs=full_specs(2),
        out_specs=full_specs(1)[0],
        compiler_params=params(4),
        name="fold",
    )(for_y, from_core)
    from_y = over_head(folded, 2)

    emb = w_proj.shape[1]
    vectors, single = pl.pallas_call(
        project_kernel,
        out_shape=[
            jax.ShapeDtypeStruct((n_doc, quarter + EXTRA, emb), jnp.bfloat16),
            jax.ShapeDtypeStruct((quarter, emb), jnp.bfloat16),
        ],
        in_specs=full_specs(9),
        out_specs=full_specs(2),
        compiler_params=params(8),
        name="project",
    )(own, from_core, from_y, gain_two.reshape(1, -1), w_proj, *att_pieces)
    queries = lax.all_to_all(vectors, "doc", 0, 0, tiled=True).reshape(-1, emb)

    rated = pl.pallas_call(
        score_kernel,
        out_shape=jax.ShapeDtypeStruct((n_doc, n_head) + tile, jnp.float32),
        in_specs=[smem] + full_specs(1) + [pl.BlockSpec(memory_space=pltpu.HBM)],
        out_specs=full_specs(1)[0],
        scratch_shapes=[
            pltpu.VMEM(doc_vectors.shape, jnp.bfloat16),
            pltpu.VMEM((2 * n_doc, LANES), jnp.int32),
            pltpu.SMEM((2 * n_doc, LANES), jnp.int32),
            pltpu.SemaphoreType.DMA((8,)),
            pltpu.SemaphoreType.DMA,
        ],
        compiler_params=params(16),
        name="rate",
    )(doc_lengths, queries, far(doc_vectors))
    back = lax.all_to_all(rated.reshape(-1, LANES), ("doc", "head"), 0, 0, tiled=True)

    single, _ = lax.optimization_barrier((single, rated))
    shares = [single] + [over_head(single, k) for k in range(1, n_head)]
    query_vectors = pl.pallas_call(
        arrange_kernel,
        out_shape=jax.ShapeDtypeStruct((rows, emb), jnp.bfloat16),
        in_specs=full_specs(n_head),
        out_specs=full_specs(1)[0],
        compiler_params=params(4),
        name="arrange",
    )(*shares)

    scores = pl.pallas_call(
        collect_kernel,
        out_shape=jax.ShapeDtypeStruct((cols, cand_rows), jnp.float32),
        in_specs=full_specs(1),
        out_specs=full_specs(1)[0],
        compiler_params=params(4),
        name="collect",
    )(back.reshape((n_doc, n_head) + tile))
    return (query_vectors, scores.T)


def solution(mesh):
    placed = (
        P("doc", None),
        P(None, None, "head"),
        P("head", None),
        P(None, "head"),
        P("head", None),
        P(),
        P(),
        P(),
        P(None, "doc", "head"),
        P(),
        P("doc", None, None),
        P("doc"),
        P("doc"),
        P("doc", "head"),
    )
    fits = mesh.shape["head"] == 4 and mesh.shape["doc"] == 8
    return jax.shard_map(
        body if fits else body_any,
        mesh=mesh,
        in_specs=placed,
        out_specs=(P("doc", None), P("doc", "head")),
        check_vma=False,
    )
```

```python
import functools
import math

import jax
import jax.numpy as jnp
from jax import lax
from jax.experimental import pallas as pl
from jax.experimental.pallas import tpu as pltpu
from jax.sharding import PartitionSpec as P

HD = 64
RELS = 512
QLEN = 32
PLEN = 64
DOC_DEV = 64


def layer_norm(values, gain):
    centre = values - jnp.mean(values, axis=-1, keepdims=True)
    spread = jnp.mean(centre * centre, axis=-1, keepdims=True)
    return centre * lax.rsqrt(spread + 1e-07) * gain


def slot_order(holders):
    count = holders.shape[0]
    same = holders[:, None] == holders[None, :]
    earlier = jnp.arange(count)[:, None] > jnp.arange(count)[None, :]
    return jnp.sum(same & earlier, axis=1)


def rate_slots(slot_query, slot_doc, doc_vectors, doc_lengths):
    shape = slot_doc.shape
    flat_doc = slot_doc.reshape(-1)
    flat_query = slot_query.reshape((flat_doc.shape[0],) + slot_query.shape[-2:])
    safe_doc = jnp.maximum(flat_doc, 0)
    documents = doc_vectors[safe_doc]
    lengths = doc_lengths[safe_doc]
    sims = jnp.einsum("sqe,sje->sqj", flat_query, documents, preferred_element_type=jnp.float32)
    live = jnp.arange(documents.shape[1], dtype=jnp.int32)[None, None, :] < lengths[:, None, None]
    best = jnp.max(jnp.where(live, sims, -jnp.inf), axis=2)
    totals = jnp.where(flat_doc >= 0, jnp.sum(best, axis=1), 0.0)
    return totals.reshape(shape)


def body_any(
    tokens,
    w_qkv,
    w_out,
    w_up,
    w_down,
    gain_one,
    gain_two,
    rel_table,
    prompt_cache,
    w_proj,
    doc_vectors,
    doc_lengths,
    group_ids,
    candidates,
):
    rows_dev = tokens.shape[0]
    req_dev = rows_dev // QLEN
    width = w_qkv.shape[2]
    heads_loc = width // HD
    half = RELS // 2
    scale_root = math.sqrt(3 * HD)
    gathered = lax.all_gather(prompt_cache, "doc", axis=1, tiled=True)
    weights_split = w_qkv.reshape(w_qkv.shape[0], 3, heads_loc, HD)
    projected_all = jnp.einsum(
        "td,dchf->chtf", tokens, weights_split, preferred_element_type=jnp.float32
    ).astype(jnp.bfloat16)
    rel_both = jnp.einsum(
        "rd,dchf->chrf", rel_table, weights_split[:, :2], preferred_element_type=jnp.float32
    ).astype(jnp.bfloat16)
    head_shape = (heads_loc, req_dev, QLEN, HD)
    query_four = projected_all[0].reshape(head_shape)
    keys_four = projected_all[1].reshape(head_shape)
    values_four = projected_all[2].reshape(head_shape)
    groups_all = gathered.shape[1] // PLEN
    cache_all = gathered.reshape(2, groups_all, PLEN, heads_loc, HD)
    picked = jnp.transpose(cache_all[:, group_ids], (0, 3, 1, 2, 4))
    keys = jnp.concatenate([keys_four, picked[0]], axis=2)
    values = jnp.concatenate([values_four, picked[1]], axis=2)
    pos_query = PLEN + jnp.arange(QLEN, dtype=jnp.int32)
    pos_key = jnp.concatenate([pos_query, jnp.arange(PLEN, dtype=jnp.int32)])
    index_one = pos_query[:, None] - pos_key[None, :] + half
    index_two = pos_key[:, None] - pos_query[None, :] + half
    rel_k_rows = rel_both[1][:, index_one]
    rel_q_rows = rel_both[0][:, index_two]
    c2p = jnp.einsum("hrqd,hqkd->hrqk", query_four, rel_k_rows, preferred_element_type=jnp.float32)
    p2c = jnp.einsum("hrkd,hkqd->hrqk", keys, rel_q_rows, preferred_element_type=jnp.float32)
    content = jnp.einsum("hrqd,hrkd->hrqk", query_four, keys, preferred_element_type=jnp.float32)
    logits = (content + c2p + p2c) / scale_root
    largest = jnp.max(logits, axis=-1, keepdims=True)
    weights = jnp.exp(logits - largest)
    denominator = jnp.sum(weights, axis=-1)
    summed = jnp.einsum(
        "hrqk,hrkd->hrqd", weights.astype(jnp.bfloat16), values, preferred_element_type=jnp.float32
    )
    attended = (summed / denominator[..., None]).astype(jnp.bfloat16)
    out_split = w_out.reshape(heads_loc, HD, w_out.shape[1])
    attn_part = jnp.einsum(
        "hrqd,hde->rqe", attended, out_split, preferred_element_type=jnp.float32
    ).reshape(rows_dev, w_out.shape[1])
    attn_total = lax.psum(attn_part.astype(jnp.bfloat16), "head").astype(jnp.float32)
    hidden_one = layer_norm(tokens.astype(jnp.float32) + attn_total, gain_one).astype(jnp.bfloat16)
    inner = jax.nn.gelu(
        jnp.dot(hidden_one, w_up, preferred_element_type=jnp.float32), approximate=False
    ).astype(jnp.bfloat16)
    ffn_total = lax.psum(
        jnp.dot(inner, w_down, preferred_element_type=jnp.float32).astype(jnp.bfloat16), "head"
    ).astype(jnp.float32)
    hidden_two = layer_norm(hidden_one.astype(jnp.float32) + ffn_total, gain_two).astype(
        jnp.bfloat16
    )
    projected = jnp.dot(hidden_two, w_proj, preferred_element_type=jnp.float32)
    query_vectors = (
        projected * lax.rsqrt(jnp.sum(projected * projected, axis=-1, keepdims=True) + 1e-06)
    ).astype(jnp.bfloat16)
    shards = lax.axis_size("doc")
    cand_dev = candidates.shape[1]
    pairs = req_dev * cand_dev
    capacity = max(2, 2 * pairs // shards)
    flat_cand = candidates.reshape(-1)
    holders = flat_cand // DOC_DEV
    request_of = jnp.arange(pairs, dtype=jnp.int32) // cand_dev
    slot_rank = slot_order(holders)
    copies, cand_copies = (
        lax.all_gather(query_vectors, "doc", axis=0, tiled=True),
        lax.all_gather(candidates, "doc", axis=0, tiled=True),
    )
    all_query = copies.reshape(shards, req_dev, QLEN, copies.shape[1])
    all_cand = cand_copies.reshape(shards, pairs)
    holder_all = all_cand // DOC_DEV
    local_all = all_cand % DOC_DEV
    rank_all = jax.vmap(slot_order)(holder_all)
    own_index = lax.axis_index("doc")
    chosen = (holder_all[:, None, :] == own_index) & (
        rank_all[:, None, :] == jnp.arange(capacity, dtype=jnp.int32)[None, :, None]
    )
    filled = jnp.any(chosen, axis=2)
    slot_request = jnp.sum(jnp.where(chosen, request_of[None, None, :], 0), axis=2)
    slot_doc = jnp.where(
        filled, jnp.sum(jnp.where(chosen, local_all[:, None, :], 0), axis=2), -1
    ).astype(jnp.int32)
    slot_query = all_query[jnp.arange(shards)[:, None], slot_request]
    slot_scores = rate_slots(slot_query, slot_doc, doc_vectors, doc_lengths)
    returned = lax.all_to_all(slot_scores, "doc", split_axis=0, concat_axis=0, tiled=True)
    scores = returned.reshape(-1)[holders * capacity + slot_rank].reshape(candidates.shape)
    return (query_vectors, scores)


LANES = 128
MIB = 1 << 20
EXTRA = 16
PREP_UNROLL = 6
ATT_UNROLL = 12
SCORE_UNROLL = 32


def full_specs(count):
    return [pl.BlockSpec(memory_space=pltpu.VMEM)] * count


def far(x):
    return pltpu.with_memory_space_constraint(x, pltpu.HBM)


def params(mib):
    return pltpu.CompilerParams(vmem_limit_bytes=mib * MIB)


def by_head(values):
    head_of = lax.broadcasted_iota(jnp.int32, values.shape, 1) // HD
    heads = values.shape[1] // HD
    zero = jnp.zeros_like(values)
    return jnp.concatenate([jnp.where(head_of == h, values, zero) for h in range(heads)], axis=0)


def times_rows(left, right):
    return lax.dot_general(left, right, (((1,), (1,)), ((), ())), preferred_element_type=jnp.float32)


def key_terms(key_rel, first):
    slot = lax.broadcasted_iota(jnp.int32, (key_rel.shape[0], LANES), 1) // QLEN
    turned = None
    for h in range(key_rel.shape[1] // LANES):
        shift = (LANES - PLEN - QLEN + first + h * QLEN) % LANES
        rolled = pltpu.roll(
            key_rel[:, h * LANES : (h + 1) * LANES], shift, 1, stride=1, stride_axis=0
        )
        turned = rolled if turned is None else jnp.where(slot == h, rolled, turned)
    return turned


def prepare_kernel(
    tokens_far, weight_far, rel_table, qkv, base, rel_q_heads, q_heads, query_rel, key_rel, *scratch
):
    tokens, weight, rel_rows, arrived = scratch
    rel_far = rel_table.at[pl.ds(RELS // 2 - PLEN - QLEN, rel_rows.shape[0])]
    copies = [pltpu.make_async_copy(tokens_far, tokens, arrived.at[0])]
    copies += [pltpu.make_async_copy(weight_far.at[i], weight.at[i], arrived.at[1 + i]) for i in range(3)]
    copies += [pltpu.make_async_copy(rel_far, rel_rows, arrived.at[4])]
    for copy in copies:
        copy.start()
    copies[0].wait()
    width = weight.shape[2]
    heads = width // HD
    for i in range(3):
        copies[1 + i].wait()
        qkv[:, i * width : (i + 1) * width] = jnp.dot(
            tokens[...], weight[i], preferred_element_type=jnp.float32
        ).astype(jnp.bfloat16)
    count = rel_rows.shape[0]
    copies[4].wait()
    rel = [
        jnp.dot(rel_rows[...], weight[i], preferred_element_type=jnp.float32).astype(jnp.bfloat16)
        for i in range(2)
    ]
    both = lax.broadcasted_iota(jnp.int32, (LANES, count), 0) + lax.broadcasted_iota(
        jnp.int32, (LANES, count), 1
    )
    flip_q = jnp.where(both == LANES, 1.0, 0.0).astype(jnp.bfloat16)
    flip_k = jnp.where(both == LANES + PLEN - 1, 1.0, 0.0).astype(jnp.bfloat16)
    rel_q = jnp.dot(flip_q, rel[0], preferred_element_type=jnp.float32)
    rel_k = jnp.dot(flip_k, rel[1], preferred_element_type=jnp.float32)
    rel_q_heads[...] = by_head(rel_q.astype(jnp.bfloat16))
    requests, _, many = base.shape
    for r in range(requests):
        q_heads[r * many : (r + 1) * many, :] = by_head(qkv[r * QLEN : (r + 1) * QLEN, :width])
    query_rel[...] = times_rows(q_heads[...], rel_k.astype(jnp.bfloat16))
    key_rel[...] = times_rows(qkv[:, width : 2 * width], rel_q_heads[...])
    scale = 1.0 / math.sqrt(3 * HD)

    def one_request(r, carry):
        rows = pl.ds(pl.multiple_of(r * QLEN, QLEN), QLEN)
        spread = pl.ds(pl.multiple_of(r * many, many), many)
        turned = times_rows(qkv[rows, width : 2 * width], q_heads[spread, :])
        turned = turned + key_terms(key_rel[rows, :], PLEN)
        spread_rel = query_rel[spread, :]
        c2p = jnp.concatenate(
            [
                pltpu.roll(
                    spread_rel[h * QLEN : (h + 1) * QLEN],
                    LANES - QLEN + 1,
                    1,
                    stride=1,
                    stride_axis=0,
                )
                for h in range(heads)
            ],
            axis=0,
        )
        c2p = c2p.T
        base[r, :PLEN] = c2p[:PLEN] * scale
        base[r, PLEN:] = (c2p[PLEN : PLEN + QLEN] + turned) * scale
        return carry

    lax.fori_loop(0, requests, one_request, 0, unroll=PREP_UNROLL)


def prepare(tokens, weight, rel_table):
    rows = tokens.shape[0]
    width = weight.shape[2]
    heads = width // HD
    return pl.pallas_call(
        prepare_kernel,
        out_shape=[
            jax.ShapeDtypeStruct((rows, 3 * width), jnp.bfloat16),
            jax.ShapeDtypeStruct((rows // QLEN, PLEN + QLEN, heads * QLEN), jnp.float32),
            jax.ShapeDtypeStruct((heads * LANES, width), jnp.bfloat16),
        ],
        in_specs=[pl.BlockSpec(memory_space=pltpu.HBM)] * 3,
        out_specs=full_specs(3),
        scratch_shapes=[
            pltpu.VMEM((rows * heads, width), jnp.bfloat16),
            pltpu.VMEM((rows * heads, LANES), jnp.float32),
            pltpu.VMEM((rows, heads * LANES), jnp.float32),
            pltpu.VMEM(tokens.shape, jnp.bfloat16),
            pltpu.VMEM(weight.shape, jnp.bfloat16),
            pltpu.VMEM((2 * (PLEN + QLEN), rel_table.shape[1]), jnp.bfloat16),
            pltpu.SemaphoreType.DMA((5,)),
        ],
        compiler_params=params(16),
        cost_estimate=pl.CostEstimate(flops=4000 * MIB, bytes_accessed=4 * MIB, transcendentals=0),
        name="prepare",
    )(far(tokens), far(weight), far(rel_table))


def attend_kernel(group_ids, qkv, base, rel_q_heads, columns, *rest):
    pieces, (att, cache, picked, key_rel, shares, arrived) = rest[:-6], rest[-6:]
    copies = [
        [
            pltpu.make_async_copy(piece.at[kind], cache.at[kind, at], arrived.at[kind, at])
            for at, piece in enumerate(pieces)
        ]
        for kind in range(2)
    ]
    for copy in copies[0] + copies[1]:
        copy.start()
    requests, _, _ = base.shape
    tokens = requests * QLEN
    ids = columns[...].T
    spare = jnp.zeros((1, LANES - columns.shape[0] * columns.shape[1]), jnp.int32)
    line = jnp.concatenate([ids[r : r + 1, :] for r in range(ids.shape[0])] + [spare], axis=1)
    line = jnp.concatenate([line // DOC_DEV, line % DOC_DEV], axis=1)
    extra = jnp.broadcast_to(line.astype(jnp.float32), (EXTRA, line.shape[1]))
    att[tokens:, :] = extra.astype(att.dtype)
    width = att.shape[1]
    heads = width // HD
    groups_dev = cache.shape[2] // PLEN
    me = lax.axis_index("doc")
    small_head = lax.broadcasted_iota(jnp.int32, (QLEN, width), 1) // HD
    scale = 1.0 / math.sqrt(3 * HD)

    def place_of(r):
        owner = group_ids[r] // groups_dev
        within = pl.multiple_of((group_ids[r] - owner * groups_dev) * PLEN, PLEN)
        return owner ^ me, pl.ds(within, PLEN)

    for copy in copies[0]:
        copy.wait()
    for r in range(requests):
        piece, within = place_of(r)
        picked[r * PLEN : (r + 1) * PLEN, :] = cache[0, piece, within, :]
    key_rel[...] = times_rows(picked[...], rel_q_heads[...])

    def one_softmax(r, carry):
        rows = pl.ds(pl.multiple_of(r * QLEN, QLEN), QLEN)
        cached = pl.ds(pl.multiple_of(r * PLEN, PLEN), PLEN)
        turned = times_rows(picked[cached, :], by_head(qkv[rows, 0:width]))
        turned = (turned + key_terms(key_rel[cached, :], 0)) * scale
        logits = jnp.concatenate([base[r, :PLEN] + turned, base[r, PLEN:]], axis=0)
        weights = jnp.exp(logits - jnp.max(logits, axis=0, keepdims=True))
        weights = weights * (1.0 / jnp.sum(weights, axis=0, keepdims=True))
        shares[r] = weights.astype(shares.dtype)
        return carry

    lax.fori_loop(0, requests, one_softmax, 0, unroll=ATT_UNROLL)
    for copy in copies[1]:
        copy.wait()

    def one_sum(r, carry):
        rows = pl.ds(pl.multiple_of(r * QLEN, QLEN), QLEN)
        piece, within = place_of(r)
        values = jnp.concatenate(
            [cache[1, piece, within, :], qkv[rows, 2 * width : 3 * width]], axis=0
        )
        summed = lax.dot_general(
            shares[r],
            values,
            (((0,), (0,)), ((), ())),
            preferred_element_type=jnp.float32,
        )
        out = summed[:QLEN]
        for h in range(1, heads):
            out = jnp.where(small_head == h, summed[h * QLEN : (h + 1) * QLEN], out)
        att[rows, :] = out.astype(jnp.bfloat16)
        return carry

    lax.fori_loop(0, requests, one_sum, 0, unroll=ATT_UNROLL)


def attend(group_ids, qkv, base, rel_q_heads, columns, pieces):
    rows = qkv.shape[0]
    width = qkv.shape[1] // 3
    cached = rows // QLEN * PLEN
    return pl.pallas_call(
        attend_kernel,
        out_shape=jax.ShapeDtypeStruct((rows + EXTRA, width), jnp.bfloat16),
        in_specs=[pl.BlockSpec(memory_space=pltpu.SMEM)]
        + full_specs(4)
        + [pl.BlockSpec(memory_space=pl.ANY)] * len(pieces),
        out_specs=pl.BlockSpec(memory_space=pltpu.VMEM),
        scratch_shapes=[
            pltpu.VMEM((2, len(pieces)) + pieces[0].shape[1:], jnp.bfloat16),
            pltpu.VMEM((cached, width), jnp.bfloat16),
            pltpu.VMEM((cached, rel_q_heads.shape[0]), jnp.float32),
            pltpu.VMEM(base.shape, jnp.bfloat16),
            pltpu.SemaphoreType.DMA((2, len(pieces))),
        ],
        compiler_params=params(12),
        cost_estimate=pl.CostEstimate(flops=2000 * MIB, bytes_accessed=2 * MIB, transcendentals=0),
        name="attend",
    )(group_ids, qkv, base, rel_q_heads, columns, *pieces)


def norm_rows(values, gain):
    centre = values - jnp.mean(values, axis=-1, keepdims=True)
    spread = jnp.mean(centre * centre, axis=-1, keepdims=True)
    return centre * lax.rsqrt(spread + 1e-07) * gain


def feed_rows(start, count, a, w, tokens, gain, w_up, w_down):
    rows = pl.ds(pl.multiple_of(start, 32), count)
    mixed = tokens[rows, :].astype(jnp.float32)
    for piece, weight in zip(a, w):
        mixed = mixed + jnp.dot(piece[rows, :], weight[...], preferred_element_type=jnp.float32)
    hidden = norm_rows(mixed, gain[...]).astype(jnp.bfloat16)
    total = None
    step = 256
    for at in range(0, w_up.shape[1], step):
        up = jnp.dot(hidden, w_up[:, at : at + step], preferred_element_type=jnp.float32)
        inner = (0.5 * up * (1.0 + lax.erf(up * math.sqrt(0.5)))).astype(jnp.bfloat16)
        part = jnp.dot(inner, w_down[at : at + step, :], preferred_element_type=jnp.float32)
        total = part if total is None else total + part
    return hidden, total


def feed_other_kernel(a0, a1, a2, a3, w0, w1, w2, w3, tokens, gain, w_up, w_down, out):
    core = lax.axis_index("head") % 2
    _, total = feed_rows(
        (1 - core) * out.shape[0], out.shape[0], (a0, a1, a2, a3), (w0, w1, w2, w3), tokens, gain, w_up, w_down
    )
    out[...] = total.astype(out.dtype)


def feed_own_kernel(a0, a1, a2, a3, w0, w1, w2, w3, tokens, gain, w_up, w_down, out, own):
    pieces, weights = (a0, a1, a2, a3), (w0, w1, w2, w3)
    count = out.shape[0]
    place = lax.axis_index("head")
    start = place % 2 * (2 * count)
    hidden, total = feed_rows(start, 2 * count, pieces, weights, tokens, gain, w_up, w_down)

    @pl.when(place // 2 == 0)
    def first():
        out[...] = total[count:]
        own[...] = hidden[:count].astype(jnp.float32) + total[:count]

    @pl.when(place // 2 != 0)
    def second():
        out[...] = total[:count]
        own[...] = hidden[count:].astype(jnp.float32) + total[count:]


def feed(kernel, pieces, weights, tokens, gain, w_up, w_down, outs, name):
    return pl.pallas_call(
        kernel,
        out_shape=outs,
        in_specs=full_specs(12),
        out_specs=full_specs(len(outs)),
        compiler_params=params(20),
        cost_estimate=pl.CostEstimate(flops=1600 * MIB, bytes_accessed=6 * MIB, transcendentals=0),
        name=name,
    )(*pieces, *weights, tokens, gain, w_up, w_down)


def fold_kernel(for_y, from_core, out):
    count = out.shape[0]
    other = 1 - lax.axis_index("head") // 2
    rows = pl.ds(pl.multiple_of(other * count, 32), count)
    out[...] = (for_y[...] + from_core[rows, :].astype(jnp.float32)).astype(out.dtype)


def block_of(head):
    return head % 2 * 2 + head // 2


def project_kernel(own, from_core, from_y, gain, w_proj, a0, a1, a2, a3, out, single):
    count = own.shape[0]
    place = lax.axis_index("head")
    rows = pl.ds(pl.multiple_of(place // 2 * count, 32), count)
    after = own[...] + from_core[rows, :].astype(jnp.float32) + from_y[...].astype(jnp.float32)
    hidden = norm_rows(after, gain[...]).astype(jnp.bfloat16)
    projected = jnp.dot(hidden, w_proj[...], preferred_element_type=jnp.float32)
    length = jnp.sum(projected * projected, axis=-1, keepdims=True)
    vectors = (projected * lax.rsqrt(length + 1e-06)).astype(jnp.bfloat16)
    single[...] = vectors
    pieces = (a0, a1, a2, a3)
    part = LANES // len(pieces) * 3 // 4
    lane = lax.broadcasted_iota(jnp.int32, (EXTRA, LANES), 1)
    lines = []
    for kind in range(2):
        line = jnp.zeros((EXTRA, LANES), jnp.float32)
        for x, piece in enumerate(pieces):
            from_head = place ^ x
            values = piece[piece.shape[0] - EXTRA :, kind * LANES : (kind + 1) * LANES]
            shift = lax.rem((from_head - block_of(place)) * part + LANES, LANES)
            rolled = pltpu.roll(values.astype(jnp.float32), shift, 1)
            line = jnp.where(lane // part == from_head, rolled, line)
        lines.append(line)
    which = lax.broadcasted_iota(jnp.int32, (EXTRA, LANES), 0)
    tail = jnp.where(which == 0, lines[0], lines[1]).astype(out.dtype)
    for o in range(out.shape[0]):
        out[o, :count] = vectors
        out[o, count:] = tail


def list_slots(queries, n_doc, listed):
    rows = queries.shape[0] // n_doc
    part = (rows - EXTRA) // QLEN * 8
    me = lax.axis_index("doc")
    shape = (n_doc, LANES)
    lane = lax.broadcasted_iota(jnp.int32, shape, 1)
    row = lax.broadcasted_iota(jnp.int32, shape, 0)
    tails = [
        queries[o * rows + rows - EXTRA : (o + 1) * rows, :].astype(jnp.float32) for o in range(n_doc)
    ]
    holder = jnp.concatenate([tail[:1] for tail in tails], axis=0).astype(jnp.int32)
    doc = jnp.concatenate([tail[1:2] for tail in tails], axis=0).astype(jnp.int32)
    mine = (lane < 4 * part) & (holder == me)
    group = (row * rows + lane % part // 8 * QLEN) // 16
    listed[n_doc : 2 * n_doc, :] = group | (doc << 8)
    ones = jnp.where(mine, 1.0, 0.0)
    until = lax.broadcasted_iota(jnp.int32, (LANES, LANES), 0) <= lax.broadcasted_iota(
        jnp.int32, (LANES, LANES), 1
    )
    until = jnp.where(until, 1.0, 0.0).astype(jnp.bfloat16)
    reached = jnp.dot(ones.astype(jnp.bfloat16), until, preferred_element_type=jnp.float32)
    in_row = jnp.sum(ones, axis=1, keepdims=True)
    above = jnp.zeros((1, 1), jnp.float32)
    starts = []
    for o in range(n_doc):
        starts.append(above)
        above = above + in_row[o : o + 1]
    reached = (reached + jnp.concatenate(starts, axis=0)).astype(jnp.int32)
    pad = jnp.zeros((LANES - n_doc, LANES), jnp.int32)
    columns = jnp.concatenate([reached, pad], axis=0).T
    square_lane = lax.broadcasted_iota(jnp.int32, (LANES, LANES), 1)
    blocks = (jnp.sum(ones).astype(jnp.int32) + LANES - 1) // LANES

    def one_block(block, carry):
        total = jnp.zeros((LANES, LANES), jnp.int32)
        for o in range(n_doc):
            passed = columns[:, o : o + 1] <= square_lane + block * LANES
            total = total + jnp.where(passed, 1, 0)
        listed[pl.ds(block, 1), :] = jnp.sum(total, axis=0, keepdims=True)
        return carry

    lax.fori_loop(0, blocks, one_block, 0)
    listed[n_doc - 1 : n_doc, :] = jnp.broadcast_to(above.astype(jnp.int32), (1, LANES))


def score_kernel(lengths, queries, docs, out, held, listed, slots, arrived, ready):
    chunks = arrived.shape[0]
    per = docs.shape[0] // chunks
    copies = [
        pltpu.make_async_copy(
            docs.at[pl.ds(c * per, per)], held.at[pl.ds(c * per, per)], arrived.at[c]
        )
        for c in range(chunks)
    ]
    for copy in copies:
        copy.start()
    list_slots(queries, out.shape[0], listed)
    to_scalars = pltpu.make_async_copy(listed, slots, ready)
    to_scalars.start()
    to_scalars.wait()
    for copy in copies:
        copy.wait()

    shape = (8, LANES)
    flat = lax.broadcasted_iota(jnp.int32, shape, 0) * LANES + lax.broadcasted_iota(jnp.int32, shape, 1)
    unroll = SCORE_UNROLL
    zero = jnp.zeros((QLEN, docs.shape[2]), jnp.bfloat16)
    position = lax.broadcasted_iota(jnp.int32, (docs.shape[1], 2 * QLEN), 0)
    side = lax.broadcasted_iota(jnp.int32, (1, 2 * QLEN), 1) < QLEN
    tables = out.shape[0]
    count = slots[tables - 1, 0]

    def some(i, totals):
        for u in range(0, unroll, 2):
            left, right, marks, limits = [], [], [], []
            for v in range(2):
                s = i * unroll + u + v
                used = s < count
                entry = jnp.where(used, slots[s >> 7, s & 127], 0)
                found = slots[tables + (entry >> 7), entry & 127]
                query = queries[pl.ds(pl.multiple_of((found & 255) * 16, 16), QLEN), :]
                doc = found >> 8
                left.append(jnp.concatenate([query, zero] if v == 0 else [zero, query], axis=1))
                right.append(held[doc])
                marks.append(jnp.where(used, entry, -1))
                limits.append(lengths[doc])
            sims = times_rows(jnp.concatenate(right, axis=1), jnp.concatenate(left, axis=0))
            limit = jnp.where(side, limits[0], limits[1])
            best = jnp.max(jnp.where(position < limit, sims, -jnp.inf), axis=0, keepdims=True)
            for v in range(2):
                total = jnp.sum(jnp.where(side if v == 0 else ~side, best, 0.0), axis=1, keepdims=True)
                totals = jnp.where(flat == marks[v], total, totals)
        return totals

    totals = lax.fori_loop(
        0, (count + unroll - 1) // unroll, some, jnp.zeros(shape, jnp.float32)
    )
    for o in range(out.shape[0]):
        row = jnp.broadcast_to(totals[o : o + 1], shape)
        for h in range(out.shape[1]):
            out[o, h] = row


def arrange_kernel(*refs):
    shares, out = refs[:-1], refs[-1]
    place = lax.axis_index("head")
    for k, share in enumerate(shares):
        count = share.shape[0]
        out[pl.ds(pl.multiple_of(block_of(place ^ k) * count, 32), count), :] = share[...]


def collect_kernel(tiles, out):
    n_head = tiles.shape[1]
    cols, reqs_all = out.shape
    reqs = reqs_all // n_head
    place = lax.axis_index("head")
    lines = []
    for h in range(n_head):
        total = tiles[0, h]
        for o in range(1, tiles.shape[0]):
            total = total + tiles[o, h]
        total = pltpu.roll(total, LANES - place * (reqs * cols), 1)
        lines.append(total[:1, : reqs * cols])
    order = sorted(range(n_head), key=block_of)
    rows = [lines[h][:, r * cols : (r + 1) * cols] for h in order for r in range(reqs)]
    out[...] = jnp.concatenate(rows, axis=0).T


def body(
    tokens,
    w_qkv,
    w_out,
    w_up,
    w_down,
    gain_one,
    gain_two,
    rel_table,
    prompt_cache,
    w_proj,
    doc_vectors,
    doc_lengths,
    group_ids,
    candidates,
):
    rows, depth = tokens.shape
    n_doc = lax.axis_size("doc")
    n_head = lax.axis_size("head")
    half, quarter = rows // 2, rows // n_head
    cand_rows, cols = candidates.shape
    reqs = cand_rows // n_head
    smem = pl.BlockSpec(memory_space=pltpu.SMEM)

    def over_doc(x, k):
        return lax.ppermute(x, "doc", [(i, i ^ k) for i in range(n_doc)])

    def over_head(x, k):
        return lax.ppermute(x, "head", [(i, i ^ k) for i in range(n_head)])

    tile = (8, LANES)
    pieces = {k: over_doc(prompt_cache, k) for k in (6, 5, 4, 3, 1, 2)}
    pieces[0] = prompt_cache
    pieces[6], rel_table = lax.optimization_barrier((pieces[6], rel_table))
    pieces[7] = over_doc(pieces[6], 1)
    pieces = [pieces[k] for k in range(n_doc)]
    weight = jnp.transpose(w_qkv, (1, 0, 2))
    qkv, base, rel_q_heads = prepare(tokens, weight, rel_table)

    out_one = over_head(w_out, 2)
    out_pieces = [w_out, over_head(w_out, 1), out_one, over_head(out_one, 1)]

    att = attend(group_ids, qkv, base, rel_q_heads, candidates.T, pieces)
    att_y = over_head(att, 2)
    att_pieces = [att, over_head(att, 1), att_y, over_head(att_y, 1)]

    common = (att_pieces, out_pieces, tokens, gain_one.reshape(1, -1), w_up, w_down)
    other = feed(
        feed_other_kernel,
        *common,
        [jax.ShapeDtypeStruct((half, depth), jnp.bfloat16)],
        "feed_other",
    )[0]
    from_core = over_head(other, 1)
    for_y, own = feed(
        feed_own_kernel,
        *common,
        [jax.ShapeDtypeStruct((quarter, depth), jnp.float32)] * 2,
        "feed_own",
    )
    folded = pl.pallas_call(
        fold_kernel,
        out_shape=jax.ShapeDtypeStruct((quarter, depth), jnp.bfloat16),
        in_specs=full_specs(2),
        out_specs=full_specs(1)[0],
        compiler_params=params(4),
        name="fold",
    )(for_y, from_core)
    from_y = over_head(folded, 2)

    emb = w_proj.shape[1]
    vectors, single = pl.pallas_call(
        project_kernel,
        out_shape=[
            jax.ShapeDtypeStruct((n_doc, quarter + EXTRA, emb), jnp.bfloat16),
            jax.ShapeDtypeStruct((quarter, emb), jnp.bfloat16),
        ],
        in_specs=full_specs(9),
        out_specs=full_specs(2),
        compiler_params=params(8),
        name="project",
    )(own, from_core, from_y, gain_two.reshape(1, -1), w_proj, *att_pieces)
    queries = lax.all_to_all(vectors, "doc", 0, 0, tiled=True).reshape(-1, emb)

    rated = pl.pallas_call(
        score_kernel,
        out_shape=jax.ShapeDtypeStruct((n_doc, n_head) + tile, jnp.float32),
        in_specs=[smem] + full_specs(1) + [pl.BlockSpec(memory_space=pltpu.HBM)],
        out_specs=full_specs(1)[0],
        scratch_shapes=[
            pltpu.VMEM(doc_vectors.shape, jnp.bfloat16),
            pltpu.VMEM((2 * n_doc, LANES), jnp.int32),
            pltpu.SMEM((2 * n_doc, LANES), jnp.int32),
            pltpu.SemaphoreType.DMA((8,)),
            pltpu.SemaphoreType.DMA,
        ],
        compiler_params=params(16),
        name="rate",
    )(doc_lengths, queries, far(doc_vectors))
    back = lax.all_to_all(rated.reshape(-1, LANES), ("doc", "head"), 0, 0, tiled=True)

    single, _ = lax.optimization_barrier((single, rated))
    shares = [single] + [over_head(single, k) for k in range(1, n_head)]
    query_vectors = pl.pallas_call(
        arrange_kernel,
        out_shape=jax.ShapeDtypeStruct((rows, emb), jnp.bfloat16),
        in_specs=full_specs(n_head),
        out_specs=full_specs(1)[0],
        compiler_params=params(4),
        name="arrange",
    )(*shares)

    scores = pl.pallas_call(
        collect_kernel,
        out_shape=jax.ShapeDtypeStruct((cols, cand_rows), jnp.float32),
        in_specs=full_specs(1),
        out_specs=full_specs(1)[0],
        compiler_params=params(4),
        name="collect",
    )(back.reshape((n_doc, n_head) + tile))
    return (query_vectors, scores.T)


def solution(mesh):
    placed = (
        P("doc", None),
        P(None, None, "head"),
        P("head", None),
        P(None, "head"),
        P("head", None),
        P(),
        P(),
        P(),
        P(None, "doc", "head"),
        P(),
        P("doc", None, None),
        P("doc"),
        P("doc"),
        P("doc", "head"),
    )
    fits = mesh.shape["head"] == 4 and mesh.shape["doc"] == 8
    return jax.shard_map(
        body if fits else body_any,
        mesh=mesh,
        in_specs=placed,
        out_specs=(P("doc", None), P("doc", "head")),
        check_vma=False,
    )
```

```python
import functools
import math

import jax
import jax.numpy as jnp
from jax import lax
from jax.experimental import pallas as pl
from jax.experimental.pallas import tpu as pltpu
from jax.sharding import PartitionSpec as P

HD = 64
RELS = 512
QLEN = 32
PLEN = 64
DOC_DEV = 64


def layer_norm(values, gain):
    centre = values - jnp.mean(values, axis=-1, keepdims=True)
    spread = jnp.mean(centre * centre, axis=-1, keepdims=True)
    return centre * lax.rsqrt(spread + 1e-07) * gain


def slot_order(holders):
    count = holders.shape[0]
    same = holders[:, None] == holders[None, :]
    earlier = jnp.arange(count)[:, None] > jnp.arange(count)[None, :]
    return jnp.sum(same & earlier, axis=1)


def rate_slots(slot_query, slot_doc, doc_vectors, doc_lengths):
    shape = slot_doc.shape
    flat_doc = slot_doc.reshape(-1)
    flat_query = slot_query.reshape((flat_doc.shape[0],) + slot_query.shape[-2:])
    safe_doc = jnp.maximum(flat_doc, 0)
    documents = doc_vectors[safe_doc]
    lengths = doc_lengths[safe_doc]
    sims = jnp.einsum("sqe,sje->sqj", flat_query, documents, preferred_element_type=jnp.float32)
    live = jnp.arange(documents.shape[1], dtype=jnp.int32)[None, None, :] < lengths[:, None, None]
    best = jnp.max(jnp.where(live, sims, -jnp.inf), axis=2)
    totals = jnp.where(flat_doc >= 0, jnp.sum(best, axis=1), 0.0)
    return totals.reshape(shape)


def body_any(
    tokens,
    w_qkv,
    w_out,
    w_up,
    w_down,
    gain_one,
    gain_two,
    rel_table,
    prompt_cache,
    w_proj,
    doc_vectors,
    doc_lengths,
    group_ids,
    candidates,
):
    rows_dev = tokens.shape[0]
    req_dev = rows_dev // QLEN
    width = w_qkv.shape[2]
    heads_loc = width // HD
    half = RELS // 2
    scale_root = math.sqrt(3 * HD)
    gathered = lax.all_gather(prompt_cache, "doc", axis=1, tiled=True)
    weights_split = w_qkv.reshape(w_qkv.shape[0], 3, heads_loc, HD)
    projected_all = jnp.einsum(
        "td,dchf->chtf", tokens, weights_split, preferred_element_type=jnp.float32
    ).astype(jnp.bfloat16)
    rel_both = jnp.einsum(
        "rd,dchf->chrf", rel_table, weights_split[:, :2], preferred_element_type=jnp.float32
    ).astype(jnp.bfloat16)
    head_shape = (heads_loc, req_dev, QLEN, HD)
    query_four = projected_all[0].reshape(head_shape)
    keys_four = projected_all[1].reshape(head_shape)
    values_four = projected_all[2].reshape(head_shape)
    groups_all = gathered.shape[1] // PLEN
    cache_all = gathered.reshape(2, groups_all, PLEN, heads_loc, HD)
    picked = jnp.transpose(cache_all[:, group_ids], (0, 3, 1, 2, 4))
    keys = jnp.concatenate([keys_four, picked[0]], axis=2)
    values = jnp.concatenate([values_four, picked[1]], axis=2)
    pos_query = PLEN + jnp.arange(QLEN, dtype=jnp.int32)
    pos_key = jnp.concatenate([pos_query, jnp.arange(PLEN, dtype=jnp.int32)])
    index_one = pos_query[:, None] - pos_key[None, :] + half
    index_two = pos_key[:, None] - pos_query[None, :] + half
    rel_k_rows = rel_both[1][:, index_one]
    rel_q_rows = rel_both[0][:, index_two]
    c2p = jnp.einsum("hrqd,hqkd->hrqk", query_four, rel_k_rows, preferred_element_type=jnp.float32)
    p2c = jnp.einsum("hrkd,hkqd->hrqk", keys, rel_q_rows, preferred_element_type=jnp.float32)
    content = jnp.einsum("hrqd,hrkd->hrqk", query_four, keys, preferred_element_type=jnp.float32)
    logits = (content + c2p + p2c) / scale_root
    largest = jnp.max(logits, axis=-1, keepdims=True)
    weights = jnp.exp(logits - largest)
    denominator = jnp.sum(weights, axis=-1)
    summed = jnp.einsum(
        "hrqk,hrkd->hrqd", weights.astype(jnp.bfloat16), values, preferred_element_type=jnp.float32
    )
    attended = (summed / denominator[..., None]).astype(jnp.bfloat16)
    out_split = w_out.reshape(heads_loc, HD, w_out.shape[1])
    attn_part = jnp.einsum(
        "hrqd,hde->rqe", attended, out_split, preferred_element_type=jnp.float32
    ).reshape(rows_dev, w_out.shape[1])
    attn_total = lax.psum(attn_part.astype(jnp.bfloat16), "head").astype(jnp.float32)
    hidden_one = layer_norm(tokens.astype(jnp.float32) + attn_total, gain_one).astype(jnp.bfloat16)
    inner = jax.nn.gelu(
        jnp.dot(hidden_one, w_up, preferred_element_type=jnp.float32), approximate=False
    ).astype(jnp.bfloat16)
    ffn_total = lax.psum(
        jnp.dot(inner, w_down, preferred_element_type=jnp.float32).astype(jnp.bfloat16), "head"
    ).astype(jnp.float32)
    hidden_two = layer_norm(hidden_one.astype(jnp.float32) + ffn_total, gain_two).astype(
        jnp.bfloat16
    )
    projected = jnp.dot(hidden_two, w_proj, preferred_element_type=jnp.float32)
    query_vectors = (
        projected * lax.rsqrt(jnp.sum(projected * projected, axis=-1, keepdims=True) + 1e-06)
    ).astype(jnp.bfloat16)
    shards = lax.axis_size("doc")
    cand_dev = candidates.shape[1]
    pairs = req_dev * cand_dev
    capacity = max(2, 2 * pairs // shards)
    flat_cand = candidates.reshape(-1)
    holders = flat_cand // DOC_DEV
    request_of = jnp.arange(pairs, dtype=jnp.int32) // cand_dev
    slot_rank = slot_order(holders)
    copies, cand_copies = (
        lax.all_gather(query_vectors, "doc", axis=0, tiled=True),
        lax.all_gather(candidates, "doc", axis=0, tiled=True),
    )
    all_query = copies.reshape(shards, req_dev, QLEN, copies.shape[1])
    all_cand = cand_copies.reshape(shards, pairs)
    holder_all = all_cand // DOC_DEV
    local_all = all_cand % DOC_DEV
    rank_all = jax.vmap(slot_order)(holder_all)
    own_index = lax.axis_index("doc")
    chosen = (holder_all[:, None, :] == own_index) & (
        rank_all[:, None, :] == jnp.arange(capacity, dtype=jnp.int32)[None, :, None]
    )
    filled = jnp.any(chosen, axis=2)
    slot_request = jnp.sum(jnp.where(chosen, request_of[None, None, :], 0), axis=2)
    slot_doc = jnp.where(
        filled, jnp.sum(jnp.where(chosen, local_all[:, None, :], 0), axis=2), -1
    ).astype(jnp.int32)
    slot_query = all_query[jnp.arange(shards)[:, None], slot_request]
    slot_scores = rate_slots(slot_query, slot_doc, doc_vectors, doc_lengths)
    returned = lax.all_to_all(slot_scores, "doc", split_axis=0, concat_axis=0, tiled=True)
    scores = returned.reshape(-1)[holders * capacity + slot_rank].reshape(candidates.shape)
    return (query_vectors, scores)


LANES = 128
MIB = 1 << 20
EXTRA = 16
PREP_UNROLL = 12
ATT_UNROLL = 12
SCORE_UNROLL = 32


def full_specs(count):
    return [pl.BlockSpec(memory_space=pltpu.VMEM)] * count


def far(x):
    return pltpu.with_memory_space_constraint(x, pltpu.HBM)


def params(mib):
    return pltpu.CompilerParams(vmem_limit_bytes=mib * MIB)


def by_head(values):
    head_of = lax.broadcasted_iota(jnp.int32, values.shape, 1) // HD
    heads = values.shape[1] // HD
    zero = jnp.zeros_like(values)
    return jnp.concatenate([jnp.where(head_of == h, values, zero) for h in range(heads)], axis=0)


def times_rows(left, right):
    return lax.dot_general(left, right, (((1,), (1,)), ((), ())), preferred_element_type=jnp.float32)


def key_terms(key_rel, first):
    slot = lax.broadcasted_iota(jnp.int32, (key_rel.shape[0], LANES), 1) // QLEN
    turned = None
    for h in range(key_rel.shape[1] // LANES):
        shift = (LANES - PLEN - QLEN + first + h * QLEN) % LANES
        rolled = pltpu.roll(
            key_rel[:, h * LANES : (h + 1) * LANES], shift, 1, stride=1, stride_axis=0
        )
        turned = rolled if turned is None else jnp.where(slot == h, rolled, turned)
    return turned


def prepare_kernel(
    tokens_far, weight_far, rel_table, qkv, base, rel_q_heads, q_heads, query_rel, key_rel, *scratch
):
    tokens, weight, rel_rows, arrived = scratch
    rel_far = rel_table.at[pl.ds(RELS // 2 - PLEN - QLEN, rel_rows.shape[0])]
    copies = [pltpu.make_async_copy(tokens_far, tokens, arrived.at[0])]
    copies += [pltpu.make_async_copy(weight_far.at[i], weight.at[i], arrived.at[1 + i]) for i in range(3)]
    copies += [pltpu.make_async_copy(rel_far, rel_rows, arrived.at[4])]
    for copy in copies:
        copy.start()
    copies[0].wait()
    width = weight.shape[2]
    heads = width // HD
    for i in range(3):
        copies[1 + i].wait()
        qkv[:, i * width : (i + 1) * width] = jnp.dot(
            tokens[...], weight[i], preferred_element_type=jnp.float32
        ).astype(jnp.bfloat16)
    count = rel_rows.shape[0]
    copies[4].wait()
    rel = [
        jnp.dot(rel_rows[...], weight[i], preferred_element_type=jnp.float32).astype(jnp.bfloat16)
        for i in range(2)
    ]
    both = lax.broadcasted_iota(jnp.int32, (LANES, count), 0) + lax.broadcasted_iota(
        jnp.int32, (LANES, count), 1
    )
    flip_q = jnp.where(both == LANES, 1.0, 0.0).astype(jnp.bfloat16)
    flip_k = jnp.where(both == LANES + PLEN - 1, 1.0, 0.0).astype(jnp.bfloat16)
    rel_q = jnp.dot(flip_q, rel[0], preferred_element_type=jnp.float32)
    rel_k = jnp.dot(flip_k, rel[1], preferred_element_type=jnp.float32)
    rel_q_heads[...] = by_head(rel_q.astype(jnp.bfloat16))
    requests, _, many = base.shape
    for r in range(requests):
        q_heads[r * many : (r + 1) * many, :] = by_head(qkv[r * QLEN : (r + 1) * QLEN, :width])
    query_rel[...] = times_rows(q_heads[...], rel_k.astype(jnp.bfloat16))
    key_rel[...] = times_rows(qkv[:, width : 2 * width], rel_q_heads[...])
    scale = 1.0 / math.sqrt(3 * HD)

    def one_request(r, carry):
        rows = pl.ds(pl.multiple_of(r * QLEN, QLEN), QLEN)
        spread = pl.ds(pl.multiple_of(r * many, many), many)
        turned = times_rows(qkv[rows, width : 2 * width], q_heads[spread, :])
        turned = turned + key_terms(key_rel[rows, :], PLEN)
        spread_rel = query_rel[spread, :]
        c2p = jnp.concatenate(
            [
                pltpu.roll(
                    spread_rel[h * QLEN : (h + 1) * QLEN],
                    LANES - QLEN + 1,
                    1,
                    stride=1,
                    stride_axis=0,
                )
                for h in range(heads)
            ],
            axis=0,
        )
        c2p = c2p.T
        base[r, :PLEN] = c2p[:PLEN] * scale
        base[r, PLEN:] = (c2p[PLEN : PLEN + QLEN] + turned) * scale
        return carry

    lax.fori_loop(0, requests, one_request, 0, unroll=PREP_UNROLL)


def prepare(tokens, weight, rel_table):
    rows = tokens.shape[0]
    width = weight.shape[2]
    heads = width // HD
    return pl.pallas_call(
        prepare_kernel,
        out_shape=[
            jax.ShapeDtypeStruct((rows, 3 * width), jnp.bfloat16),
            jax.ShapeDtypeStruct((rows // QLEN, PLEN + QLEN, heads * QLEN), jnp.float32),
            jax.ShapeDtypeStruct((heads * LANES, width), jnp.bfloat16),
        ],
        in_specs=[pl.BlockSpec(memory_space=pltpu.HBM)] * 3,
        out_specs=full_specs(3),
        scratch_shapes=[
            pltpu.VMEM((rows * heads, width), jnp.bfloat16),
            pltpu.VMEM((rows * heads, LANES), jnp.float32),
            pltpu.VMEM((rows, heads * LANES), jnp.float32),
            pltpu.VMEM(tokens.shape, jnp.bfloat16),
            pltpu.VMEM(weight.shape, jnp.bfloat16),
            pltpu.VMEM((2 * (PLEN + QLEN), rel_table.shape[1]), jnp.bfloat16),
            pltpu.SemaphoreType.DMA((5,)),
        ],
        compiler_params=params(16),
        cost_estimate=pl.CostEstimate(flops=4000 * MIB, bytes_accessed=4 * MIB, transcendentals=0),
        name="prepare",
    )(far(tokens), far(weight), far(rel_table))


def attend_kernel(group_ids, qkv, base, rel_q_heads, columns, *rest):
    pieces, (att, cache, picked, key_rel, shares, arrived) = rest[:-6], rest[-6:]
    copies = [
        [
            pltpu.make_async_copy(piece.at[kind], cache.at[kind, at], arrived.at[kind, at])
            for at, piece in enumerate(pieces)
        ]
        for kind in range(2)
    ]
    for copy in copies[0] + copies[1]:
        copy.start()
    requests, _, _ = base.shape
    tokens = requests * QLEN
    ids = columns[...].T
    spare = jnp.zeros((1, LANES - columns.shape[0] * columns.shape[1]), jnp.int32)
    line = jnp.concatenate([ids[r : r + 1, :] for r in range(ids.shape[0])] + [spare], axis=1)
    line = jnp.concatenate([line // DOC_DEV, line % DOC_DEV], axis=1)
    extra = jnp.broadcast_to(line.astype(jnp.float32), (EXTRA, line.shape[1]))
    att[tokens:, :] = extra.astype(att.dtype)
    width = att.shape[1]
    heads = width // HD
    groups_dev = cache.shape[2] // PLEN
    me = lax.axis_index("doc")
    small_head = lax.broadcasted_iota(jnp.int32, (QLEN, width), 1) // HD
    scale = 1.0 / math.sqrt(3 * HD)

    def place_of(r):
        owner = group_ids[r] // groups_dev
        within = pl.multiple_of((group_ids[r] - owner * groups_dev) * PLEN, PLEN)
        return owner ^ me, pl.ds(within, PLEN)

    for copy in copies[0]:
        copy.wait()
    for r in range(requests):
        piece, within = place_of(r)
        picked[r * PLEN : (r + 1) * PLEN, :] = cache[0, piece, within, :]
    key_rel[...] = times_rows(picked[...], rel_q_heads[...])

    def one_softmax(r, carry):
        rows = pl.ds(pl.multiple_of(r * QLEN, QLEN), QLEN)
        cached = pl.ds(pl.multiple_of(r * PLEN, PLEN), PLEN)
        turned = times_rows(picked[cached, :], by_head(qkv[rows, 0:width]))
        turned = (turned + key_terms(key_rel[cached, :], 0)) * scale
        logits = jnp.concatenate([base[r, :PLEN] + turned, base[r, PLEN:]], axis=0)
        weights = jnp.exp(logits - jnp.max(logits, axis=0, keepdims=True))
        weights = weights * (1.0 / jnp.sum(weights, axis=0, keepdims=True))
        shares[r] = weights.astype(shares.dtype)
        return carry

    lax.fori_loop(0, requests, one_softmax, 0, unroll=ATT_UNROLL)
    for copy in copies[1]:
        copy.wait()

    def one_sum(r, carry):
        rows = pl.ds(pl.multiple_of(r * QLEN, QLEN), QLEN)
        piece, within = place_of(r)
        values = jnp.concatenate(
            [cache[1, piece, within, :], qkv[rows, 2 * width : 3 * width]], axis=0
        )
        summed = lax.dot_general(
            shares[r],
            values,
            (((0,), (0,)), ((), ())),
            preferred_element_type=jnp.float32,
        )
        out = summed[:QLEN]
        for h in range(1, heads):
            out = jnp.where(small_head == h, summed[h * QLEN : (h + 1) * QLEN], out)
        att[rows, :] = out.astype(jnp.bfloat16)
        return carry

    lax.fori_loop(0, requests, one_sum, 0, unroll=ATT_UNROLL)


def attend(group_ids, qkv, base, rel_q_heads, columns, pieces):
    rows = qkv.shape[0]
    width = qkv.shape[1] // 3
    cached = rows // QLEN * PLEN
    return pl.pallas_call(
        attend_kernel,
        out_shape=jax.ShapeDtypeStruct((rows + EXTRA, width), jnp.bfloat16),
        in_specs=[pl.BlockSpec(memory_space=pltpu.SMEM)]
        + full_specs(4)
        + [pl.BlockSpec(memory_space=pl.ANY)] * len(pieces),
        out_specs=pl.BlockSpec(memory_space=pltpu.VMEM),
        scratch_shapes=[
            pltpu.VMEM((2, len(pieces)) + pieces[0].shape[1:], jnp.bfloat16),
            pltpu.VMEM((cached, width), jnp.bfloat16),
            pltpu.VMEM((cached, rel_q_heads.shape[0]), jnp.float32),
            pltpu.VMEM(base.shape, jnp.bfloat16),
            pltpu.SemaphoreType.DMA((2, len(pieces))),
        ],
        compiler_params=params(12),
        cost_estimate=pl.CostEstimate(flops=2000 * MIB, bytes_accessed=2 * MIB, transcendentals=0),
        name="attend",
    )(group_ids, qkv, base, rel_q_heads, columns, *pieces)


def norm_rows(values, gain):
    centre = values - jnp.mean(values, axis=-1, keepdims=True)
    spread = jnp.mean(centre * centre, axis=-1, keepdims=True)
    return centre * lax.rsqrt(spread + 1e-07) * gain


def feed_rows(start, count, a, w, tokens, gain, w_up, w_down):
    rows = pl.ds(pl.multiple_of(start, 32), count)
    mixed = tokens[rows, :].astype(jnp.float32)
    for piece, weight in zip(a, w):
        mixed = mixed + jnp.dot(piece[rows, :], weight[...], preferred_element_type=jnp.float32)
    hidden = norm_rows(mixed, gain[...]).astype(jnp.bfloat16)
    up = jnp.dot(hidden, w_up[...], preferred_element_type=jnp.float32)
    inner = (0.5 * up * (1.0 + lax.erf(up * math.sqrt(0.5)))).astype(jnp.bfloat16)
    total = jnp.dot(inner, w_down[...], preferred_element_type=jnp.float32)
    return hidden, total


def feed_other_kernel(a0, a1, a2, a3, w0, w1, w2, w3, tokens, gain, w_up, w_down, out):
    core = lax.axis_index("head") % 2
    _, total = feed_rows(
        (1 - core) * out.shape[0], out.shape[0], (a0, a1, a2, a3), (w0, w1, w2, w3), tokens, gain, w_up, w_down
    )
    out[...] = total.astype(out.dtype)


def feed_own_kernel(a0, a1, a2, a3, w0, w1, w2, w3, tokens, gain, w_up, w_down, out, own):
    pieces, weights = (a0, a1, a2, a3), (w0, w1, w2, w3)
    count = out.shape[0]
    place = lax.axis_index("head")
    start = place % 2 * (2 * count)
    hidden, total = feed_rows(start, 2 * count, pieces, weights, tokens, gain, w_up, w_down)

    @pl.when(place // 2 == 0)
    def first():
        out[...] = total[count:]
        own[...] = hidden[:count].astype(jnp.float32) + total[:count]

    @pl.when(place // 2 != 0)
    def second():
        out[...] = total[:count]
        own[...] = hidden[count:].astype(jnp.float32) + total[count:]


def feed(kernel, pieces, weights, tokens, gain, w_up, w_down, outs, name):
    return pl.pallas_call(
        kernel,
        out_shape=outs,
        in_specs=full_specs(12),
        out_specs=full_specs(len(outs)),
        compiler_params=params(20),
        cost_estimate=pl.CostEstimate(flops=1600 * MIB, bytes_accessed=6 * MIB, transcendentals=0),
        name=name,
    )(*pieces, *weights, tokens, gain, w_up, w_down)


def fold_kernel(for_y, from_core, out):
    count = out.shape[0]
    other = 1 - lax.axis_index("head") // 2
    rows = pl.ds(pl.multiple_of(other * count, 32), count)
    out[...] = (for_y[...] + from_core[rows, :].astype(jnp.float32)).astype(out.dtype)


def block_of(head):
    return head % 2 * 2 + head // 2


def project_kernel(own, from_core, from_y, gain, w_proj, a0, a1, a2, a3, out, single):
    count = own.shape[0]
    place = lax.axis_index("head")
    rows = pl.ds(pl.multiple_of(place // 2 * count, 32), count)
    after = own[...] + from_core[rows, :].astype(jnp.float32) + from_y[...].astype(jnp.float32)
    hidden = norm_rows(after, gain[...]).astype(jnp.bfloat16)
    projected = jnp.dot(hidden, w_proj[...], preferred_element_type=jnp.float32)
    length = jnp.sum(projected * projected, axis=-1, keepdims=True)
    vectors = (projected * lax.rsqrt(length + 1e-06)).astype(jnp.bfloat16)
    single[...] = vectors
    pieces = (a0, a1, a2, a3)
    part = LANES // len(pieces) * 3 // 4
    lane = lax.broadcasted_iota(jnp.int32, (EXTRA, LANES), 1)
    lines = []
    for kind in range(2):
        line = jnp.zeros((EXTRA, LANES), jnp.float32)
        for x, piece in enumerate(pieces):
            from_head = place ^ x
            values = piece[piece.shape[0] - EXTRA :, kind * LANES : (kind + 1) * LANES]
            shift = lax.rem((from_head - block_of(place)) * part + LANES, LANES)
            rolled = pltpu.roll(values.astype(jnp.float32), shift, 1)
            line = jnp.where(lane // part == from_head, rolled, line)
        lines.append(line)
    which = lax.broadcasted_iota(jnp.int32, (EXTRA, LANES), 0)
    tail = jnp.where(which == 0, lines[0], lines[1]).astype(out.dtype)
    for o in range(out.shape[0]):
        out[o, :count] = vectors
        out[o, count:] = tail


def list_slots(queries, n_doc, listed):
    rows = queries.shape[0] // n_doc
    part = (rows - EXTRA) // QLEN * 8
    me = lax.axis_index("doc")
    shape = (n_doc, LANES)
    lane = lax.broadcasted_iota(jnp.int32, shape, 1)
    row = lax.broadcasted_iota(jnp.int32, shape, 0)
    tails = [
        queries[o * rows + rows - EXTRA : (o + 1) * rows, :].astype(jnp.float32) for o in range(n_doc)
    ]
    holder = jnp.concatenate([tail[:1] for tail in tails], axis=0).astype(jnp.int32)
    doc = jnp.concatenate([tail[1:2] for tail in tails], axis=0).astype(jnp.int32)
    mine = (lane < 4 * part) & (holder == me)
    group = (row * rows + lane % part // 8 * QLEN) // 16
    listed[n_doc : 2 * n_doc, :] = group | (doc << 8)
    ones = jnp.where(mine, 1.0, 0.0)
    until = lax.broadcasted_iota(jnp.int32, (LANES, LANES), 0) <= lax.broadcasted_iota(
        jnp.int32, (LANES, LANES), 1
    )
    until = jnp.where(until, 1.0, 0.0).astype(jnp.bfloat16)
    reached = jnp.dot(ones.astype(jnp.bfloat16), until, preferred_element_type=jnp.float32)
    in_row = jnp.sum(ones, axis=1, keepdims=True)
    above = jnp.zeros((1, 1), jnp.float32)
    starts = []
    for o in range(n_doc):
        starts.append(above)
        above = above + in_row[o : o + 1]
    reached = (reached + jnp.concatenate(starts, axis=0)).astype(jnp.int32)
    pad = jnp.zeros((LANES - n_doc, LANES), jnp.int32)
    columns = jnp.concatenate([reached, pad], axis=0).T
    square_lane = lax.broadcasted_iota(jnp.int32, (LANES, LANES), 1)
    blocks = (jnp.sum(ones).astype(jnp.int32) + LANES - 1) // LANES

    def one_block(block, carry):
        total = jnp.zeros((LANES, LANES), jnp.int32)
        for o in range(n_doc):
            passed = columns[:, o : o + 1] <= square_lane + block * LANES
            total = total + jnp.where(passed, 1, 0)
        listed[pl.ds(block, 1), :] = jnp.sum(total, axis=0, keepdims=True)
        return carry

    lax.fori_loop(0, blocks, one_block, 0)
    listed[n_doc - 1 : n_doc, :] = jnp.broadcast_to(above.astype(jnp.int32), (1, LANES))


def score_kernel(lengths, queries, docs, out, held, listed, slots, arrived, ready):
    chunks = arrived.shape[0]
    per = docs.shape[0] // chunks
    copies = [
        pltpu.make_async_copy(
            docs.at[pl.ds(c * per, per)], held.at[pl.ds(c * per, per)], arrived.at[c]
        )
        for c in range(chunks)
    ]
    for copy in copies:
        copy.start()
    list_slots(queries, out.shape[0], listed)
    to_scalars = pltpu.make_async_copy(listed, slots, ready)
    to_scalars.start()
    to_scalars.wait()
    for copy in copies:
        copy.wait()

    shape = (8, LANES)
    flat = lax.broadcasted_iota(jnp.int32, shape, 0) * LANES + lax.broadcasted_iota(jnp.int32, shape, 1)
    unroll = SCORE_UNROLL
    zero = jnp.zeros((QLEN, docs.shape[2]), jnp.bfloat16)
    position = lax.broadcasted_iota(jnp.int32, (docs.shape[1], 2 * QLEN), 0)
    side = lax.broadcasted_iota(jnp.int32, (1, 2 * QLEN), 1) < QLEN
    tables = out.shape[0]
    count = slots[tables - 1, 0]

    def some(i, totals):
        for u in range(0, unroll, 2):
            left, right, marks, limits = [], [], [], []
            for v in range(2):
                s = i * unroll + u + v
                used = s < count
                entry = jnp.where(used, slots[s >> 7, s & 127], 0)
                found = slots[tables + (entry >> 7), entry & 127]
                query = queries[pl.ds(pl.multiple_of((found & 255) * 16, 16), QLEN), :]
                doc = found >> 8
                left.append(jnp.concatenate([query, zero] if v == 0 else [zero, query], axis=1))
                right.append(held[doc])
                marks.append(jnp.where(used, entry, -1))
                limits.append(lengths[doc])
            sims = times_rows(jnp.concatenate(right, axis=1), jnp.concatenate(left, axis=0))
            limit = jnp.where(side, limits[0], limits[1])
            best = jnp.max(jnp.where(position < limit, sims, -jnp.inf), axis=0, keepdims=True)
            for v in range(2):
                total = jnp.sum(jnp.where(side if v == 0 else ~side, best, 0.0), axis=1, keepdims=True)
                totals = jnp.where(flat == marks[v], total, totals)
        return totals

    totals = lax.fori_loop(
        0, (count + unroll - 1) // unroll, some, jnp.zeros(shape, jnp.float32)
    )
    for o in range(out.shape[0]):
        row = jnp.broadcast_to(totals[o : o + 1], shape)
        for h in range(out.shape[1]):
            out[o, h] = row


def arrange_kernel(*refs):
    shares, out = refs[:-1], refs[-1]
    place = lax.axis_index("head")
    for k, share in enumerate(shares):
        count = share.shape[0]
        out[pl.ds(pl.multiple_of(block_of(place ^ k) * count, 32), count), :] = share[...]


def collect_kernel(tiles, out):
    n_head = tiles.shape[1]
    cols, reqs_all = out.shape
    reqs = reqs_all // n_head
    place = lax.axis_index("head")
    lines = []
    for h in range(n_head):
        total = tiles[0, h]
        for o in range(1, tiles.shape[0]):
            total = total + tiles[o, h]
        total = pltpu.roll(total, LANES - place * (reqs * cols), 1)
        lines.append(total[:1, : reqs * cols])
    order = sorted(range(n_head), key=block_of)
    rows = [lines[h][:, r * cols : (r + 1) * cols] for h in order for r in range(reqs)]
    out[...] = jnp.concatenate(rows, axis=0).T


def body(
    tokens,
    w_qkv,
    w_out,
    w_up,
    w_down,
    gain_one,
    gain_two,
    rel_table,
    prompt_cache,
    w_proj,
    doc_vectors,
    doc_lengths,
    group_ids,
    candidates,
):
    rows, depth = tokens.shape
    n_doc = lax.axis_size("doc")
    n_head = lax.axis_size("head")
    half, quarter = rows // 2, rows // n_head
    cand_rows, cols = candidates.shape
    reqs = cand_rows // n_head
    smem = pl.BlockSpec(memory_space=pltpu.SMEM)

    def over_doc(x, k):
        return lax.ppermute(x, "doc", [(i, i ^ k) for i in range(n_doc)])

    def over_head(x, k):
        return lax.ppermute(x, "head", [(i, i ^ k) for i in range(n_head)])

    tile = (8, LANES)
    pieces = {k: over_doc(prompt_cache, k) for k in (6, 5, 4, 3, 1, 2)}
    pieces[0] = prompt_cache
    pieces[6], rel_table = lax.optimization_barrier((pieces[6], rel_table))
    pieces[7] = over_doc(pieces[6], 1)
    pieces = [pieces[k] for k in range(n_doc)]
    weight = jnp.transpose(w_qkv, (1, 0, 2))
    qkv, base, rel_q_heads = prepare(tokens, weight, rel_table)

    out_one = over_head(w_out, 2)
    out_pieces = [w_out, over_head(w_out, 1), out_one, over_head(out_one, 1)]

    att = attend(group_ids, qkv, base, rel_q_heads, candidates.T, pieces)
    att_y = over_head(att, 2)
    att_pieces = [att, over_head(att, 1), att_y, over_head(att_y, 1)]

    common = (att_pieces, out_pieces, tokens, gain_one.reshape(1, -1), w_up, w_down)
    other = feed(
        feed_other_kernel,
        *common,
        [jax.ShapeDtypeStruct((half, depth), jnp.bfloat16)],
        "feed_other",
    )[0]
    from_core = over_head(other, 1)
    for_y, own = feed(
        feed_own_kernel,
        *common,
        [jax.ShapeDtypeStruct((quarter, depth), jnp.float32)] * 2,
        "feed_own",
    )
    folded = pl.pallas_call(
        fold_kernel,
        out_shape=jax.ShapeDtypeStruct((quarter, depth), jnp.bfloat16),
        in_specs=full_specs(2),
        out_specs=full_specs(1)[0],
        compiler_params=params(4),
        name="fold",
    )(for_y, from_core)
    from_y = over_head(folded, 2)

    emb = w_proj.shape[1]
    vectors, single = pl.pallas_call(
        project_kernel,
        out_shape=[
            jax.ShapeDtypeStruct((n_doc, quarter + EXTRA, emb), jnp.bfloat16),
            jax.ShapeDtypeStruct((quarter, emb), jnp.bfloat16),
        ],
        in_specs=full_specs(9),
        out_specs=full_specs(2),
        compiler_params=params(8),
        name="project",
    )(own, from_core, from_y, gain_two.reshape(1, -1), w_proj, *att_pieces)
    queries = lax.all_to_all(vectors, "doc", 0, 0, tiled=True).reshape(-1, emb)

    rated = pl.pallas_call(
        score_kernel,
        out_shape=jax.ShapeDtypeStruct((n_doc, n_head) + tile, jnp.float32),
        in_specs=[smem] + full_specs(1) + [pl.BlockSpec(memory_space=pltpu.HBM)],
        out_specs=full_specs(1)[0],
        scratch_shapes=[
            pltpu.VMEM(doc_vectors.shape, jnp.bfloat16),
            pltpu.VMEM((2 * n_doc, LANES), jnp.int32),
            pltpu.SMEM((2 * n_doc, LANES), jnp.int32),
            pltpu.SemaphoreType.DMA((8,)),
            pltpu.SemaphoreType.DMA,
        ],
        compiler_params=params(16),
        name="rate",
    )(doc_lengths, queries, far(doc_vectors))
    back = lax.all_to_all(rated.reshape(-1, LANES), ("doc", "head"), 0, 0, tiled=True)

    single, _ = lax.optimization_barrier((single, rated))
    shares = [single] + [over_head(single, k) for k in range(1, n_head)]
    query_vectors = pl.pallas_call(
        arrange_kernel,
        out_shape=jax.ShapeDtypeStruct((rows, emb), jnp.bfloat16),
        in_specs=full_specs(n_head),
        out_specs=full_specs(1)[0],
        compiler_params=params(4),
        name="arrange",
    )(*shares)

    scores = pl.pallas_call(
        collect_kernel,
        out_shape=jax.ShapeDtypeStruct((cols, cand_rows), jnp.float32),
        in_specs=full_specs(1),
        out_specs=full_specs(1)[0],
        compiler_params=params(4),
        name="collect",
    )(back.reshape((n_doc, n_head) + tile))
    return (query_vectors, scores.T)


def solution(mesh):
    placed = (
        P("doc", None),
        P(None, None, "head"),
        P("head", None),
        P(None, "head"),
        P("head", None),
        P(),
        P(),
        P(),
        P(None, "doc", "head"),
        P(),
        P("doc", None, None),
        P("doc"),
        P("doc"),
        P("doc", "head"),
    )
    fits = mesh.shape["head"] == 4 and mesh.shape["doc"] == 8
    return jax.shard_map(
        body if fits else body_any,
        mesh=mesh,
        in_specs=placed,
        out_specs=(P("doc", None), P("doc", "head")),
        check_vma=False,
    )
```

```python
import functools
import math

import jax
import jax.numpy as jnp
from jax import lax
from jax.experimental import pallas as pl
from jax.experimental.pallas import tpu as pltpu
from jax.sharding import PartitionSpec as P

HD = 64
RELS = 512
QLEN = 32
PLEN = 64
DOC_DEV = 64


def layer_norm(values, gain):
    centre = values - jnp.mean(values, axis=-1, keepdims=True)
    spread = jnp.mean(centre * centre, axis=-1, keepdims=True)
    return centre * lax.rsqrt(spread + 1e-07) * gain


def slot_order(holders):
    count = holders.shape[0]
    same = holders[:, None] == holders[None, :]
    earlier = jnp.arange(count)[:, None] > jnp.arange(count)[None, :]
    return jnp.sum(same & earlier, axis=1)


def rate_slots(slot_query, slot_doc, doc_vectors, doc_lengths):
    shape = slot_doc.shape
    flat_doc = slot_doc.reshape(-1)
    flat_query = slot_query.reshape((flat_doc.shape[0],) + slot_query.shape[-2:])
    safe_doc = jnp.maximum(flat_doc, 0)
    documents = doc_vectors[safe_doc]
    lengths = doc_lengths[safe_doc]
    sims = jnp.einsum("sqe,sje->sqj", flat_query, documents, preferred_element_type=jnp.float32)
    live = jnp.arange(documents.shape[1], dtype=jnp.int32)[None, None, :] < lengths[:, None, None]
    best = jnp.max(jnp.where(live, sims, -jnp.inf), axis=2)
    totals = jnp.where(flat_doc >= 0, jnp.sum(best, axis=1), 0.0)
    return totals.reshape(shape)


def body_any(
    tokens,
    w_qkv,
    w_out,
    w_up,
    w_down,
    gain_one,
    gain_two,
    rel_table,
    prompt_cache,
    w_proj,
    doc_vectors,
    doc_lengths,
    group_ids,
    candidates,
):
    rows_dev = tokens.shape[0]
    req_dev = rows_dev // QLEN
    width = w_qkv.shape[2]
    heads_loc = width // HD
    half = RELS // 2
    scale_root = math.sqrt(3 * HD)
    gathered = lax.all_gather(prompt_cache, "doc", axis=1, tiled=True)
    weights_split = w_qkv.reshape(w_qkv.shape[0], 3, heads_loc, HD)
    projected_all = jnp.einsum(
        "td,dchf->chtf", tokens, weights_split, preferred_element_type=jnp.float32
    ).astype(jnp.bfloat16)
    rel_both = jnp.einsum(
        "rd,dchf->chrf", rel_table, weights_split[:, :2], preferred_element_type=jnp.float32
    ).astype(jnp.bfloat16)
    head_shape = (heads_loc, req_dev, QLEN, HD)
    query_four = projected_all[0].reshape(head_shape)
    keys_four = projected_all[1].reshape(head_shape)
    values_four = projected_all[2].reshape(head_shape)
    groups_all = gathered.shape[1] // PLEN
    cache_all = gathered.reshape(2, groups_all, PLEN, heads_loc, HD)
    picked = jnp.transpose(cache_all[:, group_ids], (0, 3, 1, 2, 4))
    keys = jnp.concatenate([keys_four, picked[0]], axis=2)
    values = jnp.concatenate([values_four, picked[1]], axis=2)
    pos_query = PLEN + jnp.arange(QLEN, dtype=jnp.int32)
    pos_key = jnp.concatenate([pos_query, jnp.arange(PLEN, dtype=jnp.int32)])
    index_one = pos_query[:, None] - pos_key[None, :] + half
    index_two = pos_key[:, None] - pos_query[None, :] + half
    rel_k_rows = rel_both[1][:, index_one]
    rel_q_rows = rel_both[0][:, index_two]
    c2p = jnp.einsum("hrqd,hqkd->hrqk", query_four, rel_k_rows, preferred_element_type=jnp.float32)
    p2c = jnp.einsum("hrkd,hkqd->hrqk", keys, rel_q_rows, preferred_element_type=jnp.float32)
    content = jnp.einsum("hrqd,hrkd->hrqk", query_four, keys, preferred_element_type=jnp.float32)
    logits = (content + c2p + p2c) / scale_root
    largest = jnp.max(logits, axis=-1, keepdims=True)
    weights = jnp.exp(logits - largest)
    denominator = jnp.sum(weights, axis=-1)
    summed = jnp.einsum(
        "hrqk,hrkd->hrqd", weights.astype(jnp.bfloat16), values, preferred_element_type=jnp.float32
    )
    attended = (summed / denominator[..., None]).astype(jnp.bfloat16)
    out_split = w_out.reshape(heads_loc, HD, w_out.shape[1])
    attn_part = jnp.einsum(
        "hrqd,hde->rqe", attended, out_split, preferred_element_type=jnp.float32
    ).reshape(rows_dev, w_out.shape[1])
    attn_total = lax.psum(attn_part.astype(jnp.bfloat16), "head").astype(jnp.float32)
    hidden_one = layer_norm(tokens.astype(jnp.float32) + attn_total, gain_one).astype(jnp.bfloat16)
    inner = jax.nn.gelu(
        jnp.dot(hidden_one, w_up, preferred_element_type=jnp.float32), approximate=False
    ).astype(jnp.bfloat16)
    ffn_total = lax.psum(
        jnp.dot(inner, w_down, preferred_element_type=jnp.float32).astype(jnp.bfloat16), "head"
    ).astype(jnp.float32)
    hidden_two = layer_norm(hidden_one.astype(jnp.float32) + ffn_total, gain_two).astype(
        jnp.bfloat16
    )
    projected = jnp.dot(hidden_two, w_proj, preferred_element_type=jnp.float32)
    query_vectors = (
        projected * lax.rsqrt(jnp.sum(projected * projected, axis=-1, keepdims=True) + 1e-06)
    ).astype(jnp.bfloat16)
    shards = lax.axis_size("doc")
    cand_dev = candidates.shape[1]
    pairs = req_dev * cand_dev
    capacity = max(2, 2 * pairs // shards)
    flat_cand = candidates.reshape(-1)
    holders = flat_cand // DOC_DEV
    request_of = jnp.arange(pairs, dtype=jnp.int32) // cand_dev
    slot_rank = slot_order(holders)
    copies, cand_copies = (
        lax.all_gather(query_vectors, "doc", axis=0, tiled=True),
        lax.all_gather(candidates, "doc", axis=0, tiled=True),
    )
    all_query = copies.reshape(shards, req_dev, QLEN, copies.shape[1])
    all_cand = cand_copies.reshape(shards, pairs)
    holder_all = all_cand // DOC_DEV
    local_all = all_cand % DOC_DEV
    rank_all = jax.vmap(slot_order)(holder_all)
    own_index = lax.axis_index("doc")
    chosen = (holder_all[:, None, :] == own_index) & (
        rank_all[:, None, :] == jnp.arange(capacity, dtype=jnp.int32)[None, :, None]
    )
    filled = jnp.any(chosen, axis=2)
    slot_request = jnp.sum(jnp.where(chosen, request_of[None, None, :], 0), axis=2)
    slot_doc = jnp.where(
        filled, jnp.sum(jnp.where(chosen, local_all[:, None, :], 0), axis=2), -1
    ).astype(jnp.int32)
    slot_query = all_query[jnp.arange(shards)[:, None], slot_request]
    slot_scores = rate_slots(slot_query, slot_doc, doc_vectors, doc_lengths)
    returned = lax.all_to_all(slot_scores, "doc", split_axis=0, concat_axis=0, tiled=True)
    scores = returned.reshape(-1)[holders * capacity + slot_rank].reshape(candidates.shape)
    return (query_vectors, scores)


LANES = 128
MIB = 1 << 20
EXTRA = 16
PREP_UNROLL = 12
ATT_UNROLL = 12
SCORE_UNROLL = 32


def full_specs(count):
    return [pl.BlockSpec(memory_space=pltpu.VMEM)] * count


def far(x):
    return pltpu.with_memory_space_constraint(x, pltpu.HBM)


def params(mib):
    return pltpu.CompilerParams(vmem_limit_bytes=mib * MIB)


def by_head(values):
    head_of = lax.broadcasted_iota(jnp.int32, values.shape, 1) // HD
    heads = values.shape[1] // HD
    zero = jnp.zeros_like(values)
    return jnp.concatenate([jnp.where(head_of == h, values, zero) for h in range(heads)], axis=0)


def times_rows(left, right):
    return lax.dot_general(left, right, (((1,), (1,)), ((), ())), preferred_element_type=jnp.float32)


def key_terms(key_rel, first):
    slot = lax.broadcasted_iota(jnp.int32, (key_rel.shape[0], LANES), 1) // QLEN
    turned = None
    for h in range(key_rel.shape[1] // LANES):
        shift = (LANES - PLEN - QLEN + first + h * QLEN) % LANES
        rolled = pltpu.roll(
            key_rel[:, h * LANES : (h + 1) * LANES], shift, 1, stride=1, stride_axis=0
        )
        turned = rolled if turned is None else jnp.where(slot == h, rolled, turned)
    return turned


def prepare_kernel(
    tokens_far, weight_far, rel_table, qkv, base, rel_q_heads, q_heads, query_rel, key_rel, *scratch
):
    tokens, weight, rel_rows, arrived = scratch
    rel_far = rel_table.at[pl.ds(RELS // 2 - PLEN - QLEN, rel_rows.shape[0])]
    copies = [pltpu.make_async_copy(tokens_far, tokens, arrived.at[0])]
    copies += [pltpu.make_async_copy(weight_far.at[i], weight.at[i], arrived.at[1 + i]) for i in range(3)]
    copies += [pltpu.make_async_copy(rel_far, rel_rows, arrived.at[4])]
    for copy in copies:
        copy.start()
    copies[0].wait()
    width = weight.shape[2]
    heads = width // HD
    for i in range(3):
        copies[1 + i].wait()
        qkv[:, i * width : (i + 1) * width] = jnp.dot(
            tokens[...], weight[i], preferred_element_type=jnp.float32
        ).astype(jnp.bfloat16)
    count = rel_rows.shape[0]
    copies[4].wait()
    rel = [
        jnp.dot(rel_rows[...], weight[i], preferred_element_type=jnp.float32).astype(jnp.bfloat16)
        for i in range(2)
    ]
    both = lax.broadcasted_iota(jnp.int32, (LANES, count), 0) + lax.broadcasted_iota(
        jnp.int32, (LANES, count), 1
    )
    flip_q = jnp.where(both == LANES, 1.0, 0.0).astype(jnp.bfloat16)
    flip_k = jnp.where(both == LANES + PLEN - 1, 1.0, 0.0).astype(jnp.bfloat16)
    rel_q = jnp.dot(flip_q, rel[0], preferred_element_type=jnp.float32)
    rel_k = jnp.dot(flip_k, rel[1], preferred_element_type=jnp.float32)
    rel_q_heads[...] = by_head(rel_q.astype(jnp.bfloat16))
    requests, _, many = base.shape
    for r in range(requests):
        q_heads[r * many : (r + 1) * many, :] = by_head(qkv[r * QLEN : (r + 1) * QLEN, :width])
    query_rel[...] = times_rows(q_heads[...], rel_k.astype(jnp.bfloat16))
    key_rel[...] = times_rows(qkv[:, width : 2 * width], rel_q_heads[...])
    scale = 1.0 / math.sqrt(3 * HD)

    def one_request(r, carry):
        rows = pl.ds(pl.multiple_of(r * QLEN, QLEN), QLEN)
        spread = pl.ds(pl.multiple_of(r * many, many), many)
        turned = times_rows(qkv[rows, width : 2 * width], q_heads[spread, :])
        turned = turned + key_terms(key_rel[rows, :], PLEN)
        spread_rel = query_rel[spread, :]
        c2p = jnp.concatenate(
            [
                pltpu.roll(
                    spread_rel[h * QLEN : (h + 1) * QLEN],
                    LANES - QLEN + 1,
                    1,
                    stride=1,
                    stride_axis=0,
                )
                for h in range(heads)
            ],
            axis=0,
        )
        c2p = c2p.T
        base[r, :PLEN] = c2p[:PLEN] * scale
        base[r, PLEN:] = (c2p[PLEN : PLEN + QLEN] + turned) * scale
        return carry

    lax.fori_loop(0, requests, one_request, 0, unroll=PREP_UNROLL)


def prepare(tokens, weight, rel_table):
    rows = tokens.shape[0]
    width = weight.shape[2]
    heads = width // HD
    return pl.pallas_call(
        prepare_kernel,
        out_shape=[
            jax.ShapeDtypeStruct((rows, 3 * width), jnp.bfloat16),
            jax.ShapeDtypeStruct((rows // QLEN, PLEN + QLEN, heads * QLEN), jnp.float32),
            jax.ShapeDtypeStruct((heads * LANES, width), jnp.bfloat16),
        ],
        in_specs=[pl.BlockSpec(memory_space=pltpu.HBM)] * 3,
        out_specs=full_specs(3),
        scratch_shapes=[
            pltpu.VMEM((rows * heads, width), jnp.bfloat16),
            pltpu.VMEM((rows * heads, LANES), jnp.float32),
            pltpu.VMEM((rows, heads * LANES), jnp.float32),
            pltpu.VMEM(tokens.shape, jnp.bfloat16),
            pltpu.VMEM(weight.shape, jnp.bfloat16),
            pltpu.VMEM((2 * (PLEN + QLEN), rel_table.shape[1]), jnp.bfloat16),
            pltpu.SemaphoreType.DMA((5,)),
        ],
        compiler_params=params(16),
        cost_estimate=pl.CostEstimate(flops=4000 * MIB, bytes_accessed=4 * MIB, transcendentals=0),
        name="prepare",
    )(far(tokens), far(weight), far(rel_table))


def attend_kernel(group_ids, qkv, base, rel_q_heads, columns, *rest):
    pieces, (att, cache, picked, key_rel, shares, arrived) = rest[:-6], rest[-6:]
    copies = [
        [
            pltpu.make_async_copy(piece.at[kind], cache.at[kind, at], arrived.at[kind, at])
            for at, piece in enumerate(pieces)
        ]
        for kind in range(2)
    ]
    for copy in copies[0] + copies[1]:
        copy.start()
    requests, _, _ = base.shape
    tokens = requests * QLEN
    ids = columns[...].T
    spare = jnp.zeros((1, LANES - columns.shape[0] * columns.shape[1]), jnp.int32)
    line = jnp.concatenate([ids[r : r + 1, :] for r in range(ids.shape[0])] + [spare], axis=1)
    line = jnp.concatenate([line // DOC_DEV, line % DOC_DEV], axis=1)
    extra = jnp.broadcast_to(line.astype(jnp.float32), (EXTRA, line.shape[1]))
    att[tokens:, :] = extra.astype(att.dtype)
    width = att.shape[1]
    heads = width // HD
    groups_dev = cache.shape[2] // PLEN
    me = lax.axis_index("doc")
    small_head = lax.broadcasted_iota(jnp.int32, (QLEN, width), 1) // HD
    scale = 1.0 / math.sqrt(3 * HD)

    def place_of(r):
        owner = group_ids[r] // groups_dev
        within = pl.multiple_of((group_ids[r] - owner * groups_dev) * PLEN, PLEN)
        return owner ^ me, pl.ds(within, PLEN)

    for copy in copies[0]:
        copy.wait()
    for r in range(requests):
        piece, within = place_of(r)
        picked[r * PLEN : (r + 1) * PLEN, :] = cache[0, piece, within, :]
    key_rel[...] = times_rows(picked[...], rel_q_heads[...])

    def one_softmax(r, carry):
        rows = pl.ds(pl.multiple_of(r * QLEN, QLEN), QLEN)
        cached = pl.ds(pl.multiple_of(r * PLEN, PLEN), PLEN)
        turned = times_rows(picked[cached, :], by_head(qkv[rows, 0:width]))
        turned = (turned + key_terms(key_rel[cached, :], 0)) * scale
        logits = jnp.concatenate([base[r, :PLEN] + turned, base[r, PLEN:]], axis=0)
        weights = jnp.exp(logits - jnp.max(logits, axis=0, keepdims=True))
        weights = weights * (1.0 / jnp.sum(weights, axis=0, keepdims=True))
        shares[r] = weights.astype(shares.dtype)
        return carry

    lax.fori_loop(0, requests, one_softmax, 0, unroll=ATT_UNROLL)
    for copy in copies[1]:
        copy.wait()

    def one_sum(r, carry):
        rows = pl.ds(pl.multiple_of(r * QLEN, QLEN), QLEN)
        piece, within = place_of(r)
        values = jnp.concatenate(
            [cache[1, piece, within, :], qkv[rows, 2 * width : 3 * width]], axis=0
        )
        summed = lax.dot_general(
            shares[r],
            values,
            (((0,), (0,)), ((), ())),
            preferred_element_type=jnp.float32,
        )
        out = summed[:QLEN]
        for h in range(1, heads):
            out = jnp.where(small_head == h, summed[h * QLEN : (h + 1) * QLEN], out)
        att[rows, :] = out.astype(jnp.bfloat16)
        return carry

    lax.fori_loop(0, requests, one_sum, 0, unroll=ATT_UNROLL)


def attend(group_ids, qkv, base, rel_q_heads, columns, pieces):
    rows = qkv.shape[0]
    width = qkv.shape[1] // 3
    cached = rows // QLEN * PLEN
    return pl.pallas_call(
        attend_kernel,
        out_shape=jax.ShapeDtypeStruct((rows + EXTRA, width), jnp.bfloat16),
        in_specs=[pl.BlockSpec(memory_space=pltpu.SMEM)]
        + full_specs(4)
        + [pl.BlockSpec(memory_space=pl.ANY)] * len(pieces),
        out_specs=pl.BlockSpec(memory_space=pltpu.VMEM),
        scratch_shapes=[
            pltpu.VMEM((2, len(pieces)) + pieces[0].shape[1:], jnp.bfloat16),
            pltpu.VMEM((cached, width), jnp.bfloat16),
            pltpu.VMEM((cached, rel_q_heads.shape[0]), jnp.float32),
            pltpu.VMEM(base.shape, jnp.bfloat16),
            pltpu.SemaphoreType.DMA((2, len(pieces))),
        ],
        compiler_params=params(12),
        cost_estimate=pl.CostEstimate(flops=2000 * MIB, bytes_accessed=2 * MIB, transcendentals=0),
        name="attend",
    )(group_ids, qkv, base, rel_q_heads, columns, *pieces)


def norm_rows(values, gain):
    centre = values - jnp.mean(values, axis=-1, keepdims=True)
    spread = jnp.mean(centre * centre, axis=-1, keepdims=True)
    return centre * lax.rsqrt(spread + 1e-07) * gain


def feed_rows(start, count, a, w, tokens, gain, w_up, w_down):
    rows = pl.ds(pl.multiple_of(start, 32), count)
    mixed = tokens[rows, :].astype(jnp.float32)
    for piece, weight in zip(a, w):
        mixed = mixed + jnp.dot(piece[rows, :], weight[...], preferred_element_type=jnp.float32)
    hidden = norm_rows(mixed, gain[...]).astype(jnp.bfloat16)
    up = jnp.dot(hidden, w_up[...], preferred_element_type=jnp.float32)
    inner = (0.5 * up * (1.0 + lax.erf(up * math.sqrt(0.5)))).astype(jnp.bfloat16)
    total = jnp.dot(inner, w_down[...], preferred_element_type=jnp.float32)
    return hidden, total


def feed_other_kernel(a0, a1, a2, a3, w0, w1, w2, w3, tokens, gain, w_up, w_down, out):
    core = lax.axis_index("head") % 2
    _, total = feed_rows(
        (1 - core) * out.shape[0], out.shape[0], (a0, a1, a2, a3), (w0, w1, w2, w3), tokens, gain, w_up, w_down
    )
    out[...] = total.astype(out.dtype)


def feed_own_kernel(a0, a1, a2, a3, w0, w1, w2, w3, tokens, gain, w_up, w_down, out, own):
    pieces, weights = (a0, a1, a2, a3), (w0, w1, w2, w3)
    count = out.shape[0]
    place = lax.axis_index("head")
    start = place % 2 * (2 * count)
    hidden, total = feed_rows(start, 2 * count, pieces, weights, tokens, gain, w_up, w_down)

    @pl.when(place // 2 == 0)
    def first():
        out[...] = total[count:]
        own[...] = hidden[:count].astype(jnp.float32) + total[:count]

    @pl.when(place // 2 != 0)
    def second():
        out[...] = total[:count]
        own[...] = hidden[count:].astype(jnp.float32) + total[count:]


def feed(kernel, pieces, weights, tokens, gain, w_up, w_down, outs, name):
    return pl.pallas_call(
        kernel,
        out_shape=outs,
        in_specs=full_specs(12),
        out_specs=full_specs(len(outs)),
        compiler_params=params(20),
        cost_estimate=pl.CostEstimate(flops=1600 * MIB, bytes_accessed=6 * MIB, transcendentals=0),
        name=name,
    )(*pieces, *weights, tokens, gain, w_up, w_down)


def fold_kernel(for_y, from_core, out):
    count = out.shape[0]
    other = 1 - lax.axis_index("head") // 2
    rows = pl.ds(pl.multiple_of(other * count, 32), count)
    out[...] = (for_y[...] + from_core[rows, :].astype(jnp.float32)).astype(out.dtype)


def block_of(head):
    return head % 2 * 2 + head // 2


def project_kernel(own, from_core, from_y, gain, w_proj, a0, a1, a2, a3, out, single):
    count = own.shape[0]
    place = lax.axis_index("head")
    rows = pl.ds(pl.multiple_of(place // 2 * count, 32), count)
    after = own[...] + from_core[rows, :].astype(jnp.float32) + from_y[...].astype(jnp.float32)
    hidden = norm_rows(after, gain[...]).astype(jnp.bfloat16)
    projected = jnp.dot(hidden, w_proj[...], preferred_element_type=jnp.float32)
    length = jnp.sum(projected * projected, axis=-1, keepdims=True)
    vectors = (projected * lax.rsqrt(length + 1e-06)).astype(jnp.bfloat16)
    single[...] = vectors
    pieces = (a0, a1, a2, a3)
    part = LANES // len(pieces) * 3 // 4
    lane = lax.broadcasted_iota(jnp.int32, (EXTRA, LANES), 1)
    lines = []
    for kind in range(2):
        line = jnp.zeros((EXTRA, LANES), jnp.float32)
        for x, piece in enumerate(pieces):
            from_head = place ^ x
            values = piece[piece.shape[0] - EXTRA :, kind * LANES : (kind + 1) * LANES]
            shift = lax.rem((from_head - block_of(place)) * part + LANES, LANES)
            rolled = pltpu.roll(values.astype(jnp.float32), shift, 1)
            line = jnp.where(lane // part == from_head, rolled, line)
        lines.append(line)
    which = lax.broadcasted_iota(jnp.int32, (EXTRA, LANES), 0)
    tail = jnp.where(which == 0, lines[0], lines[1]).astype(out.dtype)
    for o in range(out.shape[0]):
        out[o, :count] = vectors
        out[o, count:] = tail


def list_slots(queries, n_doc, listed):
    rows = queries.shape[0] // n_doc
    part = (rows - EXTRA) // QLEN * 8
    me = lax.axis_index("doc")
    shape = (n_doc, LANES)
    lane = lax.broadcasted_iota(jnp.int32, shape, 1)
    row = lax.broadcasted_iota(jnp.int32, shape, 0)
    tails = [
        queries[o * rows + rows - EXTRA : (o + 1) * rows, :].astype(jnp.float32) for o in range(n_doc)
    ]
    holder = jnp.concatenate([tail[:1] for tail in tails], axis=0).astype(jnp.int32)
    doc = jnp.concatenate([tail[1:2] for tail in tails], axis=0).astype(jnp.int32)
    mine = (lane < 4 * part) & (holder == me)
    group = (row * rows + lane % part // 8 * QLEN) // 16
    listed[n_doc : 2 * n_doc, :] = group | (doc << 8)
    ones = jnp.where(mine, 1.0, 0.0)
    until = lax.broadcasted_iota(jnp.int32, (LANES, LANES), 0) <= lax.broadcasted_iota(
        jnp.int32, (LANES, LANES), 1
    )
    until = jnp.where(until, 1.0, 0.0).astype(jnp.bfloat16)
    reached = jnp.dot(ones.astype(jnp.bfloat16), until, preferred_element_type=jnp.float32)
    in_row = jnp.sum(ones, axis=1, keepdims=True)
    above = jnp.zeros((1, 1), jnp.float32)
    starts = []
    for o in range(n_doc):
        starts.append(above)
        above = above + in_row[o : o + 1]
    reached = (reached + jnp.concatenate(starts, axis=0)).astype(jnp.int32)
    pad = jnp.zeros((LANES - n_doc, LANES), jnp.int32)
    columns = jnp.concatenate([reached, pad], axis=0).T
    square_lane = lax.broadcasted_iota(jnp.int32, (LANES, LANES), 1)
    blocks = (jnp.sum(ones).astype(jnp.int32) + LANES - 1) // LANES

    def one_block(block, carry):
        total = jnp.zeros((LANES, LANES), jnp.int32)
        for o in range(n_doc):
            passed = columns[:, o : o + 1] <= square_lane + block * LANES
            total = total + jnp.where(passed, 1, 0)
        listed[pl.ds(block, 1), :] = jnp.sum(total, axis=0, keepdims=True)
        return carry

    lax.fori_loop(0, blocks, one_block, 0)
    listed[n_doc - 1 : n_doc, :] = jnp.broadcast_to(above.astype(jnp.int32), (1, LANES))


def score_kernel(lengths, queries, docs, out, held, listed, slots, arrived, ready):
    chunks = arrived.shape[0]
    per = docs.shape[0] // chunks
    copies = [
        pltpu.make_async_copy(
            docs.at[pl.ds(c * per, per)], held.at[pl.ds(c * per, per)], arrived.at[c]
        )
        for c in range(chunks)
    ]
    for copy in copies:
        copy.start()
    list_slots(queries, out.shape[0], listed)
    to_scalars = pltpu.make_async_copy(listed, slots, ready)
    to_scalars.start()
    to_scalars.wait()
    for copy in copies:
        copy.wait()

    shape = (8, LANES)
    flat = lax.broadcasted_iota(jnp.int32, shape, 0) * LANES + lax.broadcasted_iota(jnp.int32, shape, 1)
    unroll = SCORE_UNROLL
    zero = jnp.zeros((QLEN, docs.shape[2]), jnp.bfloat16)
    position = lax.broadcasted_iota(jnp.int32, (docs.shape[1], 2 * QLEN), 0)
    side = lax.broadcasted_iota(jnp.int32, (1, 2 * QLEN), 1) < QLEN
    tables = out.shape[0]
    count = slots[tables - 1, 0]

    def some(i, totals):
        for u in range(0, unroll, 2):
            left, right, marks, limits = [], [], [], []
            for v in range(2):
                s = i * unroll + u + v
                used = s < count
                entry = jnp.where(used, slots[s >> 7, s & 127], 0)
                found = slots[tables + (entry >> 7), entry & 127]
                query = queries[pl.ds(pl.multiple_of((found & 255) * 16, 16), QLEN), :]
                doc = found >> 8
                left.append(jnp.concatenate([query, zero] if v == 0 else [zero, query], axis=1))
                right.append(held[doc])
                marks.append(jnp.where(used, entry, -1))
                limits.append(lengths[doc])
            sims = times_rows(jnp.concatenate(right, axis=1), jnp.concatenate(left, axis=0))
            limit = jnp.where(side, limits[0], limits[1])
            best = jnp.max(jnp.where(position < limit, sims, -jnp.inf), axis=0, keepdims=True)
            for v in range(2):
                total = jnp.sum(jnp.where(side if v == 0 else ~side, best, 0.0), axis=1, keepdims=True)
                totals = jnp.where(flat == marks[v], total, totals)
        return totals

    totals = lax.fori_loop(
        0, (count + unroll - 1) // unroll, some, jnp.zeros(shape, jnp.float32)
    )
    for o in range(out.shape[0]):
        row = jnp.broadcast_to(totals[o : o + 1], shape)
        for h in range(out.shape[1]):
            out[o, h] = row


def arrange_kernel(*refs):
    shares, out = refs[:-1], refs[-1]
    place = lax.axis_index("head")
    for k, share in enumerate(shares):
        count = share.shape[0]
        out[pl.ds(pl.multiple_of(block_of(place ^ k) * count, 32), count), :] = share[...]


def collect_kernel(tiles, out):
    n_head = tiles.shape[1]
    cols, reqs_all = out.shape
    reqs = reqs_all // n_head
    place = lax.axis_index("head")
    lines = []
    for h in range(n_head):
        total = tiles[0, h]
        for o in range(1, tiles.shape[0]):
            total = total + tiles[o, h]
        total = pltpu.roll(total, LANES - place * (reqs * cols), 1)
        lines.append(total[:1, : reqs * cols])
    order = sorted(range(n_head), key=block_of)
    rows = [lines[h][:, r * cols : (r + 1) * cols] for h in order for r in range(reqs)]
    out[...] = jnp.concatenate(rows, axis=0).T


def body(
    tokens,
    w_qkv,
    w_out,
    w_up,
    w_down,
    gain_one,
    gain_two,
    rel_table,
    prompt_cache,
    w_proj,
    doc_vectors,
    doc_lengths,
    group_ids,
    candidates,
):
    rows, depth = tokens.shape
    n_doc = lax.axis_size("doc")
    n_head = lax.axis_size("head")
    half, quarter = rows // 2, rows // n_head
    cand_rows, cols = candidates.shape
    reqs = cand_rows // n_head
    smem = pl.BlockSpec(memory_space=pltpu.SMEM)

    def over_doc(x, k):
        return lax.ppermute(x, "doc", [(i, i ^ k) for i in range(n_doc)])

    def over_head(x, k):
        return lax.ppermute(x, "head", [(i, i ^ k) for i in range(n_head)])

    tile = (8, LANES)
    pieces = {k: over_doc(prompt_cache, k) for k in (6, 5, 4, 3, 1, 2)}
    pieces[0] = prompt_cache
    pieces[1], w_out = lax.optimization_barrier((pieces[1], w_out))
    pieces[6], rel_table = lax.optimization_barrier((pieces[6], rel_table))
    pieces[7] = over_doc(pieces[6], 1)
    pieces = [pieces[k] for k in range(n_doc)]
    weight = jnp.transpose(w_qkv, (1, 0, 2))
    qkv, base, rel_q_heads = prepare(tokens, weight, rel_table)

    out_one = over_head(w_out, 2)
    out_pieces = [w_out, over_head(w_out, 1), out_one, over_head(out_one, 1)]

    att = attend(group_ids, qkv, base, rel_q_heads, candidates.T, pieces)
    att_y = over_head(att, 2)
    att_pieces = [att, over_head(att, 1), att_y, over_head(att_y, 1)]

    common = (att_pieces, out_pieces, tokens, gain_one.reshape(1, -1), w_up, w_down)
    other = feed(
        feed_other_kernel,
        *common,
        [jax.ShapeDtypeStruct((half, depth), jnp.bfloat16)],
        "feed_other",
    )[0]
    from_core = over_head(other, 1)
    for_y, own = feed(
        feed_own_kernel,
        *common,
        [jax.ShapeDtypeStruct((quarter, depth), jnp.float32)] * 2,
        "feed_own",
    )
    folded = pl.pallas_call(
        fold_kernel,
        out_shape=jax.ShapeDtypeStruct((quarter, depth), jnp.bfloat16),
        in_specs=full_specs(2),
        out_specs=full_specs(1)[0],
        compiler_params=params(4),
        name="fold",
    )(for_y, from_core)
    from_y = over_head(folded, 2)

    emb = w_proj.shape[1]
    vectors, single = pl.pallas_call(
        project_kernel,
        out_shape=[
            jax.ShapeDtypeStruct((n_doc, quarter + EXTRA, emb), jnp.bfloat16),
            jax.ShapeDtypeStruct((quarter, emb), jnp.bfloat16),
        ],
        in_specs=full_specs(9),
        out_specs=full_specs(2),
        compiler_params=params(8),
        name="project",
    )(own, from_core, from_y, gain_two.reshape(1, -1), w_proj, *att_pieces)
    queries = lax.all_to_all(vectors, "doc", 0, 0, tiled=True).reshape(-1, emb)

    rated = pl.pallas_call(
        score_kernel,
        out_shape=jax.ShapeDtypeStruct((n_doc, n_head) + tile, jnp.float32),
        in_specs=[smem] + full_specs(1) + [pl.BlockSpec(memory_space=pltpu.HBM)],
        out_specs=full_specs(1)[0],
        scratch_shapes=[
            pltpu.VMEM(doc_vectors.shape, jnp.bfloat16),
            pltpu.VMEM((2 * n_doc, LANES), jnp.int32),
            pltpu.SMEM((2 * n_doc, LANES), jnp.int32),
            pltpu.SemaphoreType.DMA((8,)),
            pltpu.SemaphoreType.DMA,
        ],
        compiler_params=params(16),
        name="rate",
    )(doc_lengths, queries, far(doc_vectors))
    back = lax.all_to_all(rated.reshape(-1, LANES), ("doc", "head"), 0, 0, tiled=True)

    single, _ = lax.optimization_barrier((single, rated))
    shares = [single] + [over_head(single, k) for k in range(1, n_head)]
    query_vectors = pl.pallas_call(
        arrange_kernel,
        out_shape=jax.ShapeDtypeStruct((rows, emb), jnp.bfloat16),
        in_specs=full_specs(n_head),
        out_specs=full_specs(1)[0],
        compiler_params=params(4),
        name="arrange",
    )(*shares)

    scores = pl.pallas_call(
        collect_kernel,
        out_shape=jax.ShapeDtypeStruct((cols, cand_rows), jnp.float32),
        in_specs=full_specs(1),
        out_specs=full_specs(1)[0],
        compiler_params=params(4),
        name="collect",
    )(back.reshape((n_doc, n_head) + tile))
    return (query_vectors, scores.T)


def solution(mesh):
    placed = (
        P("doc", None),
        P(None, None, "head"),
        P("head", None),
        P(None, "head"),
        P("head", None),
        P(),
        P(),
        P(),
        P(None, "doc", "head"),
        P(),
        P("doc", None, None),
        P("doc"),
        P("doc"),
        P("doc", "head"),
    )
    fits = mesh.shape["head"] == 4 and mesh.shape["doc"] == 8
    return jax.shard_map(
        body if fits else body_any,
        mesh=mesh,
        in_specs=placed,
        out_specs=(P("doc", None), P("doc", "head")),
        check_vma=False,
    )
```

```python
import functools
import math

import jax
import jax.numpy as jnp
from jax import lax
from jax.experimental import pallas as pl
from jax.experimental.pallas import tpu as pltpu
from jax.sharding import PartitionSpec as P

HD = 64
RELS = 512
QLEN = 32
PLEN = 64
DOC_DEV = 64


def layer_norm(values, gain):
    centre = values - jnp.mean(values, axis=-1, keepdims=True)
    spread = jnp.mean(centre * centre, axis=-1, keepdims=True)
    return centre * lax.rsqrt(spread + 1e-07) * gain


def slot_order(holders):
    count = holders.shape[0]
    same = holders[:, None] == holders[None, :]
    earlier = jnp.arange(count)[:, None] > jnp.arange(count)[None, :]
    return jnp.sum(same & earlier, axis=1)


def rate_slots(slot_query, slot_doc, doc_vectors, doc_lengths):
    shape = slot_doc.shape
    flat_doc = slot_doc.reshape(-1)
    flat_query = slot_query.reshape((flat_doc.shape[0],) + slot_query.shape[-2:])
    safe_doc = jnp.maximum(flat_doc, 0)
    documents = doc_vectors[safe_doc]
    lengths = doc_lengths[safe_doc]
    sims = jnp.einsum("sqe,sje->sqj", flat_query, documents, preferred_element_type=jnp.float32)
    live = jnp.arange(documents.shape[1], dtype=jnp.int32)[None, None, :] < lengths[:, None, None]
    best = jnp.max(jnp.where(live, sims, -jnp.inf), axis=2)
    totals = jnp.where(flat_doc >= 0, jnp.sum(best, axis=1), 0.0)
    return totals.reshape(shape)


def body_any(
    tokens,
    w_qkv,
    w_out,
    w_up,
    w_down,
    gain_one,
    gain_two,
    rel_table,
    prompt_cache,
    w_proj,
    doc_vectors,
    doc_lengths,
    group_ids,
    candidates,
):
    rows_dev = tokens.shape[0]
    req_dev = rows_dev // QLEN
    width = w_qkv.shape[2]
    heads_loc = width // HD
    half = RELS // 2
    scale_root = math.sqrt(3 * HD)
    gathered = lax.all_gather(prompt_cache, "doc", axis=1, tiled=True)
    weights_split = w_qkv.reshape(w_qkv.shape[0], 3, heads_loc, HD)
    projected_all = jnp.einsum(
        "td,dchf->chtf", tokens, weights_split, preferred_element_type=jnp.float32
    ).astype(jnp.bfloat16)
    rel_both = jnp.einsum(
        "rd,dchf->chrf", rel_table, weights_split[:, :2], preferred_element_type=jnp.float32
    ).astype(jnp.bfloat16)
    head_shape = (heads_loc, req_dev, QLEN, HD)
    query_four = projected_all[0].reshape(head_shape)
    keys_four = projected_all[1].reshape(head_shape)
    values_four = projected_all[2].reshape(head_shape)
    groups_all = gathered.shape[1] // PLEN
    cache_all = gathered.reshape(2, groups_all, PLEN, heads_loc, HD)
    picked = jnp.transpose(cache_all[:, group_ids], (0, 3, 1, 2, 4))
    keys = jnp.concatenate([keys_four, picked[0]], axis=2)
    values = jnp.concatenate([values_four, picked[1]], axis=2)
    pos_query = PLEN + jnp.arange(QLEN, dtype=jnp.int32)
    pos_key = jnp.concatenate([pos_query, jnp.arange(PLEN, dtype=jnp.int32)])
    index_one = pos_query[:, None] - pos_key[None, :] + half
    index_two = pos_key[:, None] - pos_query[None, :] + half
    rel_k_rows = rel_both[1][:, index_one]
    rel_q_rows = rel_both[0][:, index_two]
    c2p = jnp.einsum("hrqd,hqkd->hrqk", query_four, rel_k_rows, preferred_element_type=jnp.float32)
    p2c = jnp.einsum("hrkd,hkqd->hrqk", keys, rel_q_rows, preferred_element_type=jnp.float32)
    content = jnp.einsum("hrqd,hrkd->hrqk", query_four, keys, preferred_element_type=jnp.float32)
    logits = (content + c2p + p2c) / scale_root
    largest = jnp.max(logits, axis=-1, keepdims=True)
    weights = jnp.exp(logits - largest)
    denominator = jnp.sum(weights, axis=-1)
    summed = jnp.einsum(
        "hrqk,hrkd->hrqd", weights.astype(jnp.bfloat16), values, preferred_element_type=jnp.float32
    )
    attended = (summed / denominator[..., None]).astype(jnp.bfloat16)
    out_split = w_out.reshape(heads_loc, HD, w_out.shape[1])
    attn_part = jnp.einsum(
        "hrqd,hde->rqe", attended, out_split, preferred_element_type=jnp.float32
    ).reshape(rows_dev, w_out.shape[1])
    attn_total = lax.psum(attn_part.astype(jnp.bfloat16), "head").astype(jnp.float32)
    hidden_one = layer_norm(tokens.astype(jnp.float32) + attn_total, gain_one).astype(jnp.bfloat16)
    inner = jax.nn.gelu(
        jnp.dot(hidden_one, w_up, preferred_element_type=jnp.float32), approximate=False
    ).astype(jnp.bfloat16)
    ffn_total = lax.psum(
        jnp.dot(inner, w_down, preferred_element_type=jnp.float32).astype(jnp.bfloat16), "head"
    ).astype(jnp.float32)
    hidden_two = layer_norm(hidden_one.astype(jnp.float32) + ffn_total, gain_two).astype(
        jnp.bfloat16
    )
    projected = jnp.dot(hidden_two, w_proj, preferred_element_type=jnp.float32)
    query_vectors = (
        projected * lax.rsqrt(jnp.sum(projected * projected, axis=-1, keepdims=True) + 1e-06)
    ).astype(jnp.bfloat16)
    shards = lax.axis_size("doc")
    cand_dev = candidates.shape[1]
    pairs = req_dev * cand_dev
    capacity = max(2, 2 * pairs // shards)
    flat_cand = candidates.reshape(-1)
    holders = flat_cand // DOC_DEV
    request_of = jnp.arange(pairs, dtype=jnp.int32) // cand_dev
    slot_rank = slot_order(holders)
    copies, cand_copies = (
        lax.all_gather(query_vectors, "doc", axis=0, tiled=True),
        lax.all_gather(candidates, "doc", axis=0, tiled=True),
    )
    all_query = copies.reshape(shards, req_dev, QLEN, copies.shape[1])
    all_cand = cand_copies.reshape(shards, pairs)
    holder_all = all_cand // DOC_DEV
    local_all = all_cand % DOC_DEV
    rank_all = jax.vmap(slot_order)(holder_all)
    own_index = lax.axis_index("doc")
    chosen = (holder_all[:, None, :] == own_index) & (
        rank_all[:, None, :] == jnp.arange(capacity, dtype=jnp.int32)[None, :, None]
    )
    filled = jnp.any(chosen, axis=2)
    slot_request = jnp.sum(jnp.where(chosen, request_of[None, None, :], 0), axis=2)
    slot_doc = jnp.where(
        filled, jnp.sum(jnp.where(chosen, local_all[:, None, :], 0), axis=2), -1
    ).astype(jnp.int32)
    slot_query = all_query[jnp.arange(shards)[:, None], slot_request]
    slot_scores = rate_slots(slot_query, slot_doc, doc_vectors, doc_lengths)
    returned = lax.all_to_all(slot_scores, "doc", split_axis=0, concat_axis=0, tiled=True)
    scores = returned.reshape(-1)[holders * capacity + slot_rank].reshape(candidates.shape)
    return (query_vectors, scores)


LANES = 128
MIB = 1 << 20
EXTRA = 16
PREP_UNROLL = 12
ATT_UNROLL = 12
SCORE_UNROLL = 32


def full_specs(count):
    return [pl.BlockSpec(memory_space=pltpu.VMEM)] * count


def far(x):
    return pltpu.with_memory_space_constraint(x, pltpu.HBM)


def params(mib):
    return pltpu.CompilerParams(vmem_limit_bytes=mib * MIB)


def by_head(values):
    head_of = lax.broadcasted_iota(jnp.int32, values.shape, 1) // HD
    heads = values.shape[1] // HD
    zero = jnp.zeros_like(values)
    return jnp.concatenate([jnp.where(head_of == h, values, zero) for h in range(heads)], axis=0)


def times_rows(left, right):
    return lax.dot_general(left, right, (((1,), (1,)), ((), ())), preferred_element_type=jnp.float32)


def key_terms(key_rel, first):
    slot = lax.broadcasted_iota(jnp.int32, (key_rel.shape[0], LANES), 1) // QLEN
    turned = None
    for h in range(key_rel.shape[1] // LANES):
        shift = (LANES - PLEN - QLEN + first + h * QLEN) % LANES
        rolled = pltpu.roll(
            key_rel[:, h * LANES : (h + 1) * LANES], shift, 1, stride=1, stride_axis=0
        )
        turned = rolled if turned is None else jnp.where(slot == h, rolled, turned)
    return turned


def prepare_kernel(
    tokens_far, weight_far, rel_table, qkv, base, rel_q_heads, q_heads, query_rel, key_rel, *scratch
):
    tokens, weight, rel_rows, arrived = scratch
    rel_far = rel_table.at[pl.ds(RELS // 2 - PLEN - QLEN, rel_rows.shape[0])]
    copies = [pltpu.make_async_copy(tokens_far, tokens, arrived.at[0])]
    copies += [pltpu.make_async_copy(weight_far.at[i], weight.at[i], arrived.at[1 + i]) for i in range(3)]
    copies += [pltpu.make_async_copy(rel_far, rel_rows, arrived.at[4])]
    for copy in copies:
        copy.start()
    copies[0].wait()
    width = weight.shape[2]
    heads = width // HD
    for i in range(3):
        copies[1 + i].wait()
        qkv[:, i * width : (i + 1) * width] = jnp.dot(
            tokens[...], weight[i], preferred_element_type=jnp.float32
        ).astype(jnp.bfloat16)
    count = rel_rows.shape[0]
    copies[4].wait()
    rel = [
        jnp.dot(rel_rows[...], weight[i], preferred_element_type=jnp.float32).astype(jnp.bfloat16)
        for i in range(2)
    ]
    both = lax.broadcasted_iota(jnp.int32, (LANES, count), 0) + lax.broadcasted_iota(
        jnp.int32, (LANES, count), 1
    )
    flip_q = jnp.where(both == LANES, 1.0, 0.0).astype(jnp.bfloat16)
    flip_k = jnp.where(both == LANES + PLEN - 1, 1.0, 0.0).astype(jnp.bfloat16)
    rel_q = jnp.dot(flip_q, rel[0], preferred_element_type=jnp.float32)
    rel_k = jnp.dot(flip_k, rel[1], preferred_element_type=jnp.float32)
    rel_q_heads[...] = by_head(rel_q.astype(jnp.bfloat16))
    requests, _, many = base.shape
    for r in range(requests):
        q_heads[r * many : (r + 1) * many, :] = by_head(qkv[r * QLEN : (r + 1) * QLEN, :width])
    query_rel[...] = times_rows(q_heads[...], rel_k.astype(jnp.bfloat16))
    key_rel[...] = times_rows(qkv[:, width : 2 * width], rel_q_heads[...])
    scale = 1.0 / math.sqrt(3 * HD)

    def one_request(r, carry):
        rows = pl.ds(pl.multiple_of(r * QLEN, QLEN), QLEN)
        spread = pl.ds(pl.multiple_of(r * many, many), many)
        turned = times_rows(qkv[rows, width : 2 * width], q_heads[spread, :])
        turned = turned + key_terms(key_rel[rows, :], PLEN)
        spread_rel = query_rel[spread, :]
        c2p = jnp.concatenate(
            [
                pltpu.roll(
                    spread_rel[h * QLEN : (h + 1) * QLEN],
                    LANES - QLEN + 1,
                    1,
                    stride=1,
                    stride_axis=0,
                )
                for h in range(heads)
            ],
            axis=0,
        )
        c2p = c2p.T
        base[r, :PLEN] = c2p[:PLEN] * scale
        base[r, PLEN:] = (c2p[PLEN : PLEN + QLEN] + turned) * scale
        return carry

    lax.fori_loop(0, requests, one_request, 0, unroll=PREP_UNROLL)


def prepare(tokens, weight, rel_table):
    rows = tokens.shape[0]
    width = weight.shape[2]
    heads = width // HD
    return pl.pallas_call(
        prepare_kernel,
        out_shape=[
            jax.ShapeDtypeStruct((rows, 3 * width), jnp.bfloat16),
            jax.ShapeDtypeStruct((rows // QLEN, PLEN + QLEN, heads * QLEN), jnp.float32),
            jax.ShapeDtypeStruct((heads * LANES, width), jnp.bfloat16),
        ],
        in_specs=[pl.BlockSpec(memory_space=pltpu.HBM)] * 3,
        out_specs=full_specs(3),
        scratch_shapes=[
            pltpu.VMEM((rows * heads, width), jnp.bfloat16),
            pltpu.VMEM((rows * heads, LANES), jnp.float32),
            pltpu.VMEM((rows, heads * LANES), jnp.float32),
            pltpu.VMEM(tokens.shape, jnp.bfloat16),
            pltpu.VMEM(weight.shape, jnp.bfloat16),
            pltpu.VMEM((2 * (PLEN + QLEN), rel_table.shape[1]), jnp.bfloat16),
            pltpu.SemaphoreType.DMA((5,)),
        ],
        compiler_params=params(16),
        cost_estimate=pl.CostEstimate(flops=4000 * MIB, bytes_accessed=4 * MIB, transcendentals=0),
        name="prepare",
    )(far(tokens), far(weight), far(rel_table))


def attend_kernel(group_ids, qkv, base, rel_q_heads, columns, *rest):
    pieces, (att, cache, picked, key_rel, shares, arrived) = rest[:-6], rest[-6:]
    copies = [
        [
            pltpu.make_async_copy(piece.at[kind], cache.at[kind, at], arrived.at[kind, at])
            for at, piece in enumerate(pieces)
        ]
        for kind in range(2)
    ]
    for copy in copies[0] + copies[1]:
        copy.start()
    requests, _, _ = base.shape
    tokens = requests * QLEN
    ids = columns[...].T
    spare = jnp.zeros((1, LANES - columns.shape[0] * columns.shape[1]), jnp.int32)
    line = jnp.concatenate([ids[r : r + 1, :] for r in range(ids.shape[0])] + [spare], axis=1)
    line = jnp.concatenate([line // DOC_DEV, line % DOC_DEV], axis=1)
    extra = jnp.broadcast_to(line.astype(jnp.float32), (EXTRA, line.shape[1]))
    att[tokens:, :] = extra.astype(att.dtype)
    width = att.shape[1]
    heads = width // HD
    groups_dev = cache.shape[2] // PLEN
    me = lax.axis_index("doc")
    small_head = lax.broadcasted_iota(jnp.int32, (QLEN, width), 1) // HD
    scale = 1.0 / math.sqrt(3 * HD)

    def place_of(r):
        owner = group_ids[r] // groups_dev
        within = pl.multiple_of((group_ids[r] - owner * groups_dev) * PLEN, PLEN)
        return owner ^ me, pl.ds(within, PLEN)

    for copy in copies[0]:
        copy.wait()
    for r in range(requests):
        piece, within = place_of(r)
        picked[r * PLEN : (r + 1) * PLEN, :] = cache[0, piece, within, :]
    key_rel[...] = times_rows(picked[...], rel_q_heads[...])

    def one_softmax(r, carry):
        rows = pl.ds(pl.multiple_of(r * QLEN, QLEN), QLEN)
        cached = pl.ds(pl.multiple_of(r * PLEN, PLEN), PLEN)
        turned = times_rows(picked[cached, :], by_head(qkv[rows, 0:width]))
        turned = (turned + key_terms(key_rel[cached, :], 0)) * scale
        logits = jnp.concatenate([base[r, :PLEN] + turned, base[r, PLEN:]], axis=0)
        weights = jnp.exp(logits - jnp.max(logits, axis=0, keepdims=True))
        weights = weights * (1.0 / jnp.sum(weights, axis=0, keepdims=True))
        shares[r] = weights.astype(shares.dtype)
        return carry

    lax.fori_loop(0, requests, one_softmax, 0, unroll=ATT_UNROLL)
    for copy in copies[1]:
        copy.wait()

    def one_sum(r, carry):
        rows = pl.ds(pl.multiple_of(r * QLEN, QLEN), QLEN)
        piece, within = place_of(r)
        values = jnp.concatenate(
            [cache[1, piece, within, :], qkv[rows, 2 * width : 3 * width]], axis=0
        )
        summed = lax.dot_general(
            shares[r],
            values,
            (((0,), (0,)), ((), ())),
            preferred_element_type=jnp.float32,
        )
        out = summed[:QLEN]
        for h in range(1, heads):
            out = jnp.where(small_head == h, summed[h * QLEN : (h + 1) * QLEN], out)
        att[rows, :] = out.astype(jnp.bfloat16)
        return carry

    lax.fori_loop(0, requests, one_sum, 0, unroll=ATT_UNROLL)


def attend(group_ids, qkv, base, rel_q_heads, columns, pieces):
    rows = qkv.shape[0]
    width = qkv.shape[1] // 3
    cached = rows // QLEN * PLEN
    return pl.pallas_call(
        attend_kernel,
        out_shape=jax.ShapeDtypeStruct((rows + EXTRA, width), jnp.bfloat16),
        in_specs=[pl.BlockSpec(memory_space=pltpu.SMEM)]
        + full_specs(4)
        + [pl.BlockSpec(memory_space=pl.ANY)] * len(pieces),
        out_specs=pl.BlockSpec(memory_space=pltpu.VMEM),
        scratch_shapes=[
            pltpu.VMEM((2, len(pieces)) + pieces[0].shape[1:], jnp.bfloat16),
            pltpu.VMEM((cached, width), jnp.bfloat16),
            pltpu.VMEM((cached, rel_q_heads.shape[0]), jnp.float32),
            pltpu.VMEM(base.shape, jnp.bfloat16),
            pltpu.SemaphoreType.DMA((2, len(pieces))),
        ],
        compiler_params=params(12),
        cost_estimate=pl.CostEstimate(flops=2000 * MIB, bytes_accessed=2 * MIB, transcendentals=0),
        name="attend",
    )(group_ids, qkv, base, rel_q_heads, columns, *pieces)


def norm_rows(values, gain):
    centre = values - jnp.mean(values, axis=-1, keepdims=True)
    spread = jnp.mean(centre * centre, axis=-1, keepdims=True)
    return centre * lax.rsqrt(spread + 1e-07) * gain


def feed_rows(start, count, a, w, tokens, gain, w_up, w_down):
    rows = pl.ds(pl.multiple_of(start, 32), count)
    mixed = tokens[rows, :].astype(jnp.float32)
    for piece, weight in zip(a, w):
        mixed = mixed + jnp.dot(piece[rows, :], weight[...], preferred_element_type=jnp.float32)
    hidden = norm_rows(mixed, gain[...]).astype(jnp.bfloat16)
    up = jnp.dot(hidden, w_up[...], preferred_element_type=jnp.float32)
    inner = (0.5 * up * (1.0 + lax.erf(up * math.sqrt(0.5)))).astype(jnp.bfloat16)
    total = jnp.dot(inner, w_down[...], preferred_element_type=jnp.float32)
    return hidden, total


def feed_other_kernel(a0, a1, a2, a3, w0, w1, w2, w3, tokens, gain, w_up, w_down, out):
    core = lax.axis_index("head") % 2
    _, total = feed_rows(
        (1 - core) * out.shape[0], out.shape[0], (a0, a1, a2, a3), (w0, w1, w2, w3), tokens, gain, w_up, w_down
    )
    out[...] = total.astype(out.dtype)


def feed_own_kernel(a0, a1, a2, a3, w0, w1, w2, w3, tokens, gain, w_up, w_down, out, own):
    pieces, weights = (a0, a1, a2, a3), (w0, w1, w2, w3)
    count = out.shape[0]
    place = lax.axis_index("head")
    start = place % 2 * (2 * count)
    hidden, total = feed_rows(start, 2 * count, pieces, weights, tokens, gain, w_up, w_down)

    @pl.when(place // 2 == 0)
    def first():
        out[...] = total[count:]
        own[...] = hidden[:count].astype(jnp.float32) + total[:count]

    @pl.when(place // 2 != 0)
    def second():
        out[...] = total[:count]
        own[...] = hidden[count:].astype(jnp.float32) + total[count:]


def feed(kernel, pieces, weights, tokens, gain, w_up, w_down, outs, name):
    return pl.pallas_call(
        kernel,
        out_shape=outs,
        in_specs=full_specs(12),
        out_specs=full_specs(len(outs)),
        compiler_params=params(20),
        cost_estimate=pl.CostEstimate(flops=1600 * MIB, bytes_accessed=6 * MIB, transcendentals=0),
        name=name,
    )(*pieces, *weights, tokens, gain, w_up, w_down)


def fold_kernel(for_y, from_core, out):
    count = out.shape[0]
    other = 1 - lax.axis_index("head") // 2
    rows = pl.ds(pl.multiple_of(other * count, 32), count)
    out[...] = (for_y[...] + from_core[rows, :].astype(jnp.float32)).astype(out.dtype)


def block_of(head):
    return head % 2 * 2 + head // 2


def project_kernel(own, from_core, from_y, gain, w_proj, a0, a1, a2, a3, out, single):
    count = own.shape[0]
    place = lax.axis_index("head")
    rows = pl.ds(pl.multiple_of(place // 2 * count, 32), count)
    after = own[...] + from_core[rows, :].astype(jnp.float32) + from_y[...].astype(jnp.float32)
    hidden = norm_rows(after, gain[...]).astype(jnp.bfloat16)
    projected = jnp.dot(hidden, w_proj[...], preferred_element_type=jnp.float32)
    length = jnp.sum(projected * projected, axis=-1, keepdims=True)
    vectors = (projected * lax.rsqrt(length + 1e-06)).astype(jnp.bfloat16)
    single[...] = vectors
    pieces = (a0, a1, a2, a3)
    part = LANES // len(pieces) * 3 // 4
    lane = lax.broadcasted_iota(jnp.int32, (EXTRA, LANES), 1)
    lines = []
    for kind in range(2):
        line = jnp.zeros((EXTRA, LANES), jnp.float32)
        for x, piece in enumerate(pieces):
            from_head = place ^ x
            values = piece[piece.shape[0] - EXTRA :, kind * LANES : (kind + 1) * LANES]
            shift = lax.rem((from_head - block_of(place)) * part + LANES, LANES)
            rolled = pltpu.roll(values.astype(jnp.float32), shift, 1)
            line = jnp.where(lane // part == from_head, rolled, line)
        lines.append(line)
    which = lax.broadcasted_iota(jnp.int32, (EXTRA, LANES), 0)
    tail = jnp.where(which == 0, lines[0], lines[1]).astype(out.dtype)
    for o in range(out.shape[0]):
        out[o, :count] = vectors
        out[o, count:] = tail


def list_slots(queries, n_doc, listed):
    rows = queries.shape[0] // n_doc
    part = (rows - EXTRA) // QLEN * 8
    me = lax.axis_index("doc")
    shape = (n_doc, LANES)
    lane = lax.broadcasted_iota(jnp.int32, shape, 1)
    row = lax.broadcasted_iota(jnp.int32, shape, 0)
    tails = [
        queries[o * rows + rows - EXTRA : (o + 1) * rows, :].astype(jnp.float32) for o in range(n_doc)
    ]
    holder = jnp.concatenate([tail[:1] for tail in tails], axis=0).astype(jnp.int32)
    doc = jnp.concatenate([tail[1:2] for tail in tails], axis=0).astype(jnp.int32)
    mine = (lane < 4 * part) & (holder == me)
    group = (row * rows + lane % part // 8 * QLEN) // 16
    listed[n_doc : 2 * n_doc, :] = group | (doc << 8)
    ones = jnp.where(mine, 1.0, 0.0)
    until = lax.broadcasted_iota(jnp.int32, (LANES, LANES), 0) <= lax.broadcasted_iota(
        jnp.int32, (LANES, LANES), 1
    )
    until = jnp.where(until, 1.0, 0.0).astype(jnp.bfloat16)
    reached = jnp.dot(ones.astype(jnp.bfloat16), until, preferred_element_type=jnp.float32)
    in_row = jnp.sum(ones, axis=1, keepdims=True)
    above = jnp.zeros((1, 1), jnp.float32)
    starts = []
    for o in range(n_doc):
        starts.append(above)
        above = above + in_row[o : o + 1]
    reached = (reached + jnp.concatenate(starts, axis=0)).astype(jnp.int32)
    pad = jnp.zeros((LANES - n_doc, LANES), jnp.int32)
    columns = jnp.concatenate([reached, pad], axis=0).T
    square_lane = lax.broadcasted_iota(jnp.int32, (LANES, LANES), 1)
    blocks = (jnp.sum(ones).astype(jnp.int32) + LANES - 1) // LANES

    def one_block(block, carry):
        total = jnp.zeros((LANES, LANES), jnp.int32)
        for o in range(n_doc):
            passed = columns[:, o : o + 1] <= square_lane + block * LANES
            total = total + jnp.where(passed, 1, 0)
        listed[pl.ds(block, 1), :] = jnp.sum(total, axis=0, keepdims=True)
        return carry

    lax.fori_loop(0, blocks, one_block, 0)
    listed[n_doc - 1 : n_doc, :] = jnp.broadcast_to(above.astype(jnp.int32), (1, LANES))


def score_kernel(lengths, queries, docs, out, held, listed, slots, arrived, ready):
    chunks = arrived.shape[0]
    per = docs.shape[0] // chunks
    copies = [
        pltpu.make_async_copy(
            docs.at[pl.ds(c * per, per)], held.at[pl.ds(c * per, per)], arrived.at[c]
        )
        for c in range(chunks)
    ]
    for copy in copies:
        copy.start()
    list_slots(queries, out.shape[0], listed)
    to_scalars = pltpu.make_async_copy(listed, slots, ready)
    to_scalars.start()
    to_scalars.wait()
    for copy in copies:
        copy.wait()

    shape = (8, LANES)
    flat = lax.broadcasted_iota(jnp.int32, shape, 0) * LANES + lax.broadcasted_iota(jnp.int32, shape, 1)
    unroll = SCORE_UNROLL
    zero = jnp.zeros((QLEN, docs.shape[2]), jnp.bfloat16)
    position = lax.broadcasted_iota(jnp.int32, (docs.shape[1], 2 * QLEN), 0)
    side = lax.broadcasted_iota(jnp.int32, (1, 2 * QLEN), 1) < QLEN
    tables = out.shape[0]
    count = slots[tables - 1, 0]

    def some(i, totals):
        for u in range(0, unroll, 2):
            left, right, marks, limits = [], [], [], []
            for v in range(2):
                s = i * unroll + u + v
                used = s < count
                entry = jnp.where(used, slots[s >> 7, s & 127], 0)
                found = slots[tables + (entry >> 7), entry & 127]
                query = queries[pl.ds(pl.multiple_of((found & 255) * 16, 16), QLEN), :]
                doc = found >> 8
                left.append(jnp.concatenate([query, zero] if v == 0 else [zero, query], axis=1))
                right.append(held[doc])
                marks.append(jnp.where(used, entry, -1))
                limits.append(lengths[doc])
            sims = times_rows(jnp.concatenate(right, axis=1), jnp.concatenate(left, axis=0))
            limit = jnp.where(side, limits[0], limits[1])
            best = jnp.max(jnp.where(position < limit, sims, -jnp.inf), axis=0, keepdims=True)
            for v in range(2):
                total = jnp.sum(jnp.where(side if v == 0 else ~side, best, 0.0), axis=1, keepdims=True)
                totals = jnp.where(flat == marks[v], total, totals)
        return totals

    totals = lax.fori_loop(
        0, (count + unroll - 1) // unroll, some, jnp.zeros(shape, jnp.float32)
    )
    for o in range(out.shape[0]):
        row = jnp.broadcast_to(totals[o : o + 1], shape)
        for h in range(out.shape[1]):
            out[o, h] = row


def arrange_kernel(*refs):
    shares, out = refs[:-1], refs[-1]
    place = lax.axis_index("head")
    for k, share in enumerate(shares):
        count = share.shape[0]
        out[pl.ds(pl.multiple_of(block_of(place ^ k) * count, 32), count), :] = share[...]


def collect_kernel(tiles, out):
    n_head = tiles.shape[1]
    cols, reqs_all = out.shape
    reqs = reqs_all // n_head
    place = lax.axis_index("head")
    lines = []
    for h in range(n_head):
        total = tiles[0, h]
        for o in range(1, tiles.shape[0]):
            total = total + tiles[o, h]
        total = pltpu.roll(total, LANES - place * (reqs * cols), 1)
        lines.append(total[:1, : reqs * cols])
    order = sorted(range(n_head), key=block_of)
    rows = [lines[h][:, r * cols : (r + 1) * cols] for h in order for r in range(reqs)]
    out[...] = jnp.concatenate(rows, axis=0).T


def body(
    tokens,
    w_qkv,
    w_out,
    w_up,
    w_down,
    gain_one,
    gain_two,
    rel_table,
    prompt_cache,
    w_proj,
    doc_vectors,
    doc_lengths,
    group_ids,
    candidates,
):
    rows, depth = tokens.shape
    n_doc = lax.axis_size("doc")
    n_head = lax.axis_size("head")
    half, quarter = rows // 2, rows // n_head
    cand_rows, cols = candidates.shape
    reqs = cand_rows // n_head
    smem = pl.BlockSpec(memory_space=pltpu.SMEM)

    def over_doc(x, k):
        return lax.ppermute(x, "doc", [(i, i ^ k) for i in range(n_doc)])

    def over_head(x, k):
        return lax.ppermute(x, "head", [(i, i ^ k) for i in range(n_head)])

    tile = (8, LANES)
    pieces = {k: over_doc(prompt_cache, k) for k in (6, 5, 4, 3, 1, 2)}
    pieces[0] = prompt_cache
    pieces[2], w_out = lax.optimization_barrier((pieces[2], w_out))
    pieces[6], rel_table = lax.optimization_barrier((pieces[6], rel_table))
    pieces[7] = over_doc(pieces[6], 1)
    pieces = [pieces[k] for k in range(n_doc)]
    weight = jnp.transpose(w_qkv, (1, 0, 2))
    qkv, base, rel_q_heads = prepare(tokens, weight, rel_table)

    out_one = over_head(w_out, 2)
    out_pieces = [w_out, over_head(w_out, 1), out_one, over_head(out_one, 1)]

    att = attend(group_ids, qkv, base, rel_q_heads, candidates.T, pieces)
    att_y = over_head(att, 2)
    att_pieces = [att, over_head(att, 1), att_y, over_head(att_y, 1)]

    common = (att_pieces, out_pieces, tokens, gain_one.reshape(1, -1), w_up, w_down)
    other = feed(
        feed_other_kernel,
        *common,
        [jax.ShapeDtypeStruct((half, depth), jnp.bfloat16)],
        "feed_other",
    )[0]
    from_core = over_head(other, 1)
    for_y, own = feed(
        feed_own_kernel,
        *common,
        [jax.ShapeDtypeStruct((quarter, depth), jnp.float32)] * 2,
        "feed_own",
    )
    folded = pl.pallas_call(
        fold_kernel,
        out_shape=jax.ShapeDtypeStruct((quarter, depth), jnp.bfloat16),
        in_specs=full_specs(2),
        out_specs=full_specs(1)[0],
        compiler_params=params(4),
        name="fold",
    )(for_y, from_core)
    from_y = over_head(folded, 2)

    emb = w_proj.shape[1]
    vectors, single = pl.pallas_call(
        project_kernel,
        out_shape=[
            jax.ShapeDtypeStruct((n_doc, quarter + EXTRA, emb), jnp.bfloat16),
            jax.ShapeDtypeStruct((quarter, emb), jnp.bfloat16),
        ],
        in_specs=full_specs(9),
        out_specs=full_specs(2),
        compiler_params=params(8),
        name="project",
    )(own, from_core, from_y, gain_two.reshape(1, -1), w_proj, *att_pieces)
    queries = lax.all_to_all(vectors, "doc", 0, 0, tiled=True).reshape(-1, emb)

    rated = pl.pallas_call(
        score_kernel,
        out_shape=jax.ShapeDtypeStruct((n_doc, n_head) + tile, jnp.float32),
        in_specs=[smem] + full_specs(1) + [pl.BlockSpec(memory_space=pltpu.HBM)],
        out_specs=full_specs(1)[0],
        scratch_shapes=[
            pltpu.VMEM(doc_vectors.shape, jnp.bfloat16),
            pltpu.VMEM((2 * n_doc, LANES), jnp.int32),
            pltpu.SMEM((2 * n_doc, LANES), jnp.int32),
            pltpu.SemaphoreType.DMA((8,)),
            pltpu.SemaphoreType.DMA,
        ],
        compiler_params=params(16),
        name="rate",
    )(doc_lengths, queries, far(doc_vectors))
    back = lax.all_to_all(rated.reshape(-1, LANES), ("doc", "head"), 0, 0, tiled=True)

    single, _ = lax.optimization_barrier((single, rated))
    shares = [single] + [over_head(single, k) for k in range(1, n_head)]
    query_vectors = pl.pallas_call(
        arrange_kernel,
        out_shape=jax.ShapeDtypeStruct((rows, emb), jnp.bfloat16),
        in_specs=full_specs(n_head),
        out_specs=full_specs(1)[0],
        compiler_params=params(4),
        name="arrange",
    )(*shares)

    scores = pl.pallas_call(
        collect_kernel,
        out_shape=jax.ShapeDtypeStruct((cols, cand_rows), jnp.float32),
        in_specs=full_specs(1),
        out_specs=full_specs(1)[0],
        compiler_params=params(4),
        name="collect",
    )(back.reshape((n_doc, n_head) + tile))
    return (query_vectors, scores.T)


def solution(mesh):
    placed = (
        P("doc", None),
        P(None, None, "head"),
        P("head", None),
        P(None, "head"),
        P("head", None),
        P(),
        P(),
        P(),
        P(None, "doc", "head"),
        P(),
        P("doc", None, None),
        P("doc"),
        P("doc"),
        P("doc", "head"),
    )
    fits = mesh.shape["head"] == 4 and mesh.shape["doc"] == 8
    return jax.shard_map(
        body if fits else body_any,
        mesh=mesh,
        in_specs=placed,
        out_specs=(P("doc", None), P("doc", "head")),
        check_vma=False,
    )
```
